32 devices in a mesh: dp: 8 (over z, y), mp: 4 (over x, core).
Axes of the slice: x: 2, y: 2, z: 4, core: 2. Of those that a mesh axis runs over, the one named last changes fastest.
Arguments:
- entity_table: float32 [65536, 400], P(('dp', 'mp'))
- entity_rows: float32 [65536], P(('dp', 'mp')), may hold values from 2.0954758e-13 to 8.381903e-13
- entity_cols: float32 [400], replicated, may hold values from 2.0954758e-13 to 8.381903e-13
- relation_table: float32 [2, 25088, 400], P(None, ('dp', 'mp')), may hold values from -0.21 to 0.21
- relation_rows: float32 [2, 25088], P(None, ('dp', 'mp')), may hold values from 1.824632e-13 to 7.298528e-13
- relation_cols: float32 [2, 400], replicated, may hold values from 1.824632e-13 to 7.298528e-13
- requests: int32 [32, 8, 4, 8], P(('dp', 'mp')), may hold values from 0 to 2047
- relation_requests: int32 [32, 8, 4, 8], P(('dp', 'mp')), may hold values from 0 to 783, as said below
- src_slot: int32 [2, 65536], P(None, ('dp', 'mp')), may hold values from 0 to 255
- dst_slot: int32 [2, 65536], P(None, ('dp', 'mp')), may hold values from 0 to 255
- relation_ids: int32 [2, 65536], P(None, ('dp', 'mp')), may hold values from 0 to 255
- edge_valid: int32 [2, 65536], P(None, ('dp', 'mp')), may hold values from 0 to 1, as said below
- neg_slot: int32 [2, 8, 1000], P(None, 'dp', 'mp'), may hold values from 0 to 255
Outputs:
- loss: float32 [2], replicated
- entity_weight: float32 [65536, 400], P(('dp', 'mp'))
- entity_grad: float32 [65536, 400], P(('dp', 'mp'))
- entity_rows_new: float32 [65536], P(('dp', 'mp'))
- entity_cols_new: float32 [400], replicated
- entity_copy: bfloat16 [65536, 400], P(('dp', 'mp'))
- relation_weight: float32 [2, 25088, 400], P(None, ('dp', 'mp'))
- relation_grad: float32 [2, 25088, 400], P(None, ('dp', 'mp'))
- relation_rows_new: float32 [2, 25088], P(None, ('dp', 'mp'))
- relation_cols_new: float32 [2, 400], replicated
- relation_copy: bfloat16 [2, 25088, 400], P(None, ('dp', 'mp'))
The draws below stay inside these ranges and needn't reach their ends.
Inputs may be any that keep to these rules, and one draw needn't show every extreme that they name: `requests`: a row index within its owner's 2048 rows. `relation_requests`: a relation within its owner's 784 relations; the 8 relations that one device requests from one owner are distinct. `edge_valid`: the share of valid slots rises along the devices.
All inputs are finite; a program needn't handle non-finite values.
Results may differ from the reference program's by a relative error of at most 0.001.
Values sent between devices are 32-bit elements; how exact they have to be, the bound alone decides.
A program may use at most 384 MiB of HBM per device.

```python
import math
from functools import partial
import jax
import jax.numpy as jnp
import numpy as np
from jax import lax

W = 400
ENT_DEV = 2048
NREL = 25088
L = 2
NEG = 1000
CAP = 8
RCAP = 8
MB = 2
EDGE_DEV = 2048
ENT = 65536
SLOTS = 256
RREL_DEV = 784
RSLOTS = 256
EDGES = 65536
N_DP = 8
N_MP = 4


def draw_entity_table(key, part):
    key = jax.random.fold_in(key, 5)
    first, second = jax.random.split(key)
    position = jnp.arange(ENT, dtype=jnp.float32) / ENT
    spread = jnp.exp(jax.random.uniform(first, (ENT, 1), jnp.float32, math.log(0.5), math.log(2.0)))
    rise = 0.5 + position
    base = jax.random.normal(second, (ENT, W), jnp.float32)
    return 0.05 * rise[:, None] * spread * base


def draw_relation_requests(key, part):
    key = jax.random.fold_in(key, 17)
    devices = N_DP * N_MP
    keys = jax.random.split(key, devices * devices)
    owned = NREL // devices
    picks = jax.vmap(lambda single: jax.random.permutation(single, owned)[:RCAP])(keys)
    return picks.reshape(devices, N_DP, N_MP, RCAP).astype(jnp.int32)


def draw_edge_valid(key, part):
    key = jax.random.fold_in(key, 11)
    position = jnp.arange(EDGES, dtype=jnp.int32)
    border = 300 + 600 * position // EDGES
    rolled = jax.random.randint(key, (MB, EDGES), 0, 1000)
    return (rolled < border[None, :]).astype(jnp.int32)


def set_ends(array, key, low, largest):
    index_at = [jax.random.randint(jax.random.fold_in(key, axis), (), 0, length) for axis, length in enumerate(array.shape)]
    longest = array.shape.index(max(array.shape))
    next_to = index_at[:longest] + [(index_at[longest] + 1) % array.shape[longest]] + index_at[longest + 1:]
    return array.at[tuple(index_at)].set(low).at[tuple(next_to)].set(largest)


def levels(own_key, extent, cuts, least, largest):
    level, own = 1.0, jax.random.fold_in(own_key, 6)
    for axis_at, shards_of in cuts:
        heights = jnp.exp(jax.random.uniform(jax.random.fold_in(own, axis_at), (shards_of,), jnp.float32, least / len(cuts), largest / len(cuts)))
        level = level * jnp.repeat(heights, extent[axis_at] // shards_of).reshape([-1 if axis == axis_at else 1 for axis in range(len(extent))])
    return level


def rank_table(count, slope):
    loads = [(1 << 20) // math.isqrt(grade ** slope) + 1 for grade in range(1, count + 1)]
    scale = 1 + sum(loads) // (1 << 30)
    return np.cumsum(np.array([max(1, weight // scale) for weight in loads]))


def ranked_ids(stream_key, dims, count, slope):
    table = rank_table(count, slope)
    ticket = jax.random.randint(jax.random.fold_in(stream_key, 1), dims, 0, int(table[count - 1]))
    standing = jnp.searchsorted(jnp.asarray(table, jnp.int32), ticket, side="right")
    return jax.random.permutation(jax.random.fold_in(stream_key, 2), count)[standing].astype(jnp.int32)


def bell_draw(key, extent, deviation, bound, cuts=(), kind=jnp.bfloat16):
    result = jax.random.normal(key, extent, jnp.float32) * deviation
    if len(cuts) > 0:
        result = levels(key, extent, cuts, -0.22, 0.18) * result
    return jnp.clip(result, min=-bound, max=bound).astype(kind)


def setup_inputs(seed: int = 0) -> dict:
    arg_keys = jax.random.split(jax.random.key(seed), 14)
    entity_table = draw_entity_table(jax.random.fold_in(arg_keys[13], 71), 0)
    entity_rows = jnp.clip(jnp.exp(math.log(8.381903027557258e-13) - 1.3862944 * jax.random.uniform(arg_keys[1], (ENT,), jnp.float32) ** levels(arg_keys[1], (ENT,), ((0, 32),), -0.2, 0.2)), 2.0954757568893145e-13, 8.381903027557258e-13)
    entity_cols = jnp.clip(jnp.exp(jax.random.uniform(arg_keys[2], (W,), jnp.float32, math.log(2.0954757568893145e-13), math.log(8.381903027557258e-13))), 2.0954757568893145e-13, 8.381903027557258e-13)
    relation_table = bell_draw(arg_keys[3], (L, NREL, W), 0.035, 0.21, ((1, 32),), jnp.float32)
    relation_rows = jnp.clip(jnp.exp(math.log(7.29852810132936e-13) - 1.3862944 * jax.random.uniform(arg_keys[4], (L, NREL), jnp.float32) ** levels(arg_keys[4], (L, NREL), ((1, 32),), -0.2, 0.2)), 1.82463202533234e-13, 7.29852810132936e-13)
    relation_cols = jnp.clip(jnp.exp(jax.random.uniform(arg_keys[5], (L, W), jnp.float32, math.log(1.82463202533234e-13), math.log(7.29852810132936e-13))), 1.82463202533234e-13, 7.29852810132936e-13)
    requests = set_ends(jax.random.randint(arg_keys[6], (N_DP * N_MP, N_DP, N_MP, CAP), 0, ENT_DEV), jax.random.fold_in(arg_keys[6], 1), 0, ENT_DEV - 1).astype(jnp.int32)
    relation_requests = draw_relation_requests(jax.random.fold_in(arg_keys[13], 71), 0)
    src_slot = set_ends(jax.random.randint(arg_keys[8], (MB, EDGES), 0, SLOTS), jax.random.fold_in(arg_keys[8], 1), 0, SLOTS - 1).astype(jnp.int32)
    dst_slot = set_ends(jax.random.randint(arg_keys[9], (MB, EDGES), 0, SLOTS), jax.random.fold_in(arg_keys[9], 1), 0, SLOTS - 1).astype(jnp.int32)
    relation_ids = set_ends(ranked_ids(arg_keys[10], (MB, EDGES), RSLOTS, 2), jax.random.fold_in(arg_keys[10], 3), 0, RSLOTS - 1).astype(jnp.int32)
    edge_valid = draw_edge_valid(jax.random.fold_in(arg_keys[13], 71), 0)
    neg_slot = set_ends(jax.random.randint(arg_keys[12], (MB, N_DP, NEG), 0, SLOTS), jax.random.fold_in(arg_keys[12], 1), 0, SLOTS - 1).astype(jnp.int32)
    return dict(entity_table=entity_table, entity_rows=entity_rows, entity_cols=entity_cols, relation_table=relation_table, relation_rows=relation_rows, relation_cols=relation_cols, requests=requests, relation_requests=relation_requests, src_slot=src_slot, dst_slot=dst_slot, relation_ids=relation_ids, edge_valid=edge_valid, neg_slot=neg_slot)


MARGIN = 0.1
EPS_DIST = 1e-06
EPS_SQ = 1e-30
DECAY = 0.5
LEARN = 0.3
CLIP = 0.1

def pair_terms(heads, tails, negative_rows, valid_row):
    offset = heads - tails
    near_dist = jnp.sqrt(lax.optimization_barrier(jnp.sum(offset * offset, 1)) + EPS_DIST)
    cross = jnp.dot(heads, negative_rows.T, precision=lax.Precision.HIGHEST, preferred_element_type=jnp.float32)
    far_dist = jnp.sqrt(lax.optimization_barrier(jnp.sum(heads * heads, 1))[:, None] + lax.optimization_barrier(jnp.sum(negative_rows * negative_rows, 1))[None, :] - 2.0 * cross + EPS_DIST)
    margin_z = MARGIN + near_dist[:, None] - far_dist
    return jax.nn.softplus(margin_z) * valid_row[:, None]

def group_loss(entity, translation, pieces):
    source, target, relation, valid_row, negative = pieces
    heads = entity[source] + translation[relation]
    return jnp.sum(pair_terms(heads, entity[target], entity[negative], valid_row))

def adafactor(weight, grad, row_moment, col_moment):
    squares = grad * grad + EPS_SQ
    rows_new = DECAY * row_moment + (1.0 - DECAY) * lax.optimization_barrier(jnp.mean(squares, 1))
    cols_new = DECAY * col_moment + (1.0 - DECAY) * lax.optimization_barrier(jnp.mean(squares, 0))
    update = grad * lax.rsqrt(rows_new[:, None] * cols_new[None, :] / jnp.mean(rows_new))
    rms_value = jnp.sqrt(jnp.mean(update * update))
    update = update / jnp.maximum(1.0, rms_value / CLIP)
    return (weight - LEARN * update, rows_new, cols_new)

def reference(entity_table, entity_rows, entity_cols, relation_table, relation_rows, relation_cols, requests, relation_requests, src_slot, dst_slot, relation_ids, edge_valid, neg_slot):
    devices = N_DP * N_MP
    owner = jnp.arange(devices, dtype=jnp.int32).reshape(N_DP, N_MP)[None, :, :, None]
    slot_entity = (requests + owner * ENT_DEV).reshape(devices, SLOTS)
    slot_relation = (relation_requests + owner * RREL_DEV).reshape(devices, RSLOTS)
    edge_device = jnp.arange(EDGES, dtype=jnp.int32) // EDGE_DEV
    src_ids = slot_entity[edge_device[None, :], src_slot]
    dst_ids = slot_entity[edge_device[None, :], dst_slot]
    rel_ids = slot_relation[edge_device[None, :], relation_ids]
    neg_device = jnp.arange(N_DP, dtype=jnp.int32)[:, None] * N_MP + jnp.arange(NEG, dtype=jnp.int32)[None, :] // (NEG // N_MP)
    neg_ids = slot_entity[neg_device[None, :, :], neg_slot]
    valid = edge_valid.astype(jnp.float32)
    count = jnp.sum(valid) * NEG
    group = EDGE_DEV * N_MP

    def forward(entity, relation):
        translation = lax.optimization_barrier(jnp.sum(relation, 0))
        total = jnp.zeros((), jnp.float32)
        for batch_index in range(MB):
            pieces = (src_ids[batch_index].reshape(N_DP, group), dst_ids[batch_index].reshape(N_DP, group), rel_ids[batch_index].reshape(N_DP, group), valid[batch_index].reshape(N_DP, group), neg_ids[batch_index])
            partial_sums = lax.map(jax.checkpoint(partial(group_loss, entity, translation)), pieces)
            total = total + jnp.sum(partial_sums)
        return (total / count, total)
    objective, backward_fn, total = jax.vjp(forward, entity_table, relation_table, has_aux=True)
    entity_grad, relation_grad = backward_fn(jnp.ones_like(objective))
    entity_weight, entity_rows_new, entity_cols_new = adafactor(entity_table, entity_grad, entity_rows, entity_cols)
    outcomes = [adafactor(relation_table[layer], relation_grad[layer], relation_rows[layer], relation_cols[layer]) for layer in range(L)]
    relation_weight = jnp.stack([item[0] for item in outcomes])
    relation_rows_new = jnp.stack([item[1] for item in outcomes])
    relation_cols_new = jnp.stack([item[2] for item in outcomes])
    loss = jnp.stack([total, count])
    return (loss, entity_weight, entity_grad, entity_rows_new, entity_cols_new, entity_weight.astype(jnp.bfloat16), relation_weight, relation_grad, relation_rows_new, relation_cols_new, relation_weight.astype(jnp.bfloat16))
```

```python
import functools
import jax
import jax.numpy as jnp
from jax import lax
from jax.experimental import pallas as pl
from jax.experimental.pallas import tpu as pltpu
from jax.sharding import PartitionSpec as P

MARGIN = 0.1
EPS_DIST = 1e-06
EPS_SQ = 1e-30
DECAY = 0.5
LEARN = 0.3
CLIP = 0.1
HIGH = lax.Precision.HIGHEST


def score_forward(heads, tails, negative_rows, valid_row):
    offset = heads - tails
    near_dist = jnp.sqrt(jnp.sum(offset * offset, 1) + EPS_DIST)
    cross = jnp.dot(heads, negative_rows.T, precision=HIGH, preferred_element_type=jnp.float32)
    far_dist = jnp.sqrt(
        jnp.sum(heads * heads, 1)[:, None]
        + jnp.sum(negative_rows * negative_rows, 1)[None, :]
        - 2.0 * cross
        + EPS_DIST
    )
    margin_z = MARGIN + near_dist[:, None] - far_dist
    part_sum = jnp.sum(jax.nn.softplus(margin_z) * valid_row[:, None])
    return ((offset, near_dist, far_dist, margin_z), part_sum)


def score_backward(heads, negative_rows, valid_row, kept, pairs):
    offset, near_dist, far_dist, margin_z = kept
    weight = jax.nn.sigmoid(margin_z) * valid_row[:, None] / pairs
    along = weight / far_dist
    pull = jnp.sum(weight, 1) / near_dist
    grad_head = (
        pull[:, None] * offset
        - jnp.sum(along, 1)[:, None] * heads
        + jnp.dot(along, negative_rows, precision=HIGH, preferred_element_type=jnp.float32)
    )
    grad_tail = -pull[:, None] * offset
    return (grad_head, grad_tail, along)


def local_moments(grad, row_moment):
    squares = grad * grad + EPS_SQ
    rows_new = DECAY * row_moment + (1.0 - DECAY) * jnp.mean(squares, 1)
    weighted = jnp.sum(grad * grad / rows_new[:, None], 0)
    return (rows_new, jnp.sum(squares, 0), jnp.sum(rows_new), weighted)


def scaled_update(grad, rows_new, cols_new, row_mean):
    return grad * lax.rsqrt(rows_new[:, None] * cols_new[None, :] / row_mean)


def shards(
    entity_table,
    entity_rows,
    entity_cols,
    relation_table,
    relation_rows,
    relation_cols,
    requests,
    relation_requests,
    src_slot,
    dst_slot,
    relation_ids,
    edge_valid,
    neg_slot,
):
    width = entity_table.shape[1]
    n_data = lax.axis_size("dp")
    n_model = lax.axis_size("mp")
    devices = n_data * n_model
    owned_rel = relation_table.shape[1]
    translation = lax.all_gather(jnp.sum(relation_table, 0), ("dp", "mp"), axis=0, tiled=True)
    rel_wanted = relation_requests[0]
    owner_base = (
        jnp.arange(n_data, dtype=jnp.int32)[:, None] * n_model
        + jnp.arange(n_model, dtype=jnp.int32)[None, :]
    ) * owned_rel
    rel_global = (rel_wanted + owner_base[:, :, None]).reshape(-1)
    valid_all = edge_valid.astype(jnp.float32)
    negatives_total = neg_slot.shape[2] * n_model
    pairs = lax.psum(jnp.sum(valid_all), ("dp", "mp")) * negatives_total
    wanted = requests[0]
    incoming = lax.all_to_all(
        lax.all_to_all(wanted, "dp", split_axis=0, concat_axis=0, tiled=True),
        "mp",
        split_axis=1,
        concat_axis=1,
        tiled=True,
    )
    served = entity_table[incoming]
    fetched = lax.all_to_all(
        lax.all_to_all(served, "dp", split_axis=0, concat_axis=0, tiled=True),
        "mp",
        split_axis=1,
        concat_axis=1,
        tiled=True,
    )
    slot_count = fetched.shape[0] * fetched.shape[1] * fetched.shape[2]
    fetched = fetched.reshape(slot_count, width)
    slot_grad = jnp.zeros((slot_count, width), jnp.float32)
    relation_sum = jnp.zeros((rel_global.shape[0], width), jnp.float32)
    loss_part = jnp.zeros((), jnp.float32)
    for batch_index in range(src_slot.shape[0]):
        valid_row = valid_all[batch_index]
        own_negatives = fetched[neg_slot[batch_index, 0]]
        negative_rows = lax.all_gather(own_negatives, "mp", axis=0, tiled=True)
        rel_rows = rel_global[relation_ids[batch_index]]
        heads = fetched[src_slot[batch_index]] + translation[rel_rows]
        tails = fetched[dst_slot[batch_index]]
        kept, part_sum = score_forward(heads, tails, negative_rows, valid_row)
        loss_part = loss_part + part_sum
        grad_head, grad_tail, along = score_backward(heads, negative_rows, valid_row, kept, pairs)
        pulled = lax.dot_general(
            along,
            heads,
            (((0,), (0,)), ((), ())),
            precision=HIGH,
            preferred_element_type=jnp.float32,
        )
        grad_negative = lax.psum_scatter(
            pulled - jnp.sum(along, 0)[:, None] * negative_rows,
            "mp",
            scatter_dimension=0,
            tiled=True,
        )
        slot_grad = slot_grad.at[src_slot[batch_index]].add(grad_head)
        slot_grad = slot_grad.at[dst_slot[batch_index]].add(grad_tail)
        slot_grad = slot_grad.at[neg_slot[batch_index, 0]].add(grad_negative)
        relation_sum = relation_sum.at[relation_ids[batch_index]].add(grad_head)
    returned = lax.all_to_all(
        lax.all_to_all(
            slot_grad.reshape(served.shape), "dp", split_axis=0, concat_axis=0, tiled=True
        ),
        "mp",
        split_axis=1,
        concat_axis=1,
        tiled=True,
    )
    entity_grad = (
        jnp.zeros(entity_table.shape, jnp.float32)
        .at[incoming.reshape(-1)]
        .add(returned.reshape(-1, width))
    )
    rel_incoming = lax.all_to_all(
        lax.all_to_all(rel_wanted, "dp", split_axis=0, concat_axis=0, tiled=True),
        "mp",
        split_axis=1,
        concat_axis=1,
        tiled=True,
    )
    rel_returned = lax.all_to_all(
        lax.all_to_all(
            relation_sum.reshape(rel_wanted.shape + (width,)),
            "dp",
            split_axis=0,
            concat_axis=0,
            tiled=True,
        ),
        "mp",
        split_axis=1,
        concat_axis=1,
        tiled=True,
    )
    relation_shard = (
        jnp.zeros((owned_rel, width), jnp.float32)
        .at[rel_incoming.reshape(-1)]
        .add(rel_returned.reshape(-1, width))
    )
    layers = relation_table.shape[0]
    relation_grad = jnp.broadcast_to(relation_shard[None], (layers,) + relation_shard.shape)
    entity_count = entity_table.shape[0] * devices
    relation_count = relation_shard.shape[0] * devices
    ent_rows, ent_colsq, ent_rsum, ent_weighted = local_moments(entity_grad, entity_rows)
    rel_rows, rel_colsq, rel_rsum, rel_weighted = jax.vmap(local_moments, in_axes=(None, 0))(
        relation_shard, relation_rows
    )
    totals = lax.psum((loss_part, ent_colsq, ent_rsum, rel_colsq, rel_rsum), ("dp", "mp"))
    loss_total, ent_colsq, ent_rsum, rel_colsq, rel_rsum = totals
    ent_cols = DECAY * entity_cols + (1.0 - DECAY) * ent_colsq / entity_count
    rel_cols = DECAY * relation_cols + (1.0 - DECAY) * rel_colsq / relation_count
    ent_mean = ent_rsum / entity_count
    rel_mean = rel_rsum / relation_count
    ent_update = scaled_update(entity_grad, ent_rows, ent_cols, ent_mean)
    rel_update = jax.vmap(scaled_update, in_axes=(None, 0, 0, 0))(
        relation_shard, rel_rows, rel_cols, rel_mean
    )
    ent_usq, rel_usq = lax.psum(
        (jnp.sum(ent_update * ent_update), jnp.sum(rel_update * rel_update, (1, 2))), ("dp", "mp")
    )
    ent_factor = jnp.maximum(1.0, jnp.sqrt(ent_usq / (entity_count * width)) / CLIP)
    rel_factor = jnp.maximum(1.0, jnp.sqrt(rel_usq / (relation_count * width)) / CLIP)
    entity_weight = entity_table - LEARN * (ent_update / ent_factor)
    relation_weight = relation_table - LEARN * (rel_update / rel_factor[:, None, None])
    loss = jnp.stack([loss_total, pairs])
    return (
        loss,
        entity_weight,
        entity_grad,
        ent_rows,
        ent_cols,
        entity_weight.astype(jnp.bfloat16),
        relation_weight,
        relation_grad,
        rel_rows,
        rel_cols,
        relation_weight.astype(jnp.bfloat16),
    )


F32, BF16 = jnp.float32, jnp.bfloat16
LOG2E = 1.4426950408889634
FAR = 1e30
AUX = 16

def two(x):
    hi = x.astype(BF16)
    return hi, (x - hi.astype(F32)).astype(BF16)

def three(x):
    hi = x.astype(BF16)
    rest = x - hi.astype(F32)
    mid = rest.astype(BF16)
    return hi, mid, (rest - mid.astype(F32)).astype(BF16)

def mm(a, b):
    return lax.dot_general(a, b, (((1,), (0,)), ((), ())), preferred_element_type=F32)

def mm_t(a, b):
    return lax.dot_general(a, b, (((1,), (1,)), ((), ())), preferred_element_type=F32)

def score_kernel(W, KN, SL, RS, EC, RB, SKIP,
                 nt_ref, tt_ref, ft_ref, cnt_ref, src_ref, dst_ref, rel_ref, val_ref,
                 gn_ref, gf_ref, gr_ref, loss_ref,
                 neg_rows, neg_hi, neg_lo, table, along_s, head_s, s_s, oh_s, a_s, b1_s, b2_s):
    m, c = pl.program_id(0), pl.program_id(1)
    first = jnp.logical_and(m == 0, c == 0)
    last = jnp.logical_and(m == pl.num_programs(0) - 1, c == pl.num_programs(1) - 1)
    NG = nt_ref.shape[0]

    @pl.when(first if 'init' not in SKIP else m<0)
    def _():
        for g in range(NG):
            n = nt_ref[g, 0:W, :]
            nn = jnp.sum(n * n, 0, keepdims=True) * (LOG2E * LOG2E)
            hi, mid, lo = three(nn)
            row = lax.broadcasted_iota(jnp.int32, (AUX, KN), 0)
            aux = jnp.where(row == 0, hi.astype(F32), jnp.where(row == 1, mid.astype(F32), jnp.where(row == 2, lo.astype(F32), jnp.where(row < 6, 1.0, 0.0))))
            both = jnp.concatenate([n * (-2.0 * LOG2E * LOG2E), aux], 0)
            neg_rows[g * KN:(g + 1) * KN, :] = both.T.astype(BF16)
            nh, nl = two(n)
            neg_hi[:, g * KN:(g + 1) * KN] = nh
            neg_lo[:, g * KN:(g + 1) * KN] = nl
        fh, fl = two(ft_ref[0:W, :])
        th, tl = two(tt_ref[...])
        table[0, :, 0:SL] = fh
        table[1, :, 0:SL] = fl
        table[0, :, SL:SL + RS] = th
        table[1, :, SL:SL + RS] = tl
        a_s[...] = jnp.zeros_like(a_s)
        b1_s[...] = jnp.zeros_like(b1_s)
        b2_s[...] = jnp.zeros_like(b2_s)
        loss_ref[...] = jnp.zeros_like(loss_ref)

    off = pl.multiple_of(c * EC, EC)
    pick = lambda ref: ref[pl.ds(m, 1), pl.ds(off, EC)]
    src, dst, rel, val = pick(src_ref), pick(dst_ref), pick(rel_ref), pick(val_ref)
    slot = lax.broadcasted_iota(jnp.int32, (SL, EC), 0)
    oh_s[0:SL, :] = jnp.where(slot == src, 1.0, 0.0).astype(BF16)
    oh_d = jnp.where(slot == dst, 1.0, 0.0).astype(BF16)
    rslot = slot if RS == SL else lax.broadcasted_iota(jnp.int32, (RS, EC), 0)
    oh_s[SL:, :] = jnp.where(rslot == rel, 1.0, 0.0).astype(BF16)
    if "gather" in SKIP:
        head = jnp.broadcast_to(src.astype(F32), (W, EC)); tail = jnp.broadcast_to(dst.astype(F32), (W, EC))
    else:
        head = mm(table[0], oh_s[...]) + mm(table[1], oh_s[...])
        tail = mm(table[0, :, 0:SL], oh_d) + mm(table[1, :, 0:SL], oh_d)
    diff = head - tail
    near2 = jnp.sum(diff * diff, 0, keepdims=True) + EPS_DIST
    inv_near = lax.rsqrt(near2)
    near = near2 * inv_near
    hh = (jnp.sum(head * head, 0, keepdims=True) + EPS_DIST) * (LOG2E * LOG2E)
    bound = jnp.where(val > 0, (MARGIN + near) * LOG2E, -FAR)
    hi, mid, lo = three(hh)
    row = lax.broadcasted_iota(jnp.int32, (AUX, EC), 0)
    aux = jnp.where(row < 3, 1.0, jnp.where(row == 3, hi.astype(F32), jnp.where(row == 4, mid.astype(F32), jnp.where(row == 5, lo.astype(F32), 0.0))))
    head_s[...] = jnp.concatenate([head, aux], 0).astype(BF16)
    sw = jnp.zeros((8, EC), F32)
    sa = jnp.zeros((8, EC), F32)
    def elem(g, b, sw, sa):
        r0 = g * KN + b * RB
        cnt = cnt_ref[pl.ds(m, 1), r0:r0 + RB, :]
        cnt = cnt[0]
        sq = jnp.maximum(s_s[g % 2, b * RB:(b + 1) * RB, :], 1e-20)
        r = lax.rsqrt(sq)
        t = sq * r - bound
        sig = pl.reciprocal(1.0 + jnp.exp2(t), approx=True)
        om = 1.0 - sig
        low = jnp.minimum(sig, om)
        high = jnp.maximum(sig, om)
        w = cnt * sig
        sw = sw + jnp.sum(w.reshape(RB // 8, 8, EC), 0)
        wr = w * r
        sa = sa + jnp.sum(wr.reshape(RB // 8, 8, EC), 0)
        along_s[r0:r0 + RB, :] = wr.astype(BF16)
        if "loss" not in SKIP:
            q = jnp.zeros((RB, 128), F32)
            mx = jnp.zeros((RB, 128), F32)
            for i in range(EC // 128):
                sl = slice(i * 128, (i + 1) * 128)
                q = q * high[:, sl] + low[:, sl]
                mx = mx + jnp.minimum(t[:, sl], 0.0)
            part = cnt * (-jnp.log(1.0 - q) - mx * (1.0 / LOG2E))
            loss_ref[...] += jnp.sum(part.reshape(RB // 8, 8, 128), 0)
        return sw, sa
    for g in range(NG):
        if "cross" not in SKIP:
            s_s[g % 2] = mm(neg_rows[g * KN:(g + 1) * KN, :], head_s[...])
        if "elem" not in SKIP:
            for b in range(KN // RB):
                sw, sa = elem(g, b, sw, sa)
        if "A" not in SKIP:
            a_s[:, g * KN:(g + 1) * KN] += mm_t(oh_s[...], along_s[g * KN:(g + 1) * KN, :])
    p = jnp.sum(sw, 0, keepdims=True) * inv_near
    x = p - jnp.sum(sa, 0, keepdims=True) * LOG2E
    if "B" not in SKIP:
        for part in two(p):
            b1_s[...] += mm_t(oh_s[...], oh_d * part)
        for part in two(x):
            b2_s[...] += mm_t(oh_s[0:SL, :], oh_s[SL:, :] * part)

    if "final" in SKIP:
        gn_ref[...]=jnp.zeros_like(gn_ref);gf_ref[...]=jnp.zeros_like(gf_ref);gr_ref[...]=jnp.zeros_like(gr_ref)
        return
    @pl.when(last)
    def _():
        sd, rd, sr = b1_s[0:SL, :], b1_s[SL:, :], b2_s[...]
        eye_s = lax.broadcasted_iota(jnp.int32, (SL, SL), 0) == lax.broadcasted_iota(jnp.int32, (SL, SL), 1)
        eye_r = lax.broadcasted_iota(jnp.int32, (RS, RS), 0) == lax.broadcasted_iota(jnp.int32, (RS, RS), 1)
        ss = jnp.where(eye_s, jnp.sum(sr, 1, keepdims=True) + jnp.sum(sd, 0, keepdims=True), 0.0) - sd - sd.T
        rr = jnp.where(eye_r, jnp.sum(sr, 0, keepdims=True), 0.0)
        x_sr = sr - rd.T
        x_rs = x_sr.T
        big = jnp.concatenate([jnp.concatenate([ss, x_sr], 1), jnp.concatenate([x_rs, rr], 1)], 0)
        bh, bl = two(big)
        ah = (a_s[...] * LOG2E).astype(BF16)
        al = (a_s[...] * LOG2E - ah.astype(F32)).astype(BF16)
        out = mm_t(bh, table[0]) + mm_t(bh, table[1]) + mm_t(bl, table[0]) + mm_t(ah, neg_hi[...]) + mm_t(ah, neg_lo[...]) + mm_t(al, neg_hi[...])
        gf_ref[...] = out[0:SL]
        gr_ref[...] = out[SL:]
        for g in range(NG):
            ag = ah[:, g * KN:(g + 1) * KN]
            gn_ref[g] = mm(table[0], ag) + mm(table[1], ag) + mm(table[0], al[:, g * KN:(g + 1) * KN]) - (jnp.sum(a_s[0:SL, g * KN:(g + 1) * KN], 0, keepdims=True) * LOG2E) * nt_ref[g, 0:W, :]

def score(nt, tt, ft, cnt, src, dst, rel, val, EC=512, RB=32, SKIP=()):
    NG, R0, KN = nt.shape
    W, RS = tt.shape
    SL = ft.shape[1]
    MB, E = src.shape
    full = lambda a: pl.BlockSpec(a.shape, lambda m, c, n=a.ndim: (0,) * n)
    outs = [jax.ShapeDtypeStruct((NG, W, KN), F32), jax.ShapeDtypeStruct((SL, W), F32), jax.ShapeDtypeStruct((RS, W), F32), jax.ShapeDtypeStruct((8, 128), F32)]
    args = (nt, tt, ft, cnt, src, dst, rel, val)
    V = pltpu.VMEM
    return pl.pallas_call(
        functools.partial(score_kernel, W, KN, SL, RS, EC, RB, SKIP),
        grid=(MB, E // EC),
        in_specs=[full(a) for a in args],
        out_specs=[full(o) for o in outs],
        out_shape=outs,
        scratch_shapes=[V((NG * KN, W + AUX), BF16), V((W, NG * KN), BF16), V((W, NG * KN), BF16), V((2, W, SL + RS), BF16),
                        V((NG * KN, EC), BF16), V((W + AUX, EC), BF16), V((2, KN, EC), F32), V((SL + RS, EC), BF16),
                        V((SL + RS, NG * KN), F32), V((SL + RS, SL), F32), V((SL, RS), F32)],
        compiler_params=pltpu.CompilerParams(vmem_limit_bytes=56 << 20, dimension_semantics=("arbitrary", "arbitrary")),
        name="score",
    )(*args)


MESH = pl.DeviceIdType.MESH
LANES = 128


def start_barrier(me, devices, place):
    barrier = pltpu.get_barrier_semaphore()

    def tell(step, carry):
        pl.semaphore_signal(
            barrier, inc=1, device_id=place(lax.rem(me + step, devices)), device_id_type=MESH
        )
        return carry

    lax.fori_loop(1, devices, tell, 0)
    return barrier


def spread(me, devices, place, src, dst, send_sem, recv_sem):
    def step(i, carry):
        p = lax.rem(me + i, devices)
        pltpu.make_async_remote_copy(
            src_ref=src(p),
            dst_ref=dst(me),
            send_sem=send_sem.at[p],
            recv_sem=recv_sem.at[me],
            device_id=place(p),
            device_id_type=MESH,
        ).start()
        return carry

    lax.fori_loop(1, devices, step, 0)


def collect(me, devices, place, src, dst, send_sem, recv_sem):
    def step(i, carry):
        p = lax.rem(me + devices - i, devices)
        pltpu.make_async_remote_copy(
            src_ref=src(p),
            dst_ref=dst(p),
            send_sem=send_sem.at[p],
            recv_sem=recv_sem.at[p],
            device_id=place(p),
            device_id_type=MESH,
        ).wait_recv()
        return carry

    lax.fori_loop(1, devices, step, 0)


def sent(me, devices, place, src, dst, send_sem, recv_sem):
    def step(i, carry):
        p = lax.rem(me + i, devices)
        pltpu.make_async_remote_copy(
            src_ref=src(p),
            dst_ref=dst(me),
            send_sem=send_sem.at[p],
            recv_sem=recv_sem.at[me],
            device_id=place(p),
            device_id_type=MESH,
        ).wait_send()
        return carry

    lax.fori_loop(1, devices, step, 0)


def id_columns(ids, cap):
    devices = ids.shape[0]
    wide = jnp.broadcast_to(ids, (devices, cap, LANES)).reshape(devices * cap, LANES)
    row = lax.broadcasted_iota(jnp.int32, wide.shape, 0)
    lane = lax.broadcasted_iota(jnp.int32, wide.shape, 1)
    at = lax.rem(row, cap)
    ent = jnp.sum(jnp.where(lane == at, wide, 0), 1, keepdims=True)
    rel = jnp.sum(jnp.where(lane == at + cap, wide, 0), 1, keepdims=True)
    return ent, rel


def one_hot(column, count):
    lane = lax.broadcasted_iota(jnp.int32, (column.shape[0], count), 1)
    return jnp.where(lane == column, 1.0, 0.0).astype(BF16)


def fetch_kernel(
    n_mp, cap, ask_ref, counts_ref, ent_ref, rel_ref,
    neg_ref, trans_ref, ids_ref, total_ref,
    ent_s, rel_s, rel_sum, asked, out_ent, out_rel, in_ent, in_rel,
    load_sem, ask_send, ask_recv, ent_send, ent_recv, rel_send, rel_recv, mp_send, mp_recv,
):
    width, owned = ent_s.shape
    devices = ask_ref.shape[0]
    dp, mp = lax.axis_index("dp"), lax.axis_index("mp")
    me = dp * n_mp + mp
    place = lambda p: (lax.div(p, n_mp), lax.rem(p, n_mp))
    barrier = start_barrier(me, devices, place)
    load_ent = pltpu.make_async_copy(ent_ref, ent_s, load_sem.at[0])
    load_rel = pltpu.make_async_copy(rel_ref, rel_s, load_sem.at[1])
    load_ent.start()
    load_rel.start()
    asked[me] = ask_ref[me]
    load_ent.wait()
    load_rel.wait()
    owned_rel = rel_s.shape[2]
    rel_sum[...] = jnp.zeros_like(rel_sum)
    rel_sum[:, 0:owned_rel] = sum(rel_s[i] for i in range(rel_s.shape[0]))
    pl.semaphore_wait(barrier, devices - 1)

    ask = (me, devices, place, lambda p: ask_ref.at[p], lambda p: asked.at[p], ask_send, ask_recv)
    spread(*ask)
    collect(*ask)
    ent_id, rel_id = id_columns(asked[...], cap)
    lane = lax.broadcasted_iota(jnp.int32, ids_ref.shape, 1)
    ids_ref[...] = jnp.where(lane == 0, ent_id, jnp.where(lane == 1, rel_id, 0))
    valid = jnp.where(lax.broadcasted_iota(jnp.int32, asked.shape, 2) == 2 * cap, asked[...], 0)
    total_ref[...] = jnp.sum(jnp.sum(valid, 0), 1, keepdims=True).astype(F32) + jnp.zeros_like(total_ref)

    pick = one_hot(ent_id, owned)
    rows = sum(mm_t(pick, part) for part in two(ent_s[...]))
    pick = one_hot(rel_id, rel_sum.shape[1])
    rel_rows = sum(mm_t(pick, part) for part in two(rel_sum[...]))
    main = width // LANES * LANES
    rest = width - main
    tails = jnp.concatenate(
        [rows[:, main:], rel_rows[:, main:], jnp.zeros((rows.shape[0], LANES - 2 * rest), F32)], 1
    )
    out_ent[:, :, 0:main] = rows[:, 0:main].reshape(devices, cap, main)
    out_ent[:, :, main:] = tails.reshape(devices, cap, LANES)
    out_rel[...] = rel_rows[:, 0:main].reshape(devices, cap, main)
    give_ent = (me, devices, place, lambda p: out_ent.at[p], lambda p: in_ent.at[p], ent_send, ent_recv)
    give_rel = (me, devices, place, lambda p: out_rel.at[p], lambda p: in_rel.at[p], rel_send, rel_recv)
    spread(*give_ent)
    spread(*give_rel)
    in_ent[me] = out_ent[me]
    in_rel[me] = out_rel[me]

    collect(*give_ent)
    got = in_ent[...].reshape(devices * cap, main + LANES)
    neg_ref[mp, 0:width, :] = got[:, 0:width].T
    neg_ref[mp, width:, :] = counts_ref[...]
    mates = (mp + 1 - 2 * lax.rem(mp, 2), lax.rem(mp + 2, n_mp))

    def hand(step, block, to):
        return pltpu.make_async_remote_copy(
            src_ref=neg_ref.at[block],
            dst_ref=neg_ref.at[block],
            send_sem=mp_send.at[step],
            recv_sem=mp_recv.at[step],
            device_id=(dp, to),
            device_id_type=MESH,
        )

    across = hand(0, mp, mates[1])
    near = hand(1, mp, mates[0])
    across.start()
    near.start()
    hand(0, mates[1], mates[1]).wait_recv()
    onward = hand(2, mates[1], mates[0])
    onward.start()
    collect(*give_rel)
    rel_got = in_rel[...].reshape(devices * cap, main)
    trans_ref[0:main, :] = rel_got.T
    trans_ref[main:, :] = got[:, width:width + rest].T
    hand(1, mates[0], mates[0]).wait_recv()
    hand(2, mates[0] + mates[1] - mp, mates[0]).wait_recv()
    across.wait_send()
    near.wait_send()
    onward.wait_send()
    sent(*ask)
    sent(*give_ent)
    sent(*give_rel)


def fetch(n_mp, devices, cap, ask, counts, ent_t, rel_t):
    width, owned = ent_t.shape
    layers, _, owned_rel = rel_t.shape
    slots = devices * cap
    main = width // LANES * LANES
    padded_rel = -(-owned_rel // LANES) * LANES
    V, sem = pltpu.VMEM, pltpu.SemaphoreType.DMA
    vmem = pl.BlockSpec(memory_space=pltpu.VMEM)
    hbm = pl.BlockSpec(memory_space=pl.ANY)
    return pl.pallas_call(
        functools.partial(fetch_kernel, n_mp, cap),
        out_shape=[
            jax.ShapeDtypeStruct((n_mp, width + 8, slots), F32),
            jax.ShapeDtypeStruct((width, slots), F32),
            jax.ShapeDtypeStruct((slots, LANES), jnp.int32),
            jax.ShapeDtypeStruct((8, LANES), F32),
        ],
        in_specs=[vmem, vmem, hbm, hbm],
        out_specs=[vmem] * 4,
        scratch_shapes=[
            V((width, owned), F32), V((layers, width, owned_rel), F32), V((width, padded_rel), F32),
            V((devices, 1, LANES), jnp.int32),
            V((devices, cap, main + LANES), F32), V((devices, cap, main), F32),
            V((devices, cap, main + LANES), F32), V((devices, cap, main), F32),
            sem((2,)), sem((devices,)), sem((devices,)), sem((devices,)), sem((devices,)),
            sem((devices,)), sem((devices,)), sem((3,)), sem((3,)),
        ],
        compiler_params=pltpu.CompilerParams(
            collective_id=1, has_side_effects=True, vmem_limit_bytes=56 << 20
        ),
        name="fetch",
    )(ask, counts, ent_t, rel_t)


def give_back_kernel(
    n_mp, cap, negatives, edges_share,
    neg_ref, ent_ref, rel_ref, ids_ref, ent_rows_ref, rel_rows_ref, ent_cols_ref, rel_cols_ref, total_ref, loss_ref,
    ent_grad_ref, rel_grad_ref, ent_new_ref, rel_new_ref, ent_col_ref, rel_col_ref, scale_ref, loss_out_ref,
    from_mate, to_across, from_across, out_ent, out_rel, in_ent, in_rel, part_mp, part_dp,
    ent_send, ent_recv, rel_send, rel_recv, mate_send, mate_recv, sum_mp_send, sum_mp_recv, sum_dp_send, sum_dp_recv,
):
    devices = out_ent.shape[0]
    n_dp = devices // n_mp
    width, owned = ent_grad_ref.shape
    owned_rel = rel_grad_ref.shape[1]
    layers = rel_rows_ref.shape[0]
    dp, mp = lax.axis_index("dp"), lax.axis_index("mp")
    me = dp * n_mp + mp
    place = lambda p: (lax.div(p, n_mp), lax.rem(p, n_mp))
    barrier = start_barrier(me, devices, place)
    main = width // LANES * LANES
    rest = width - main
    mates = (mp + 1 - 2 * lax.rem(mp, 2), lax.rem(mp + 2, n_mp))
    far_mate = mates[0] + mates[1] - mp
    out_rel[...] = rel_ref[:, 0:main].reshape(devices, cap, main)

    def hand(step, src, dst, to):
        return pltpu.make_async_remote_copy(
            src_ref=src, dst_ref=dst, send_sem=mate_send.at[step], recv_sem=mate_recv.at[step],
            device_id=(dp, to), device_id_type=MESH,
        )

    pl.semaphore_wait(barrier, devices - 1)
    through = hand(1, neg_ref.at[far_mate], from_mate.at[1], mates[0])
    through.start()
    direct = hand(0, neg_ref.at[mates[0]], from_mate.at[0], mates[0])
    direct.start()
    give_ent = (me, devices, place, lambda p: out_ent.at[p], lambda p: in_ent.at[p], ent_send, ent_recv)
    give_rel = (me, devices, place, lambda p: out_rel.at[p], lambda p: in_rel.at[p], rel_send, rel_recv)
    through.wait_recv()
    to_across[...] = neg_ref[mates[1]] + from_mate[1]
    across = hand(2, to_across, from_across, mates[1])
    across.start()
    spread(*give_rel)
    in_rel[me] = out_rel[me]
    direct.wait_recv()
    across.wait_recv()
    rows = (neg_ref[mp] + from_mate[0] + from_across[...]).T + ent_ref[...]
    tails = jnp.concatenate(
        [rows[:, main:], rel_ref[:, main:], jnp.zeros((rows.shape[0], LANES - 2 * rest), F32)], 1
    )
    out_ent[:, :, 0:main] = rows[:, 0:main].reshape(devices, cap, main)
    out_ent[:, :, main:] = tails.reshape(devices, cap, LANES)
    spread(*give_ent)
    in_ent[me] = out_ent[me]
    ent_pick = one_hot(ids_ref[:, 0:1], owned)
    rel_pick = one_hot(ids_ref[:, 1:2], owned_rel)
    collect(*give_rel)
    collect(*give_ent)
    slots = devices * cap
    back = in_ent[...].reshape(slots, main + LANES)
    scale = 1.0 / (total_ref[0:1, 0:1] * negatives)
    ent_back = back[:, 0:width].T * scale
    rel_back = jnp.concatenate(
        [in_rel[...].reshape(slots, main), back[:, width:width + rest]], 1
    ).T * scale
    ent_grad_ref[...] = sum(mm(part, ent_pick) for part in two(ent_back))
    rel_grad_ref[...] = sum(mm(part, rel_pick) for part in two(rel_back))

    def moments(grad, moment):
        square = grad * grad
        new = DECAY * moment + (1.0 - DECAY) * (jnp.sum(square, 0, keepdims=True) / width + EPS_SQ)
        return new, square

    new, square = moments(ent_grad_ref[...], ent_rows_ref[...])
    ent_new_ref[...] = new
    lane = lax.broadcasted_iota(jnp.int32, (width, LANES), 1)
    held = jnp.where(lane == 0, jnp.sum(square, 1, keepdims=True), 0.0)
    held = jnp.where(lane == 1, jnp.sum(square / new, 1, keepdims=True), held)
    sums = [jnp.sum(loss_ref[...], (0, 1), keepdims=True), jnp.sum(new, 1, keepdims=True)]
    for layer in range(layers):
        new, square = moments(rel_grad_ref[...], rel_rows_ref[layer:layer + 1, :])
        rel_new_ref[layer:layer + 1, :] = new
        if layer == 0:
            held = jnp.where(lane == 2, jnp.sum(square, 1, keepdims=True), held)
        held = jnp.where(lane == 3 + layer, jnp.sum(square / new, 1, keepdims=True), held)
        sums.append(jnp.sum(new, 1, keepdims=True))
    flat = held.T
    count = 3 + layers
    part_mp[mp, 0:8, 0:main] = flat[0:8, 0:main]
    part_mp[mp, 0:8, main:] = jnp.concatenate([flat[0:8, main:], jnp.zeros((8, LANES - rest), F32)], 1)
    lane = lax.broadcasted_iota(jnp.int32, (1, main + LANES), 1)
    extra = jnp.zeros((1, main + LANES), F32)
    for i, value in enumerate(sums):
        extra = jnp.where(lane == i, value, extra)
    part_mp[mp, count:count + 1, :] = extra

    def share(axis, size, buffer, send, recv):
        at = {"dp": dp, "mp": mp}[axis]
        copies = []
        for i in range(1, size):
            to = lax.rem(at + i, size)
            copies.append(pltpu.make_async_remote_copy(
                src_ref=buffer.at[at], dst_ref=buffer.at[at], send_sem=send.at[i], recv_sem=recv.at[i],
                device_id={axis: to}, device_id_type=MESH,
            ))
            copies[-1].start()
        for i in range(1, size):
            came = lax.rem(at + size - i, size)
            pltpu.make_async_remote_copy(
                src_ref=buffer.at[came], dst_ref=buffer.at[came], send_sem=send.at[i], recv_sem=recv.at[i],
                device_id={axis: came}, device_id_type=MESH,
            ).wait_recv()
        return copies

    copies = share("mp", n_mp, part_mp, sum_mp_send, sum_mp_recv)
    part_dp[dp] = jnp.sum(part_mp[...], 0)
    copies += share("dp", n_dp, part_dp, sum_dp_send, sum_dp_recv)
    total = jnp.sum(part_dp[...], 0)

    last = total[count:count + 1, :]
    ent_count, rel_count = owned * devices, owned_rel * devices

    def finish(cols, col_sum, weighted, moment_sum, rows):
        new = DECAY * cols + (1.0 - DECAY) * (col_sum / rows + EPS_SQ)
        mean = moment_sum / rows
        square = jnp.sum(weighted / new, 1, keepdims=True) * mean
        factor = jnp.maximum(1.0, jnp.sqrt(square / (rows * width)) / CLIP)
        return new, LEARN * jnp.sqrt(mean) * lax.rsqrt(new) / factor

    new, step = finish(ent_cols_ref[...], total[0:1, 0:width], total[1:2, 0:width], last[:, 1:2], ent_count)
    ent_col_ref[...] = new
    scale_ref[...] = jnp.zeros_like(scale_ref)
    scale_ref[0:1, :] = step
    for layer in range(layers):
        new, step = finish(
            rel_cols_ref[layer:layer + 1, :], total[2:3, 0:width], total[3 + layer:4 + layer, 0:width],
            last[:, 2 + layer:3 + layer], rel_count,
        )
        rel_col_ref[layer:layer + 1, :] = new
        scale_ref[1 + layer:2 + layer, :] = step
    loss_out_ref[...] = jnp.zeros_like(loss_out_ref) + last[:, 0:1]
    through.wait_send()
    direct.wait_send()
    across.wait_send()
    sent(*give_ent)
    sent(*give_rel)
    for copy in copies:
        copy.wait_send()


def give_back(n_mp, devices, cap, negatives, neg, ent, rel, ids, ent_rows, rel_rows, ent_cols, rel_cols, total, loss):
    _, width, slots = neg.shape
    owned, (layers, owned_rel) = ent_rows.shape[1], rel_rows.shape
    main = width // LANES * LANES
    n_dp = devices // n_mp
    V, sem = pltpu.VMEM, pltpu.SemaphoreType.DMA
    vmem = pl.BlockSpec(memory_space=pltpu.VMEM)
    args = (neg, ent, rel, ids, ent_rows, rel_rows, ent_cols, rel_cols, total, loss)
    outs = [
        jax.ShapeDtypeStruct(shape, F32)
        for shape in (
            (width, owned), (width, owned_rel), (1, owned), (layers, owned_rel), (1, width), (layers, width),
            (8, width), (8, LANES),
        )
    ]
    return pl.pallas_call(
        functools.partial(give_back_kernel, n_mp, cap, negatives, None),
        out_shape=outs,
        in_specs=[vmem] * len(args),
        out_specs=[vmem] * len(outs),
        scratch_shapes=[
            V((2, width, slots), F32), V((width, slots), F32), V((width, slots), F32),
            V((devices, cap, main + LANES), F32), V((devices, cap, main), F32),
            V((devices, cap, main + LANES), F32), V((devices, cap, main), F32),
            V((n_mp, 8, main + LANES), F32), V((n_dp, 8, main + LANES), F32),
            sem((devices,)), sem((devices,)), sem((devices,)), sem((devices,)), sem((3,)), sem((3,)),
            sem((n_mp,)), sem((n_mp,)), sem((n_dp,)), sem((n_dp,)),
        ],
        compiler_params=pltpu.CompilerParams(
            collective_id=2, has_side_effects=True, vmem_limit_bytes=56 << 20
        ),
        name="give_back",
    )(*args)


def fused(
    entity_table, entity_rows, entity_cols, relation_table, relation_rows, relation_cols,
    requests, relation_requests, src_slot, dst_slot, relation_ids, edge_valid, neg_slot,
):
    n_mp = lax.axis_size("mp")
    devices = lax.axis_size("dp") * n_mp
    cap = requests.shape[3]
    slots = devices * cap
    negatives = neg_slot.shape[2] * n_mp
    valid = jnp.sum(edge_valid)
    ask = jnp.concatenate(
        [
            requests.reshape(devices, cap), relation_requests.reshape(devices, cap),
            jnp.broadcast_to(valid, (devices, 1)), jnp.zeros((devices, LANES - 2 * cap - 1), jnp.int32),
        ], 1,
    ).reshape(devices, 1, LANES)
    batches = src_slot.shape[0]
    hits = neg_slot[:, 0, None, :] == jnp.arange(slots, dtype=jnp.int32)[None, :, None]
    counts = jnp.sum(hits.astype(F32), 2)
    counts = jnp.concatenate([counts, jnp.zeros((8 - batches, slots), F32)], 0)
    ent_t = entity_table.T
    rel_t = jnp.swapaxes(relation_table, 1, 2)
    neg, trans, ids, total = fetch(n_mp, devices, cap, ask, counts, ent_t, rel_t)
    width = ent_t.shape[0]
    mp = lax.axis_index("mp")
    own = lax.dynamic_index_in_dim(neg, mp, 0, keepdims=False)
    every = jnp.swapaxes(neg[:, width:width + batches, :], 0, 1).reshape(batches, n_mp * slots, 1)
    grad_neg, grad_ent, grad_rel, loss_part = score(
        neg, trans, own, every, src_slot, dst_slot, relation_ids, edge_valid, EC=src_slot.shape[1]
    )
    ent_grad, rel_grad, ent_new, rel_new, ent_col, rel_col, steps, loss = give_back(
        n_mp, devices, cap, negatives, grad_neg, grad_ent, grad_rel, ids,
        entity_rows[None], relation_rows, entity_cols[None], relation_cols, total, loss_part,
    )
    ent_w = ent_t - ent_grad * lax.rsqrt(ent_new) * steps[0][:, None]
    layers = rel_t.shape[0]
    rel_w = rel_t - rel_grad[None] * lax.rsqrt(rel_new)[:, None, :] * steps[1:1 + layers][:, :, None]
    rel_grads = jnp.broadcast_to(rel_grad.T[None], relation_table.shape)
    back = lambda x: jnp.swapaxes(x, -1, -2)
    return (
        jnp.stack([loss[0, 0], total[0, 0] * negatives]),
        back(ent_w), back(ent_grad), ent_new[0], ent_col[0], back(ent_w.astype(BF16)),
        back(rel_w), rel_grads, rel_new, rel_col, back(rel_w.astype(BF16)),
    )


def solution(mesh):
    in_specs = (
        P(("dp", "mp"), None),
        P(("dp", "mp")),
        P(),
        P(None, ("dp", "mp"), None),
        P(None, ("dp", "mp")),
        P(),
        P(("dp", "mp"), None, None, None),
        P(("dp", "mp"), None, None, None),
        P(None, ("dp", "mp")),
        P(None, ("dp", "mp")),
        P(None, ("dp", "mp")),
        P(None, ("dp", "mp")),
        P(None, "dp", "mp"),
    )
    out_specs = (
        P(),
        P(("dp", "mp"), None),
        P(("dp", "mp"), None),
        P(("dp", "mp")),
        P(),
        P(("dp", "mp"), None),
        P(None, ("dp", "mp"), None),
        P(None, ("dp", "mp"), None),
        P(None, ("dp", "mp")),
        P(),
        P(None, ("dp", "mp"), None),
    )

    def step(*args):
        small = args[6].shape[1] * args[6].shape[2] * args[6].shape[3] <= 512
        return (fused if small else shards)(*args)

    return jax.shard_map(step, mesh=mesh, in_specs=in_specs, out_specs=out_specs, check_vma=False)
```

```python
import functools

import jax
import jax.numpy as jnp
from jax import lax
from jax.experimental import pallas as pl
from jax.experimental.pallas import tpu as pltpu
from jax.sharding import PartitionSpec as P

MARGIN = 0.1
EPS_DIST = 1e-06
EPS_SQ = 1e-30
DECAY = 0.5
LEARN = 0.3
CLIP = 0.1
HIGH = lax.Precision.HIGHEST


def score_forward(heads, tails, negative_rows, valid_row):
    offset = heads - tails
    near_dist = jnp.sqrt(jnp.sum(offset * offset, 1) + EPS_DIST)
    cross = jnp.dot(heads, negative_rows.T, precision=HIGH, preferred_element_type=jnp.float32)
    far_dist = jnp.sqrt(
        jnp.sum(heads * heads, 1)[:, None]
        + jnp.sum(negative_rows * negative_rows, 1)[None, :]
        - 2.0 * cross
        + EPS_DIST
    )
    margin_z = MARGIN + near_dist[:, None] - far_dist
    part_sum = jnp.sum(jax.nn.softplus(margin_z) * valid_row[:, None])
    return ((offset, near_dist, far_dist, margin_z), part_sum)


def score_backward(heads, negative_rows, valid_row, kept, pairs):
    offset, near_dist, far_dist, margin_z = kept
    weight = jax.nn.sigmoid(margin_z) * valid_row[:, None] / pairs
    along = weight / far_dist
    pull = jnp.sum(weight, 1) / near_dist
    grad_head = (
        pull[:, None] * offset
        - jnp.sum(along, 1)[:, None] * heads
        + jnp.dot(along, negative_rows, precision=HIGH, preferred_element_type=jnp.float32)
    )
    grad_tail = -pull[:, None] * offset
    return (grad_head, grad_tail, along)


def local_moments(grad, row_moment):
    squares = grad * grad + EPS_SQ
    rows_new = DECAY * row_moment + (1.0 - DECAY) * jnp.mean(squares, 1)
    weighted = jnp.sum(grad * grad / rows_new[:, None], 0)
    return (rows_new, jnp.sum(squares, 0), jnp.sum(rows_new), weighted)


def scaled_update(grad, rows_new, cols_new, row_mean):
    return grad * lax.rsqrt(rows_new[:, None] * cols_new[None, :] / row_mean)


def shards(
    entity_table,
    entity_rows,
    entity_cols,
    relation_table,
    relation_rows,
    relation_cols,
    requests,
    relation_requests,
    src_slot,
    dst_slot,
    relation_ids,
    edge_valid,
    neg_slot,
):
    width = entity_table.shape[1]
    n_data = lax.axis_size("dp")
    n_model = lax.axis_size("mp")
    devices = n_data * n_model
    owned_rel = relation_table.shape[1]
    translation = lax.all_gather(jnp.sum(relation_table, 0), ("dp", "mp"), axis=0, tiled=True)
    rel_wanted = relation_requests[0]
    owner_base = (
        jnp.arange(n_data, dtype=jnp.int32)[:, None] * n_model
        + jnp.arange(n_model, dtype=jnp.int32)[None, :]
    ) * owned_rel
    rel_global = (rel_wanted + owner_base[:, :, None]).reshape(-1)
    valid_all = edge_valid.astype(jnp.float32)
    negatives_total = neg_slot.shape[2] * n_model
    pairs = lax.psum(jnp.sum(valid_all), ("dp", "mp")) * negatives_total
    wanted = requests[0]
    incoming = lax.all_to_all(
        lax.all_to_all(wanted, "dp", split_axis=0, concat_axis=0, tiled=True),
        "mp",
        split_axis=1,
        concat_axis=1,
        tiled=True,
    )
    served = entity_table[incoming]
    fetched = lax.all_to_all(
        lax.all_to_all(served, "dp", split_axis=0, concat_axis=0, tiled=True),
        "mp",
        split_axis=1,
        concat_axis=1,
        tiled=True,
    )
    slot_count = fetched.shape[0] * fetched.shape[1] * fetched.shape[2]
    fetched = fetched.reshape(slot_count, width)
    slot_grad = jnp.zeros((slot_count, width), jnp.float32)
    relation_sum = jnp.zeros((rel_global.shape[0], width), jnp.float32)
    loss_part = jnp.zeros((), jnp.float32)
    for batch_index in range(src_slot.shape[0]):
        valid_row = valid_all[batch_index]
        own_negatives = fetched[neg_slot[batch_index, 0]]
        negative_rows = lax.all_gather(own_negatives, "mp", axis=0, tiled=True)
        rel_rows = rel_global[relation_ids[batch_index]]
        heads = fetched[src_slot[batch_index]] + translation[rel_rows]
        tails = fetched[dst_slot[batch_index]]
        kept, part_sum = score_forward(heads, tails, negative_rows, valid_row)
        loss_part = loss_part + part_sum
        grad_head, grad_tail, along = score_backward(heads, negative_rows, valid_row, kept, pairs)
        pulled = lax.dot_general(
            along,
            heads,
            (((0,), (0,)), ((), ())),
            precision=HIGH,
            preferred_element_type=jnp.float32,
        )
        grad_negative = lax.psum_scatter(
            pulled - jnp.sum(along, 0)[:, None] * negative_rows,
            "mp",
            scatter_dimension=0,
            tiled=True,
        )
        slot_grad = slot_grad.at[src_slot[batch_index]].add(grad_head)
        slot_grad = slot_grad.at[dst_slot[batch_index]].add(grad_tail)
        slot_grad = slot_grad.at[neg_slot[batch_index, 0]].add(grad_negative)
        relation_sum = relation_sum.at[relation_ids[batch_index]].add(grad_head)
    returned = lax.all_to_all(
        lax.all_to_all(
            slot_grad.reshape(served.shape), "dp", split_axis=0, concat_axis=0, tiled=True
        ),
        "mp",
        split_axis=1,
        concat_axis=1,
        tiled=True,
    )
    entity_grad = (
        jnp.zeros(entity_table.shape, jnp.float32)
        .at[incoming.reshape(-1)]
        .add(returned.reshape(-1, width))
    )
    rel_incoming = lax.all_to_all(
        lax.all_to_all(rel_wanted, "dp", split_axis=0, concat_axis=0, tiled=True),
        "mp",
        split_axis=1,
        concat_axis=1,
        tiled=True,
    )
    rel_returned = lax.all_to_all(
        lax.all_to_all(
            relation_sum.reshape(rel_wanted.shape + (width,)),
            "dp",
            split_axis=0,
            concat_axis=0,
            tiled=True,
        ),
        "mp",
        split_axis=1,
        concat_axis=1,
        tiled=True,
    )
    relation_shard = (
        jnp.zeros((owned_rel, width), jnp.float32)
        .at[rel_incoming.reshape(-1)]
        .add(rel_returned.reshape(-1, width))
    )
    layers = relation_table.shape[0]
    relation_grad = jnp.broadcast_to(relation_shard[None], (layers,) + relation_shard.shape)
    entity_count = entity_table.shape[0] * devices
    relation_count = relation_shard.shape[0] * devices
    ent_rows, ent_colsq, ent_rsum, ent_weighted = local_moments(entity_grad, entity_rows)
    rel_rows, rel_colsq, rel_rsum, rel_weighted = jax.vmap(local_moments, in_axes=(None, 0))(
        relation_shard, relation_rows
    )
    totals = lax.psum((loss_part, ent_colsq, ent_rsum, rel_colsq, rel_rsum), ("dp", "mp"))
    loss_total, ent_colsq, ent_rsum, rel_colsq, rel_rsum = totals
    ent_cols = DECAY * entity_cols + (1.0 - DECAY) * ent_colsq / entity_count
    rel_cols = DECAY * relation_cols + (1.0 - DECAY) * rel_colsq / relation_count
    ent_mean = ent_rsum / entity_count
    rel_mean = rel_rsum / relation_count
    ent_update = scaled_update(entity_grad, ent_rows, ent_cols, ent_mean)
    rel_update = jax.vmap(scaled_update, in_axes=(None, 0, 0, 0))(
        relation_shard, rel_rows, rel_cols, rel_mean
    )
    ent_usq, rel_usq = lax.psum(
        (jnp.sum(ent_update * ent_update), jnp.sum(rel_update * rel_update, (1, 2))), ("dp", "mp")
    )
    ent_factor = jnp.maximum(1.0, jnp.sqrt(ent_usq / (entity_count * width)) / CLIP)
    rel_factor = jnp.maximum(1.0, jnp.sqrt(rel_usq / (relation_count * width)) / CLIP)
    entity_weight = entity_table - LEARN * (ent_update / ent_factor)
    relation_weight = relation_table - LEARN * (rel_update / rel_factor[:, None, None])
    loss = jnp.stack([loss_total, pairs])
    return (
        loss,
        entity_weight,
        entity_grad,
        ent_rows,
        ent_cols,
        entity_weight.astype(jnp.bfloat16),
        relation_weight,
        relation_grad,
        rel_rows,
        rel_cols,
        relation_weight.astype(jnp.bfloat16),
    )


F32, BF16 = jnp.float32, jnp.bfloat16
LOG2E = 1.4426950408889634
OUT_OF_REACH = 1e30
AUX = 16
LANES = 128
MESH = pl.DeviceIdType.MESH


def two(x):
    hi = x.astype(BF16)
    return hi, (x - hi.astype(F32)).astype(BF16)


def three(x):
    hi = x.astype(BF16)
    rest = x - hi.astype(F32)
    mid = rest.astype(BF16)
    return hi, mid, (rest - mid.astype(F32)).astype(BF16)


def mm(a, b):
    return lax.dot_general(a, b, (((1,), (0,)), ((), ())), preferred_element_type=F32)


def mm_t(a, b):
    return lax.dot_general(a, b, (((1,), (1,)), ((), ())), preferred_element_type=F32)


def iota(shape, axis):
    return lax.broadcasted_iota(jnp.int32, shape, axis)


def stack_rows(rows, count, width):
    at = iota((count, width), 0)
    out = jnp.zeros((count, width), F32)
    for i, row in enumerate(rows):
        out = jnp.where(at == i, row, out)
    return out


def stack_columns(columns, height):
    at = iota((height, LANES), 1)
    out = jnp.zeros((height, LANES), F32)
    for i, column in enumerate(columns):
        out = jnp.where(at == i, column, out)
    return out


class Spread:
    def __init__(self, me, devices, place, src, dst, send_sem, recv_sem):
        self.me, self.devices, self.place = me, devices, place
        self.src, self.dst, self.send_sem, self.recv_sem = src, dst, send_sem, recv_sem

    def copy(self, p, at):
        return pltpu.make_async_remote_copy(
            src_ref=self.src(p),
            dst_ref=self.dst(at),
            send_sem=self.send_sem.at[p],
            recv_sem=self.recv_sem.at[at],
            device_id=self.place(p),
            device_id_type=MESH,
        )

    def each(self, act):
        def step(i, carry):
            act(lax.rem(self.me + i, self.devices))
            return carry

        lax.fori_loop(1, self.devices, step, 0)

    def start(self):
        self.each(lambda p: self.copy(p, self.me).start())

    def arrived(self):
        self.each(lambda p: self.copy(p, p).wait_recv())

    def left(self):
        self.each(lambda p: self.copy(p, self.me).wait_send())


def step_kernel(
    n_mp, cap, negatives, rb,
    ent_ref, rel_ref, req_ref, rel_req_ref, src_ref, dst_ref, rid_ref, val_ref, neg_slot_ref,
    ent_rows_ref, rel_rows_ref, ent_cols_ref, rel_cols_ref,
    ent_back_ref, rel_back_ref, ids_ref, ent_new_ref, rel_new_ref, ent_col_ref, rel_col_ref, step_ref, loss_ref,
    ent_s, rel_s, ent_parts, rel_parts, ask_s, asked, out_ent, out_rel, in_ent, in_rel, back_in_ent, back_in_rel,
    neg_s, oh_s, oh_d, lead_s, gap_s, head_s, sq_s, along_s, a_s, b1_s, b2_s, table, neg_rows, neg_parts, count_s,
    gn_s, from_mate, from_across, part_mp, part_dp, loss_s,
    load_sem, ask_send, ask_recv, ent_send, ent_recv, rel_send, rel_recv, mp_send, mp_recv,
    back_ent_send, back_ent_recv, back_rel_send, back_rel_recv, mate_send, mate_recv,
    sum_mp_send, sum_mp_recv, sum_dp_send, sum_dp_recv,
):
    width, owned = ent_s.shape
    layers, _, owned_rel = rel_s.shape
    devices = out_ent.shape[0]
    n_dp = devices // n_mp
    slots = devices * cap
    batches, edges = src_ref.shape
    main = width // LANES * LANES
    rest = width - main
    dp, mp = lax.axis_index("dp"), lax.axis_index("mp")
    me = dp * n_mp + mp
    mate, across = mp + 1 - 2 * lax.rem(mp, 2), lax.rem(mp + 2, n_mp)
    beyond = mate + across - mp

    def place(p):
        return lax.div(p, n_mp), lax.rem(p, n_mp)

    barrier = pltpu.get_barrier_semaphore()

    def tell(i, carry):
        pl.semaphore_signal(
            barrier, inc=1, device_id=place(lax.rem(me + i, devices)), device_id_type=MESH
        )
        return carry

    lax.fori_loop(1, devices, tell, 0)
    load_ent = pltpu.make_async_copy(ent_ref, ent_s, load_sem.at[0])
    load_rel = pltpu.make_async_copy(rel_ref, rel_s, load_sem.at[1])
    load_ent.start()
    load_rel.start()
    valid = jnp.sum(jnp.sum(val_ref[...], 0, keepdims=True), 1, keepdims=True)
    lane = iota(ask_s.shape, 2)
    ask_s[...] = jnp.where(lane == 2 * cap, valid[None], 0)
    ask_s[:, :, 0:cap] = req_ref[0]
    ask_s[:, :, cap:2 * cap] = rel_req_ref[0]
    asked[me] = ask_s[dp, pl.ds(mp, 1)]
    hits = [
        jnp.sum(jnp.where(iota((slots, neg_slot_ref.shape[2]), 0) == neg_slot_ref[m], 1.0, 0.0), 1, keepdims=True)
        for m in range(batches)
    ]
    own_counts = stack_columns(hits, slots).T[0:8]
    load_ent.wait()
    load_rel.wait()
    for i, part in enumerate(two(ent_s[...])):
        ent_parts[i] = part
    if rel_parts.shape[2] > owned_rel:
        rel_parts[:, :, owned_rel:] = jnp.zeros((2, width, rel_parts.shape[2] - owned_rel), BF16)
    for i, part in enumerate(two(sum(rel_s[i] for i in range(layers)))):
        rel_parts[i, :, 0:owned_rel] = part
    pl.semaphore_wait(barrier, devices - 1)

    ask = Spread(
        me, devices, place, lambda p: ask_s.at[place(p)[0], pl.ds(place(p)[1], 1)], lambda p: asked.at[p], ask_send, ask_recv
    )
    ask.start()
    for m in range(batches):
        slot = iota((slots, edges), 0)
        oh_s[m, 0:slots, :] = jnp.where(slot == src_ref[m:m + 1, :], 1.0, 0.0).astype(BF16)
        oh_s[m, slots:, :] = jnp.where(slot == rid_ref[m:m + 1, :], 1.0, 0.0).astype(BF16)
        oh_d[m] = jnp.where(slot == dst_ref[m:m + 1, :], 1.0, 0.0).astype(BF16)
    ask.arrived()
    wide = jnp.broadcast_to(asked[...], (devices, cap, LANES)).reshape(slots, LANES)
    at, lane = lax.rem(iota(wide.shape, 0), cap), iota(wide.shape, 1)
    ent_id = jnp.sum(jnp.where(lane == at, wide, 0), 1, keepdims=True)
    rel_id = jnp.sum(jnp.where(lane == at + cap, wide, 0), 1, keepdims=True)
    ids_ref[...] = jnp.where(lane == 0, ent_id, jnp.where(lane == 1, rel_id, 0))
    valid_all = jnp.sum(jnp.where(iota(asked.shape, 2) == 2 * cap, asked[...], 0), 0)
    pairs = jnp.sum(valid_all, 1, keepdims=True).astype(F32) * negatives

    pick = jnp.where(iota((slots, owned), 1) == ent_id, 1.0, 0.0).astype(BF16)
    rows = mm_t(pick, ent_parts[0]) + mm_t(pick, ent_parts[1])
    pick = jnp.where(iota((slots, rel_parts.shape[2]), 1) == rel_id, 1.0, 0.0).astype(BF16)
    rel_rows = mm_t(pick, rel_parts[0]) + mm_t(pick, rel_parts[1])

    def load_out(ent, rel):
        blank = jnp.zeros((slots, LANES - 2 * rest), F32)
        tails = jnp.concatenate([ent[:, main:], rel[:, main:], blank], 1)
        out_ent[:, :, 0:main] = ent[:, 0:main].reshape(devices, cap, main)
        out_ent[:, :, main:] = tails.reshape(devices, cap, LANES)

    def block(ref):
        return lambda p: ref.at[p]

    load_out(rows, rel_rows)
    give_ent = Spread(me, devices, place, block(out_ent), block(in_ent), ent_send, ent_recv)
    give_ent.start()
    out_rel[...] = rel_rows[:, 0:main].reshape(devices, cap, main)
    give_rel = Spread(me, devices, place, block(out_rel), block(in_rel), rel_send, rel_recv)
    give_rel.start()
    in_ent[me] = out_ent[me]
    in_rel[me] = out_rel[me]

    give_ent.arrived()
    got = in_ent[...].reshape(slots, main + LANES)
    own_t = got[:, 0:width].T
    neg_s[mp, 0:width, :] = own_t
    neg_s[mp, width:, :] = own_counts

    def hand(i, which, to):
        return pltpu.make_async_remote_copy(
            src_ref=neg_s.at[which], dst_ref=neg_s.at[which], send_sem=mp_send.at[i], recv_sem=mp_recv.at[i],
            device_id=(dp, to), device_id_type=MESH,
        )

    to_across, to_mate = hand(0, mp, across), hand(1, mp, mate)
    to_across.start()
    to_mate.start()
    for i, part in enumerate(two(own_t)):
        table[i, :, 0:slots] = part
    for m in range(batches):
        lead = mm(table[0, :, 0:slots], oh_s[m, 0:slots, :]) + mm(table[1, :, 0:slots], oh_s[m, 0:slots, :])
        lead_s[m] = lead
        gap_s[m] = lead - mm(table[0, :, 0:slots], oh_d[m]) - mm(table[1, :, 0:slots], oh_d[m])
    hand(0, across, across).wait_recv()
    onward = hand(2, across, mate)
    onward.start()

    give_rel.arrived()
    rel_got = jnp.concatenate([in_rel[...].reshape(slots, main), got[:, width:width + rest]], 1).T
    for i, part in enumerate(two(rel_got)):
        table[i, :, slots:] = part
    bounds, inv_nears = [], []
    for m in range(batches):
        moved = mm(table[0, :, slots:], oh_s[m, slots:, :]) + mm(table[1, :, slots:], oh_s[m, slots:, :])
        head = lead_s[m] + moved
        diff = gap_s[m] + moved
        near2 = jnp.sum(diff * diff, 0, keepdims=True) + EPS_DIST
        inv_near = lax.rsqrt(near2)
        inv_nears.append(inv_near)
        bounds.append(jnp.where(val_ref[m:m + 1, :] > 0, (MARGIN + near2 * inv_near) * LOG2E, -OUT_OF_REACH))
        norm = three((jnp.sum(head * head, 0, keepdims=True) + EPS_DIST) * (LOG2E * LOG2E))
        ones = jnp.ones((1, edges), F32)
        head_s[m, 0:width, :] = head.astype(BF16)
        head_s[m, width:, :] = stack_rows([ones] * 3 + [part.astype(F32) for part in norm], AUX, edges).astype(BF16)

    hand(1, mate, mate).wait_recv()
    hand(2, beyond, mate).wait_recv()
    order = (beyond, across, mate, mp)
    for g, which in enumerate(order):
        n = neg_s[which, 0:width, :]
        norm = three(jnp.sum(n * n, 0, keepdims=True) * (LOG2E * LOG2E))
        ones = jnp.ones((1, slots), F32)
        extra = stack_rows([part.astype(F32) for part in norm] + [ones] * 3, AUX, slots)
        neg_rows[g] = jnp.concatenate([n * (-2.0 * LOG2E * LOG2E), extra], 0).T.astype(BF16)
        for i, part in enumerate(two(n)):
            neg_parts[i, :, g * slots:(g + 1) * slots] = part
        blank = jnp.zeros((LANES - 8, slots), F32)
        count_s[g] = jnp.concatenate([neg_s[which, width:, :], blank], 0).T

    loss_s[...] = jnp.zeros_like(loss_s)
    weight = [jnp.zeros((8, edges), F32) for _ in range(batches)]
    pulls = [jnp.zeros((8, edges), F32) for _ in range(batches)]

    def pair_terms(g, m, spot):
        for b in range(slots // rb):
            span = slice(b * rb, (b + 1) * rb)
            count = count_s[g, span, m:m + 1]
            square = jnp.maximum(sq_s[spot, span, :], 1e-20)
            inv_far = lax.rsqrt(square)
            t = square * inv_far - bounds[m]
            sig = pl.reciprocal(1.0 + jnp.exp2(t), approx=True)
            rest_sig = 1.0 - sig
            low, high = jnp.minimum(sig, rest_sig), jnp.maximum(sig, rest_sig)
            w = count * sig
            pulls[m] = pulls[m] + jnp.sum(w.reshape(rb // 8, 8, edges), 0)
            w = w * inv_far
            weight[m] = weight[m] + jnp.sum(w.reshape(rb // 8, 8, edges), 0)
            along_s[spot, span, :] = w.astype(BF16)
            q = jnp.zeros((rb, LANES), F32)
            over = jnp.zeros((rb, LANES), F32)
            for i in range(edges // LANES):
                part = slice(i * LANES, (i + 1) * LANES)
                q = q * high[:, part] + low[:, part]
                over = over + jnp.minimum(t[:, part], 0.0)
            term = count * (-jnp.log(1.0 - q) - over * (1.0 / LOG2E))
            loss_s[...] += jnp.sum(term.reshape(rb // 8, 8, LANES), 0)

    def negative_grad(g, which):
        total = a_s[g] * LOG2E
        hi, lo = two(total)
        whole = jnp.sum(total[0:slots], 0, keepdims=True)
        return mm(table[0], hi) + mm(table[1], hi) + mm(table[0], lo) - whole * neg_s[which, 0:width, :]

    def swap(i, src, dst, to):
        return pltpu.make_async_remote_copy(
            src_ref=src, dst_ref=dst, send_sem=mate_send.at[i], recv_sem=mate_recv.at[i],
            device_id=(dp, to), device_id_type=MESH,
        )

    through = swap(0, gn_s.at[0], from_mate.at[0], mate)
    over_x = swap(1, gn_s.at[1], from_across, across)
    direct = swap(2, gn_s.at[2], from_mate.at[1], mate)
    spot = 0
    for g, which in enumerate(order):
        for m in range(batches):
            sq_s[spot] = mm(neg_rows[g], head_s[m])
            pair_terms(g, m, spot)
            part = mm_t(oh_s[m], along_s[spot])
            a_s[g] = part if m == 0 else a_s[g] + part
            spot = 1 - spot
        grad = negative_grad(g, which)
        if g == 0:
            gn_s[0] = grad
            through.start()
        elif g == 1:
            through.wait_recv()
            gn_s[1] = grad + from_mate[0]
            over_x.start()
        elif g == 2:
            gn_s[2] = grad
            direct.start()
        else:
            own_grad = grad

    for m in range(batches):
        pull = jnp.sum(pulls[m], 0, keepdims=True) * inv_nears[m]
        excess = pull - jnp.sum(weight[m], 0, keepdims=True) * LOG2E
        slot = iota((slots, edges), 0)
        part = sum(
            mm_t(oh_s[m], jnp.where(slot == dst_ref[m:m + 1, :], piece.astype(F32), 0.0).astype(BF16)) for piece in two(pull)
        )
        b1_s[...] = part if m == 0 else b1_s[...] + part
        part = sum(
            mm_t(oh_s[m, 0:slots, :], jnp.where(slot == rid_ref[m:m + 1, :], piece.astype(F32), 0.0).astype(BF16))
            for piece in two(excess)
        )
        b2_s[...] = part if m == 0 else b2_s[...] + part
    sd, rd, sr = b1_s[0:slots, :], b1_s[slots:, :], b2_s[...]
    eye = iota((slots, slots), 0) == iota((slots, slots), 1)
    ss = jnp.where(eye, jnp.sum(sr, 1, keepdims=True) + jnp.sum(sd, 0, keepdims=True), 0.0) - sd - sd.T
    rr = jnp.where(eye, jnp.sum(sr, 0, keepdims=True), 0.0)
    cross = sr - rd.T

    def grads(lo, hi, left, right):
        kept = jnp.concatenate([left, right], 1)
        out = None
        for a, b in ((0, 0), (0, 1), (1, 0)):
            term = mm_t(two(kept)[a], table[b])
            out = term if out is None else out + term
        for g in range(n_mp):
            total = two(a_s[g, lo:hi, :] * LOG2E)
            cols = slice(g * slots, (g + 1) * slots)
            for a, b in ((0, 0), (0, 1), (1, 0)):
                out = out + mm_t(total[a], neg_parts[b, :, cols])
        return out

    grad_rel = grads(slots, 2 * slots, cross.T, rr)
    give_ent.left()
    give_rel.left()
    out_rel[...] = grad_rel[:, 0:main].reshape(devices, cap, main)
    back_rel = Spread(me, devices, place, block(out_rel), block(back_in_rel), back_rel_send, back_rel_recv)
    back_ent = Spread(me, devices, place, block(out_ent), block(back_in_ent), back_ent_send, back_ent_recv)
    back_rel.start()
    grad_ent = grads(0, slots, ss, cross)
    direct.wait_recv()
    over_x.wait_recv()
    grad_ent = grad_ent + (own_grad + from_mate[1] + from_across[...]).T
    load_out(grad_ent, grad_rel)
    back_ent.start()
    back_in_rel[me] = out_rel[me]
    back_in_ent[me] = out_ent[me]
    ent_pick = jnp.where(iota((slots, owned), 1) == ent_id, 1.0, 0.0).astype(BF16)
    rel_pick = jnp.where(iota((slots, owned_rel), 1) == rel_id, 1.0, 0.0).astype(BF16)
    scale = 1.0 / pairs
    back_rel.arrived()
    back_ent.arrived()
    back = back_in_ent[...].reshape(slots, main + LANES)
    ent_back = back[:, 0:width].T * scale
    rel_back = jnp.concatenate([back_in_rel[...].reshape(slots, main), back[:, width:width + rest]], 1).T * scale
    ent_back_ref[...] = ent_back
    rel_back_ref[...] = rel_back
    ent_grad = sum(mm(part, ent_pick) for part in two(ent_back))
    rel_grad = sum(mm(part, rel_pick) for part in two(rel_back))

    def moments(square, moment):
        return DECAY * moment + (1.0 - DECAY) * (jnp.sum(square, 0, keepdims=True) / width + EPS_SQ)

    square = ent_grad * ent_grad
    new = moments(square, ent_rows_ref[...])
    ent_new_ref[...] = new
    columns = [jnp.sum(square, 1, keepdims=True), jnp.sum(square / new, 1, keepdims=True)]
    scalars = [
        jnp.sum(jnp.sum(loss_s[...], 0, keepdims=True), 1, keepdims=True), jnp.sum(new, 1, keepdims=True)
    ]
    square = rel_grad * rel_grad
    columns.append(jnp.sum(square, 1, keepdims=True))
    for layer in range(layers):
        new = moments(square, rel_rows_ref[layer:layer + 1, :])
        rel_new_ref[layer:layer + 1, :] = new
        columns.append(jnp.sum(square / new, 1, keepdims=True))
        scalars.append(jnp.sum(new, 1, keepdims=True))
    flat = stack_columns(columns, width).T
    count = len(columns)
    part_mp[mp, :, 0:main] = flat[0:8, 0:main]
    part_mp[mp, :, main:] = jnp.concatenate([flat[0:8, main:], jnp.zeros((8, LANES - rest), F32)], 1)
    lane = iota((1, main + LANES), 1)
    extra = jnp.zeros((1, main + LANES), F32)
    for i, value in enumerate(scalars):
        extra = jnp.where(lane == i, value, extra)
    part_mp[mp, count:count + 1, :] = extra

    def share(axis, size, at, buffer, send, recv):
        copies = []
        for i in range(1, size):
            copies.append(pltpu.make_async_remote_copy(
                src_ref=buffer.at[at], dst_ref=buffer.at[at], send_sem=send.at[i], recv_sem=recv.at[i],
                device_id={axis: lax.rem(at + i, size)}, device_id_type=MESH,
            ))
            copies[-1].start()
        for i in range(1, size):
            came = lax.rem(at + size - i, size)
            pltpu.make_async_remote_copy(
                src_ref=buffer.at[came], dst_ref=buffer.at[came], send_sem=send.at[i], recv_sem=recv.at[i],
                device_id={axis: came}, device_id_type=MESH,
            ).wait_recv()
        return copies

    copies = share("mp", n_mp, mp, part_mp, sum_mp_send, sum_mp_recv)
    part_dp[dp] = jnp.sum(part_mp[...], 0)
    copies += share("dp", n_dp, dp, part_dp, sum_dp_send, sum_dp_recv)
    total = jnp.sum(part_dp[...], 0)
    last = total[count:count + 1, :]

    def finish(cols, col_sum, weighted, moment_sum, height):
        new = DECAY * cols + (1.0 - DECAY) * (col_sum / height + EPS_SQ)
        mean = moment_sum / height
        square = jnp.sum(weighted / new, 1, keepdims=True) * mean
        factor = jnp.maximum(1.0, jnp.sqrt(square / (height * width)) / CLIP)
        return new, LEARN * jnp.sqrt(mean) * lax.rsqrt(new) / factor

    new, step = finish(
        ent_cols_ref[...], total[0:1, 0:width], total[1:2, 0:width], last[:, 1:2], owned * devices
    )
    ent_col_ref[...] = new
    steps = [step]
    for layer in range(layers):
        new, step = finish(
            rel_cols_ref[layer:layer + 1, :], total[2:3, 0:width], total[3 + layer:4 + layer, 0:width],
            last[:, 2 + layer:3 + layer], owned_rel * devices,
        )
        rel_col_ref[layer:layer + 1, :] = new
        steps.append(step)
    step_ref[...] = stack_rows(steps, LANES, width).T
    lane = iota(loss_ref.shape, 1)
    loss_ref[...] = jnp.where(lane == 0, last[:, 0:1], jnp.where(lane == 1, pairs, 0.0))
    for copy in [to_across, to_mate, onward, through, over_x, direct] + copies:
        copy.wait_send()
    ask.left()
    back_rel.left()
    back_ent.left()


def update_kernel(
    ent_ref, rel_ref, ent_back_ref, rel_back_ref, ids_ref, ent_rows_ref, rel_rows_ref, step_ref,
    ent_w_ref, ent_g_ref, ent_c_ref, rel_w_ref, rel_g_ref, rel_c_ref,
    ent_pick, rel_pick,
):
    @pl.when(pl.program_id(0) == 0)
    def _():
        ent_pick[...] = jnp.where(iota(ent_pick.shape, 1) == ids_ref[:, 0:1], 1.0, 0.0).astype(BF16)
        rel_pick[...] = jnp.where(iota(rel_pick.shape, 1) == ids_ref[:, 1:2], 1.0, 0.0).astype(BF16)

    grad = sum(mm(part, ent_pick[...]) for part in two(ent_back_ref[...]))
    ent_g_ref[...] = grad
    new = ent_ref[...] - grad * lax.rsqrt(ent_rows_ref[...]) * step_ref[:, 0:1]
    ent_w_ref[...] = new
    ent_c_ref[...] = new.astype(BF16)
    grad = sum(mm(part, rel_pick[...]) for part in two(rel_back_ref[...]))
    for layer in range(rel_ref.shape[0]):
        rel_g_ref[layer] = grad
        new = rel_ref[layer] - grad * lax.rsqrt(rel_rows_ref[layer:layer + 1, :]) * step_ref[:, layer + 1:layer + 2]
        rel_w_ref[layer] = new
        rel_c_ref[layer] = new.astype(BF16)


def fused(
    entity_table, entity_rows, entity_cols, relation_table, relation_rows, relation_cols,
    requests, relation_requests, src_slot, dst_slot, relation_ids, edge_valid, neg_slot,
):
    n_mp, n_dp = lax.axis_size("mp"), lax.axis_size("dp")
    devices = n_dp * n_mp
    cap = requests.shape[3]
    slots = devices * cap
    negatives = neg_slot.shape[2] * n_mp
    ent_t = entity_table.T
    rel_t = jnp.swapaxes(relation_table, 1, 2)
    width, owned = ent_t.shape
    layers, _, owned_rel = rel_t.shape
    batches, edges = src_slot.shape
    main = width // LANES * LANES
    padded_rel = -(-owned_rel // LANES) * LANES
    V, sem = pltpu.VMEM, pltpu.SemaphoreType.DMA
    vmem = pl.BlockSpec(memory_space=pltpu.VMEM)
    hbm = pl.BlockSpec(memory_space=pl.ANY)
    shape = jax.ShapeDtypeStruct
    args = (
        ent_t, rel_t, requests, relation_requests, src_slot, dst_slot, relation_ids, edge_valid, neg_slot,
        entity_rows[None], relation_rows, entity_cols[None], relation_cols,
    )
    outs = [
        shape((width, slots), F32), shape((width, slots), F32), shape((slots, LANES), jnp.int32),
        shape((1, owned), F32), shape((layers, owned_rel), F32), shape((1, width), F32), shape((layers, width), F32),
        shape((width, LANES), F32), shape((8, LANES), F32),
    ]
    many = sem((devices,))
    ent_back, rel_back, ids, ent_new, rel_new, ent_col, rel_col, steps, loss = pl.pallas_call(
        functools.partial(step_kernel, n_mp, cap, negatives, 32),
        out_shape=outs,
        in_specs=[hbm, hbm] + [vmem] * (len(args) - 2),
        out_specs=[vmem] * len(outs),
        scratch_shapes=[
            V((width, owned), F32), V((layers, width, owned_rel), F32),
            V((2, width, owned), BF16), V((2, width, padded_rel), BF16),
            V((n_dp, n_mp, LANES), jnp.int32), V((devices, 1, LANES), jnp.int32),
            V((devices, cap, main + LANES), F32), V((devices, cap, main), F32),
            V((devices, cap, main + LANES), F32), V((devices, cap, main), F32),
            V((devices, cap, main + LANES), F32), V((devices, cap, main), F32),
            V((n_mp, width + 8, slots), F32),
            V((batches, 2 * slots, edges), BF16), V((batches, slots, edges), BF16),
            V((batches, width, edges), F32), V((batches, width, edges), F32), V((batches, width + AUX, edges), BF16),
            V((2, slots, edges), F32), V((2, slots, edges), BF16),
            V((n_mp, 2 * slots, slots), F32), V((2 * slots, slots), F32), V((slots, slots), F32),
            V((2, width, 2 * slots), BF16), V((n_mp, slots, width + AUX), BF16), V((2, width, n_mp * slots), BF16),
            V((n_mp, slots, LANES), F32),
            V((3, width, slots), F32), V((2, width, slots), F32), V((width, slots), F32),
            V((n_mp, 8, main + LANES), F32), V((n_dp, 8, main + LANES), F32), V((8, LANES), F32),
            sem((2,)), many, many, many, many, many, many, sem((3,)), sem((3,)),
            many, many, many, many, sem((3,)), sem((3,)),
            sem((n_mp,)), sem((n_mp,)), sem((n_dp,)), sem((n_dp,)),
        ],
        compiler_params=pltpu.CompilerParams(
            collective_id=1, has_side_effects=True, vmem_limit_bytes=60 << 20
        ),
        name="step",
    )(*args)
    rows = 80 if width % 80 == 0 else width
    ent_block = pl.BlockSpec((rows, owned), lambda i: (i, 0))
    rel_block = pl.BlockSpec((layers, rows, owned_rel), lambda i: (0, i, 0))
    slot_block = pl.BlockSpec((rows, slots), lambda i: (i, 0))
    fixed = lambda a: pl.BlockSpec(a.shape, lambda i, n=a.ndim: (0,) * n)
    ent_w, ent_g, ent_c, rel_w, rel_g, rel_c = pl.pallas_call(
        update_kernel,
        grid=(width // rows,),
        out_shape=[
            shape(ent_t.shape, F32), shape(ent_t.shape, F32), shape(ent_t.shape, BF16),
            shape(rel_t.shape, F32), shape(rel_t.shape, F32), shape(rel_t.shape, BF16),
        ],
        in_specs=[
            ent_block, rel_block, slot_block, slot_block, fixed(ids), fixed(ent_new), fixed(rel_new),
            pl.BlockSpec((rows, LANES), lambda i: (i, 0)),
        ],
        out_specs=[ent_block] * 3 + [rel_block] * 3,
        scratch_shapes=[V((slots, owned), BF16), V((slots, owned_rel), BF16)],
        compiler_params=pltpu.CompilerParams(vmem_limit_bytes=40 << 20),
        name="update",
    )(ent_t, rel_t, ent_back, rel_back, ids, ent_new, rel_new, steps)
    back = lambda x: jnp.swapaxes(x, -1, -2)
    return (
        loss[0, 0:2], back(ent_w), back(ent_g), ent_new[0], ent_col[0], back(ent_c),
        back(rel_w), back(rel_g), rel_new, rel_col, back(rel_c),
    )


def solution(mesh):
    in_specs = (
        P(("dp", "mp"), None),
        P(("dp", "mp")),
        P(),
        P(None, ("dp", "mp"), None),
        P(None, ("dp", "mp")),
        P(),
        P(("dp", "mp"), None, None, None),
        P(("dp", "mp"), None, None, None),
        P(None, ("dp", "mp")),
        P(None, ("dp", "mp")),
        P(None, ("dp", "mp")),
        P(None, ("dp", "mp")),
        P(None, "dp", "mp"),
    )
    out_specs = (
        P(),
        P(("dp", "mp"), None),
        P(("dp", "mp"), None),
        P(("dp", "mp")),
        P(),
        P(("dp", "mp"), None),
        P(None, ("dp", "mp"), None),
        P(None, ("dp", "mp"), None),
        P(None, ("dp", "mp")),
        P(),
        P(None, ("dp", "mp"), None),
    )

    def step(*args):
        small = args[6].shape[1] * args[6].shape[2] * args[6].shape[3] <= 512
        return (fused if small else shards)(*args)

    return jax.shard_map(step, mesh=mesh, in_specs=in_specs, out_specs=out_specs, check_vma=False)
```

```python
import functools

import jax
import jax.numpy as jnp
from jax import lax
from jax.experimental import pallas as pl
from jax.experimental.pallas import tpu as pltpu
from jax.sharding import PartitionSpec as P

MARGIN = 0.1
EPS_DIST = 1e-06
EPS_SQ = 1e-30
DECAY = 0.5
LEARN = 0.3
CLIP = 0.1
HIGH = lax.Precision.HIGHEST


def score_forward(heads, tails, negative_rows, valid_row):
    offset = heads - tails
    near_dist = jnp.sqrt(jnp.sum(offset * offset, 1) + EPS_DIST)
    cross = jnp.dot(heads, negative_rows.T, precision=HIGH, preferred_element_type=jnp.float32)
    far_dist = jnp.sqrt(
        jnp.sum(heads * heads, 1)[:, None]
        + jnp.sum(negative_rows * negative_rows, 1)[None, :]
        - 2.0 * cross
        + EPS_DIST
    )
    margin_z = MARGIN + near_dist[:, None] - far_dist
    part_sum = jnp.sum(jax.nn.softplus(margin_z) * valid_row[:, None])
    return ((offset, near_dist, far_dist, margin_z), part_sum)


def score_backward(heads, negative_rows, valid_row, kept, pairs):
    offset, near_dist, far_dist, margin_z = kept
    weight = jax.nn.sigmoid(margin_z) * valid_row[:, None] / pairs
    along = weight / far_dist
    pull = jnp.sum(weight, 1) / near_dist
    grad_head = (
        pull[:, None] * offset
        - jnp.sum(along, 1)[:, None] * heads
        + jnp.dot(along, negative_rows, precision=HIGH, preferred_element_type=jnp.float32)
    )
    grad_tail = -pull[:, None] * offset
    return (grad_head, grad_tail, along)


def local_moments(grad, row_moment):
    squares = grad * grad + EPS_SQ
    rows_new = DECAY * row_moment + (1.0 - DECAY) * jnp.mean(squares, 1)
    weighted = jnp.sum(grad * grad / rows_new[:, None], 0)
    return (rows_new, jnp.sum(squares, 0), jnp.sum(rows_new), weighted)


def scaled_update(grad, rows_new, cols_new, row_mean):
    return grad * lax.rsqrt(rows_new[:, None] * cols_new[None, :] / row_mean)


def shards(
    entity_table,
    entity_rows,
    entity_cols,
    relation_table,
    relation_rows,
    relation_cols,
    requests,
    relation_requests,
    src_slot,
    dst_slot,
    relation_ids,
    edge_valid,
    neg_slot,
):
    width = entity_table.shape[1]
    n_data = lax.axis_size("dp")
    n_model = lax.axis_size("mp")
    devices = n_data * n_model
    owned_rel = relation_table.shape[1]
    translation = lax.all_gather(jnp.sum(relation_table, 0), ("dp", "mp"), axis=0, tiled=True)
    rel_wanted = relation_requests[0]
    owner_base = (
        jnp.arange(n_data, dtype=jnp.int32)[:, None] * n_model
        + jnp.arange(n_model, dtype=jnp.int32)[None, :]
    ) * owned_rel
    rel_global = (rel_wanted + owner_base[:, :, None]).reshape(-1)
    valid_all = edge_valid.astype(jnp.float32)
    negatives_total = neg_slot.shape[2] * n_model
    pairs = lax.psum(jnp.sum(valid_all), ("dp", "mp")) * negatives_total
    wanted = requests[0]
    incoming = lax.all_to_all(
        lax.all_to_all(wanted, "dp", split_axis=0, concat_axis=0, tiled=True),
        "mp",
        split_axis=1,
        concat_axis=1,
        tiled=True,
    )
    served = entity_table[incoming]
    fetched = lax.all_to_all(
        lax.all_to_all(served, "dp", split_axis=0, concat_axis=0, tiled=True),
        "mp",
        split_axis=1,
        concat_axis=1,
        tiled=True,
    )
    slot_count = fetched.shape[0] * fetched.shape[1] * fetched.shape[2]
    fetched = fetched.reshape(slot_count, width)
    slot_grad = jnp.zeros((slot_count, width), jnp.float32)
    relation_sum = jnp.zeros((rel_global.shape[0], width), jnp.float32)
    loss_part = jnp.zeros((), jnp.float32)
    for batch_index in range(src_slot.shape[0]):
        valid_row = valid_all[batch_index]
        own_negatives = fetched[neg_slot[batch_index, 0]]
        negative_rows = lax.all_gather(own_negatives, "mp", axis=0, tiled=True)
        rel_rows = rel_global[relation_ids[batch_index]]
        heads = fetched[src_slot[batch_index]] + translation[rel_rows]
        tails = fetched[dst_slot[batch_index]]
        kept, part_sum = score_forward(heads, tails, negative_rows, valid_row)
        loss_part = loss_part + part_sum
        grad_head, grad_tail, along = score_backward(heads, negative_rows, valid_row, kept, pairs)
        pulled = lax.dot_general(
            along,
            heads,
            (((0,), (0,)), ((), ())),
            precision=HIGH,
            preferred_element_type=jnp.float32,
        )
        grad_negative = lax.psum_scatter(
            pulled - jnp.sum(along, 0)[:, None] * negative_rows,
            "mp",
            scatter_dimension=0,
            tiled=True,
        )
        slot_grad = slot_grad.at[src_slot[batch_index]].add(grad_head)
        slot_grad = slot_grad.at[dst_slot[batch_index]].add(grad_tail)
        slot_grad = slot_grad.at[neg_slot[batch_index, 0]].add(grad_negative)
        relation_sum = relation_sum.at[relation_ids[batch_index]].add(grad_head)
    returned = lax.all_to_all(
        lax.all_to_all(
            slot_grad.reshape(served.shape), "dp", split_axis=0, concat_axis=0, tiled=True
        ),
        "mp",
        split_axis=1,
        concat_axis=1,
        tiled=True,
    )
    entity_grad = (
        jnp.zeros(entity_table.shape, jnp.float32)
        .at[incoming.reshape(-1)]
        .add(returned.reshape(-1, width))
    )
    rel_incoming = lax.all_to_all(
        lax.all_to_all(rel_wanted, "dp", split_axis=0, concat_axis=0, tiled=True),
        "mp",
        split_axis=1,
        concat_axis=1,
        tiled=True,
    )
    rel_returned = lax.all_to_all(
        lax.all_to_all(
            relation_sum.reshape(rel_wanted.shape + (width,)),
            "dp",
            split_axis=0,
            concat_axis=0,
            tiled=True,
        ),
        "mp",
        split_axis=1,
        concat_axis=1,
        tiled=True,
    )
    relation_shard = (
        jnp.zeros((owned_rel, width), jnp.float32)
        .at[rel_incoming.reshape(-1)]
        .add(rel_returned.reshape(-1, width))
    )
    layers = relation_table.shape[0]
    relation_grad = jnp.broadcast_to(relation_shard[None], (layers,) + relation_shard.shape)
    entity_count = entity_table.shape[0] * devices
    relation_count = relation_shard.shape[0] * devices
    ent_rows, ent_colsq, ent_rsum, ent_weighted = local_moments(entity_grad, entity_rows)
    rel_rows, rel_colsq, rel_rsum, rel_weighted = jax.vmap(local_moments, in_axes=(None, 0))(
        relation_shard, relation_rows
    )
    totals = lax.psum((loss_part, ent_colsq, ent_rsum, rel_colsq, rel_rsum), ("dp", "mp"))
    loss_total, ent_colsq, ent_rsum, rel_colsq, rel_rsum = totals
    ent_cols = DECAY * entity_cols + (1.0 - DECAY) * ent_colsq / entity_count
    rel_cols = DECAY * relation_cols + (1.0 - DECAY) * rel_colsq / relation_count
    ent_mean = ent_rsum / entity_count
    rel_mean = rel_rsum / relation_count
    ent_update = scaled_update(entity_grad, ent_rows, ent_cols, ent_mean)
    rel_update = jax.vmap(scaled_update, in_axes=(None, 0, 0, 0))(
        relation_shard, rel_rows, rel_cols, rel_mean
    )
    ent_usq, rel_usq = lax.psum(
        (jnp.sum(ent_update * ent_update), jnp.sum(rel_update * rel_update, (1, 2))), ("dp", "mp")
    )
    ent_factor = jnp.maximum(1.0, jnp.sqrt(ent_usq / (entity_count * width)) / CLIP)
    rel_factor = jnp.maximum(1.0, jnp.sqrt(rel_usq / (relation_count * width)) / CLIP)
    entity_weight = entity_table - LEARN * (ent_update / ent_factor)
    relation_weight = relation_table - LEARN * (rel_update / rel_factor[:, None, None])
    loss = jnp.stack([loss_total, pairs])
    return (
        loss,
        entity_weight,
        entity_grad,
        ent_rows,
        ent_cols,
        entity_weight.astype(jnp.bfloat16),
        relation_weight,
        relation_grad,
        rel_rows,
        rel_cols,
        relation_weight.astype(jnp.bfloat16),
    )


F32, BF16 = jnp.float32, jnp.bfloat16
LOG2E = 1.4426950408889634
OUT_OF_REACH = 1e30
AUX = 16
LANES = 128
MESH = pl.DeviceIdType.MESH


def two(x):
    hi = x.astype(BF16)
    return hi, (x - hi.astype(F32)).astype(BF16)


def three(x):
    hi = x.astype(BF16)
    rest = x - hi.astype(F32)
    mid = rest.astype(BF16)
    return hi, mid, (rest - mid.astype(F32)).astype(BF16)


def mm(a, b):
    return lax.dot_general(a, b, (((1,), (0,)), ((), ())), preferred_element_type=F32)


def mm_t(a, b):
    return lax.dot_general(a, b, (((1,), (1,)), ((), ())), preferred_element_type=F32)


def iota(shape, axis):
    return lax.broadcasted_iota(jnp.int32, shape, axis)


def stack_rows(rows, count, width):
    at = iota((count, width), 0)
    out = jnp.zeros((count, width), F32)
    for i, row in enumerate(rows):
        out = jnp.where(at == i, row, out)
    return out


def stack_columns(columns, height):
    at = iota((height, LANES), 1)
    out = jnp.zeros((height, LANES), F32)
    for i, column in enumerate(columns):
        out = jnp.where(at == i, column, out)
    return out


def pack(rows, out, tail):
    devices, cap = out.shape[0], 8
    width = rows.shape[1]
    full, rest = width // LANES, width % LANES
    for k in range(full):
        out[:, k * cap:(k + 1) * cap, :] = rows[:, k * LANES:(k + 1) * LANES].reshape(devices, cap, LANES)
    tail[:, 0:rest] = rows[:, full * LANES:]
    line = jnp.concatenate([tail[pl.ds(s, devices, stride=cap), 0:rest] for s in range(cap)], 1)
    out[:, full * cap:, :] = line.reshape(devices, 1, LANES)


def unpack(block, tail):
    devices, cap = block.shape[0], 8
    full = block.shape[1] // cap
    rest = LANES // cap
    parts = [block[:, k * cap:(k + 1) * cap, :].reshape(devices * cap, LANES) for k in range(full)]
    line = block[:, full * cap:, :].reshape(devices, LANES)
    for s in range(cap):
        tail[pl.ds(s, devices, stride=cap), 0:rest] = line[:, s * rest:(s + 1) * rest]
    return jnp.concatenate(parts + [tail[:, 0:rest]], 1)


class Spread:
    def __init__(self, me, devices, place, src, dst, send_sem, recv_sem):
        self.me, self.devices, self.place = me, devices, place
        self.src, self.dst, self.send_sem, self.recv_sem = src, dst, send_sem, recv_sem

    def copy(self, p, at):
        return pltpu.make_async_remote_copy(
            src_ref=self.src(p),
            dst_ref=self.dst(at),
            send_sem=self.send_sem.at[p],
            recv_sem=self.recv_sem.at[at],
            device_id=self.place(p),
            device_id_type=MESH,
        )

    def each(self, act):
        def step(i, carry):
            act(lax.rem(self.me + i, self.devices))
            return carry

        lax.fori_loop(1, self.devices, step, 0)

    def start(self):
        self.each(lambda p: self.copy(p, self.me).start())

    def arrived(self):
        self.each(lambda p: self.copy(p, p).wait_recv())

    def left(self):
        self.each(lambda p: self.copy(p, self.me).wait_send())


def step_kernel(
    n_mp, cap, negatives, rb,
    ent_ref, rel_ref, req_ref, rel_req_ref, src_ref, dst_ref, rid_ref, val_ref, neg_slot_ref,
    ent_rows_ref, rel_rows_ref, ent_cols_ref, rel_cols_ref,
    ent_back_ref, rel_back_ref, ids_ref, whole_ref, ent_col_ref, rel_col_ref, step_ref, loss_ref,
    ent_s, rel_s, ent_parts, rel_parts, ask_s, asked, out_ent, out_rel, in_ent, in_rel, back_in_ent, back_in_rel,
    packed, tail_s, counts_s, neg_s, oh_s, oh_d, lead_s, gap_s, head_s, sq_s, along_s, a_s, b1_s, b2_s, table, neg_rows, neg_parts, count_s,
    acc_s, gn_s, from_mate, from_across, part_mp, part_dp, loss_s,
    load_sem, ask_send, ask_recv, ent_send, ent_recv, rel_send, rel_recv, mp_send, mp_recv,
    forward_send, forward_recv, count_send, count_recv,
    back_ent_send, back_ent_recv, back_rel_send, back_rel_recv, mate_send, mate_recv,
    sum_mp_send, sum_mp_recv, sum_dp_send, sum_dp_recv,
):
    width, owned = ent_s.shape
    layers, _, owned_rel = rel_s.shape
    devices = out_ent.shape[0]
    n_dp = devices // n_mp
    slots = devices * cap
    batches, edges = src_ref.shape
    main = width // LANES * LANES
    rest = width - main
    dp, mp = lax.axis_index("dp"), lax.axis_index("mp")
    me = dp * n_mp + mp
    mate, across = mp + 1 - 2 * lax.rem(mp, 2), lax.rem(mp + 2, n_mp)
    beyond = mate + across - mp

    def place(p):
        return lax.div(p, n_mp), lax.rem(p, n_mp)

    barrier = pltpu.get_barrier_semaphore()

    def tell(i, carry):
        pl.semaphore_signal(
            barrier, inc=1, device_id=place(lax.rem(me + i, devices)), device_id_type=MESH
        )
        return carry

    lax.fori_loop(1, devices, tell, 0)
    load_ent = pltpu.make_async_copy(ent_ref, ent_s, load_sem.at[0])
    load_rel = pltpu.make_async_copy(rel_ref, rel_s, load_sem.at[1])
    load_ent.start()
    load_rel.start()
    valid = jnp.sum(jnp.sum(val_ref[...], 0, keepdims=True), 1, keepdims=True)
    lane = iota(ask_s.shape, 2)
    ask_s[...] = jnp.where(lane == 2 * cap, valid[None], 0)
    ask_s[:, :, 0:cap] = req_ref[0]
    ask_s[:, :, cap:2 * cap] = rel_req_ref[0]
    asked[me] = ask_s[dp, pl.ds(mp, 1)]
    ask = Spread(
        me, devices, place, lambda p: ask_s.at[place(p)[0], pl.ds(place(p)[1], 1)], lambda p: asked.at[p], ask_send, ask_recv
    )
    pl.semaphore_wait(barrier, devices - 1)

    ask.start()
    load_ent.wait()
    load_rel.wait()
    for i, part in enumerate(two(ent_s[...])):
        ent_parts[i] = part
    if rel_parts.shape[2] > owned_rel:
        rel_parts[:, :, owned_rel:] = jnp.zeros((2, width, rel_parts.shape[2] - owned_rel), BF16)
    for i, part in enumerate(two(sum(rel_s[i] for i in range(layers)))):
        rel_parts[i, :, 0:owned_rel] = part
    ask.arrived()
    wide = jnp.broadcast_to(asked[...], (devices, cap, LANES)).reshape(slots, LANES)
    at, lane = lax.rem(iota(wide.shape, 0), cap), iota(wide.shape, 1)
    ent_id = jnp.sum(jnp.where(lane == at, wide, 0), 1, keepdims=True)
    rel_id = jnp.sum(jnp.where(lane == at + cap, wide, 0), 1, keepdims=True)

    pick = jnp.where(iota((slots, owned), 1) == ent_id, 1.0, 0.0).astype(BF16)
    rows = mm_t(pick, ent_parts[0]) + mm_t(pick, ent_parts[1])
    pick = jnp.where(iota((slots, rel_parts.shape[2]), 1) == rel_id, 1.0, 0.0).astype(BF16)
    rel_rows = mm_t(pick, rel_parts[0]) + mm_t(pick, rel_parts[1])

    def block(ref):
        return lambda p: ref.at[p]

    pack(rows, out_ent, tail_s.at[0])
    give_ent = Spread(me, devices, place, block(out_ent), block(in_ent), ent_send, ent_recv)
    give_ent.start()
    pack(rel_rows, out_rel, tail_s.at[1])
    give_rel = Spread(me, devices, place, block(out_rel), block(in_rel), rel_send, rel_recv)
    give_rel.start()
    in_ent[me] = out_ent[me]
    in_rel[me] = out_rel[me]
    ids_ref[...] = jnp.where(iota(ids_ref.shape, 1) == 0, ent_id, jnp.where(iota(ids_ref.shape, 1) == 1, rel_id, 0))
    valid_all = jnp.sum(jnp.where(iota(asked.shape, 2) == 2 * cap, asked[...], 0), 0)
    pairs = jnp.sum(valid_all, 1, keepdims=True).astype(F32) * negatives
    for m in range(batches):
        slot = iota((slots, edges), 0)
        oh_s[m, 0:slots, :] = jnp.where(slot == src_ref[m:m + 1, :], 1.0, 0.0).astype(BF16)
        oh_s[m, slots:, :] = jnp.where(slot == rid_ref[m:m + 1, :], 1.0, 0.0).astype(BF16)
        oh_d[m] = jnp.where(slot == dst_ref[m:m + 1, :], 1.0, 0.0).astype(BF16)
    hits = [
        jnp.sum(jnp.where(iota((slots, neg_slot_ref.shape[2]), 0) == neg_slot_ref[m], 1.0, 0.0), 1, keepdims=True)
        for m in range(batches)
    ]
    counts_s[mp] = stack_columns(hits, slots).T[0:8]
    count_copies = []
    for i in range(1, n_mp):
        count_copies.append(pltpu.make_async_remote_copy(
            src_ref=counts_s.at[mp], dst_ref=counts_s.at[mp], send_sem=count_send.at[i], recv_sem=count_recv.at[i],
            device_id=(dp, lax.rem(mp + i, n_mp)), device_id_type=MESH,
        ))
        count_copies[-1].start()
    ask.left()

    def forward(p):
        return pltpu.make_async_remote_copy(
            src_ref=in_ent.at[p], dst_ref=packed.at[0, p], send_sem=forward_send.at[p], recv_sem=forward_recv.at[p],
            device_id=(dp, across), device_id_type=MESH,
        )

    forward(me).start()

    def pass_on(p):
        give_ent.copy(p, p).wait_recv()
        forward(p).start()

    give_ent.each(pass_on)

    def hand(i, src, dst):
        return pltpu.make_async_remote_copy(
            src_ref=src, dst_ref=packed.at[dst], send_sem=mp_send.at[i], recv_sem=mp_recv.at[i],
            device_id=(dp, mate), device_id_type=MESH,
        )

    to_mate, onward = hand(0, in_ent, 1), hand(1, packed.at[0], 2)
    to_mate.start()
    own_t = unpack(in_ent, tail_s.at[0]).T
    neg_s[3] = own_t
    for i, part in enumerate(two(own_t)):
        table[i, :, 0:slots] = part
    for m in range(batches):
        lead = mm(table[0, :, 0:slots], oh_s[m, 0:slots, :]) + mm(table[1, :, 0:slots], oh_s[m, 0:slots, :])
        lead_s[m] = lead
        gap_s[m] = lead - mm(table[0, :, 0:slots], oh_d[m]) - mm(table[1, :, 0:slots], oh_d[m])

    give_rel.arrived()
    rel_got = unpack(in_rel, tail_s.at[1]).T
    for i, part in enumerate(two(rel_got)):
        table[i, :, slots:] = part
    bounds, inv_nears = [], []
    for m in range(batches):
        moved = mm(table[0, :, slots:], oh_s[m, slots:, :]) + mm(table[1, :, slots:], oh_s[m, slots:, :])
        head = lead_s[m] + moved
        diff = gap_s[m] + moved
        near2 = jnp.sum(diff * diff, 0, keepdims=True) + EPS_DIST
        inv_near = lax.rsqrt(near2)
        inv_nears.append(inv_near)
        bounds.append(jnp.where(val_ref[m:m + 1, :] > 0, (MARGIN + near2 * inv_near) * LOG2E, -OUT_OF_REACH))
        norm = three((jnp.sum(head * head, 0, keepdims=True) + EPS_DIST) * (LOG2E * LOG2E))
        ones = jnp.ones((1, edges), F32)
        head_s[m, 0:width, :] = head.astype(BF16)
        head_s[m, width:, :] = stack_rows([ones] * 3 + [part.astype(F32) for part in norm], AUX, edges).astype(BF16)

    order = (across, beyond, mate, mp)

    def ready(g):
        if g == 0:
            def came(p, carry):
                forward(p).wait_recv()
                return carry

            lax.fori_loop(0, devices, came, 0)
            onward.start()
            for i in range(1, n_mp):
                from_mp = lax.rem(mp + n_mp - i, n_mp)
                pltpu.make_async_remote_copy(
                    src_ref=counts_s.at[mp], dst_ref=counts_s.at[from_mp], send_sem=count_send.at[i],
                    recv_sem=count_recv.at[i], device_id=(dp, from_mp), device_id_type=MESH,
                ).wait_recv()
        elif g == 1:
            onward.wait_recv()
        elif g == 2:
            to_mate.wait_recv()
        if g < 3:
            neg_s[g] = unpack(packed.at[(0, 2, 1)[g]], tail_s.at[0]).T
        n = neg_s[g]
        norm = three(jnp.sum(n * n, 0, keepdims=True) * (LOG2E * LOG2E))
        ones = jnp.ones((1, slots), F32)
        extra = stack_rows([part.astype(F32) for part in norm] + [ones] * 3, AUX, slots)
        neg_rows[g] = jnp.concatenate([n * (-2.0 * LOG2E * LOG2E), extra], 0).T.astype(BF16)
        for i, part in enumerate(two(n)):
            neg_parts[i, :, g * slots:(g + 1) * slots] = part
        blank = jnp.zeros((LANES - 8, slots), F32)
        count_s[g] = jnp.concatenate([counts_s[order[g]], blank], 0).T

    loss_s[...] = jnp.zeros_like(loss_s)
    weight = [jnp.zeros((8, edges), F32) for _ in range(batches)]
    pulls = [jnp.zeros((8, edges), F32) for _ in range(batches)]

    steps = [(g, m) for g in range(n_mp) for m in range(batches)]
    pieces = slots // rb

    def distances(i, b):
        g, m = steps[i]
        part = slice(b * edges // pieces, (b + 1) * edges // pieces)
        sq_s[i % 2, :, part] = mm(neg_rows[g], head_s[m, :, part])

    def pair_terms(i, b):
        g, m = steps[i]
        span = slice(b * rb, (b + 1) * rb)
        count = count_s[g, span, m:m + 1]
        square = jnp.maximum(sq_s[i % 2, span, :], 1e-20)
        inv_far = lax.rsqrt(square)
        t = square * inv_far - bounds[m]
        sig = pl.reciprocal(1.0 + jnp.exp2(t), approx=True)
        rest_sig = 1.0 - sig
        low, high = jnp.minimum(sig, rest_sig), jnp.maximum(sig, rest_sig)
        w = count * sig
        pulls[m] = pulls[m] + jnp.sum(w.reshape(rb // 8, 8, edges), 0)
        w = w * inv_far
        weight[m] = weight[m] + jnp.sum(w.reshape(rb // 8, 8, edges), 0)
        along_s[i % 2, span, :] = w.astype(BF16)
        q = jnp.zeros((rb, LANES), F32)
        over = jnp.zeros((rb, LANES), F32)
        for k in range(edges // LANES):
            part = slice(k * LANES, (k + 1) * LANES)
            q = q * high[:, part] + low[:, part]
            over = over + jnp.minimum(t[:, part], 0.0)
        term = count * (-jnp.log(1.0 - q) - over * (1.0 / LOG2E))
        loss_s[...] += jnp.sum(term.reshape(rb // 8, 8, LANES), 0)

    def by_slot(i, half):
        g, m = steps[i]
        rows = slice(half * slots, (half + 1) * slots)
        part = mm_t(oh_s[m, rows, :], along_s[i % 2])
        a_s[g, rows, :] = part if m == 0 else a_s[g, rows, :] + part

    def grads_of(g):
        total = a_s[g] * LOG2E
        hi, lo = two(total)
        whole = jnp.sum(total[0:slots], 0, keepdims=True)
        cols = slice(g * slots, (g + 1) * slots)
        slot_part = mm_t(hi, neg_parts[0, :, cols]) + mm_t(hi, neg_parts[1, :, cols]) + mm_t(lo, neg_parts[0, :, cols])
        acc_s[...] = slot_part if g == 0 else acc_s[...] + slot_part
        return mm(table[0], hi) + mm(table[1], hi) + mm(table[0], lo) - whole * neg_s[g]

    def swap(i, src, dst, to):
        return pltpu.make_async_remote_copy(
            src_ref=src, dst_ref=dst, send_sem=mate_send.at[i], recv_sem=mate_recv.at[i],
            device_id=(dp, to), device_id_type=MESH,
        )

    through = swap(0, gn_s.at[0], from_mate.at[0], mate)
    over_x = swap(1, gn_s.at[1], from_across, across)
    direct = swap(2, gn_s.at[2], from_mate.at[1], mate)
    def group_done(g):
        grad = grads_of(g)
        if g == 0:
            gn_s[1] = grad
        elif g == 1:
            gn_s[0] = grad
            through.start()
        elif g == 2:
            gn_s[2] = grad
            direct.start()
        else:
            gn_s[3] = grad

    ready(0)
    for b in range(pieces):
        distances(0, b)
    for i in range(len(steps)):
        if i + 1 < len(steps) and steps[i + 1][1] == 0:
            ready(steps[i + 1][0])
        for b in range(pieces):
            if i + 1 < len(steps):
                distances(i + 1, b)
            pair_terms(i, b)
        by_slot(i, 0)
        by_slot(i, 1)
        if steps[i][1] == batches - 1:
            group_done(steps[i][0])
        if i == 2 * batches:
            through.wait_recv()
            gn_s[1] = gn_s[1] + from_mate[0]
            over_x.start()

    for m in range(batches):
        pull = jnp.sum(pulls[m], 0, keepdims=True) * inv_nears[m]
        excess = pull - jnp.sum(weight[m], 0, keepdims=True) * LOG2E
        slot = iota((slots, edges), 0)
        part = sum(
            mm_t(oh_s[m], jnp.where(slot == dst_ref[m:m + 1, :], piece.astype(F32), 0.0).astype(BF16)) for piece in two(pull)
        )
        b1_s[...] = part if m == 0 else b1_s[...] + part
        part = sum(
            mm_t(oh_s[m, 0:slots, :], jnp.where(slot == rid_ref[m:m + 1, :], piece.astype(F32), 0.0).astype(BF16))
            for piece in two(excess)
        )
        b2_s[...] = part if m == 0 else b2_s[...] + part
    sd, rd, sr = b1_s[0:slots, :], b1_s[slots:, :], b2_s[...]
    eye = iota((slots, slots), 0) == iota((slots, slots), 1)
    ss = jnp.where(eye, jnp.sum(sr, 1, keepdims=True) + jnp.sum(sd, 0, keepdims=True), 0.0) - sd - sd.T
    rr = jnp.where(eye, jnp.sum(sr, 0, keepdims=True), 0.0)
    cross = sr - rd.T

    def grads(lo, hi, left, right):
        kept = two(jnp.concatenate([left, right], 1))
        return acc_s[lo:hi, :] + mm_t(kept[0], table[0]) + mm_t(kept[0], table[1]) + mm_t(kept[1], table[0])

    grad_rel = grads(slots, 2 * slots, cross.T, rr)
    give_ent.left()
    give_rel.left()
    pack(grad_rel, out_rel, tail_s.at[1])
    back_rel = Spread(me, devices, place, block(out_rel), block(back_in_rel), back_rel_send, back_rel_recv)
    back_ent = Spread(me, devices, place, block(out_ent), block(back_in_ent), back_ent_send, back_ent_recv)
    back_rel.start()
    grad_ent = grads(0, slots, ss, cross)
    direct.wait_recv()
    over_x.wait_recv()
    grad_ent = grad_ent + (gn_s[3] + from_mate[1] + from_across[...]).T
    pack(grad_ent, out_ent, tail_s.at[0])
    back_ent.start()
    back_in_rel[me] = out_rel[me]
    back_in_ent[me] = out_ent[me]

    def same_rows(column, rows, height):
        row = jnp.broadcast_to(column.astype(F32), (slots, LANES)).T[0:1]
        same = jnp.where(column.astype(F32) == row, 1.0, 0.0)
        share_of = 1.0 / jnp.sum(same, 1, keepdims=True)
        hit = iota((slots, height), 1) == column
        old = [jnp.sum(jnp.where(hit, r, 0.0), 1, keepdims=True) for r in rows]
        kept = [jnp.sum(DECAY * r + (1.0 - DECAY) * EPS_SQ, 1, keepdims=True) for r in rows]
        return same.astype(BF16), share_of, old, kept

    ent_same = same_rows(ent_id, [ent_rows_ref[...]], owned)
    rel_same = same_rows(rel_id, [rel_rows_ref[layer:layer + 1, :] for layer in range(layers)], owned_rel)
    scale = 1.0 / pairs

    def row_sums(back, same, share_of, old, kept):
        grad = sum(mm(same, part) for part in two(back))
        square = grad * grad
        whole = jnp.sum(square, 1, keepdims=True)
        moment = (1.0 - DECAY) / width * whole
        out = [jnp.sum(square * share_of, 0, keepdims=True)]
        sums = []
        for o, k in zip(old, kept):
            new = DECAY * o + (1.0 - DECAY) * EPS_SQ + moment
            out.append(jnp.sum(square * (share_of / new), 0, keepdims=True))
            sums.append(k + jnp.sum(moment * share_of, 0, keepdims=True))
        return whole, out, sums

    back_rel.arrived()
    rel_back = unpack(back_in_rel, tail_s.at[1]) * scale
    rel_whole, more_rows, more_sums = row_sums(rel_back, *rel_same)
    back_ent.arrived()
    ent_back = unpack(back_in_ent, tail_s.at[0]) * scale
    ent_whole, rows, sums = row_sums(ent_back, *ent_same)
    rows = rows + more_rows
    scalars = [jnp.sum(jnp.sum(loss_s[...], 0, keepdims=True), 1, keepdims=True)] + sums + more_sums
    full = main // LANES
    tails = [row[:, main:] for row in rows] + scalars
    tails.append(jnp.zeros((1, LANES - rest * len(rows) - len(scalars)), F32))
    lines = [row[:, i * LANES:(i + 1) * LANES] for row in rows for i in range(full)]
    part_mp[mp] = stack_rows(lines + [jnp.concatenate(tails, 1)], 16, LANES)

    def share(axis, size, at, buffer, send, recv, meanwhile):
        copies = []
        for i in range(1, size):
            copies.append(pltpu.make_async_remote_copy(
                src_ref=buffer.at[at], dst_ref=buffer.at[at], send_sem=send.at[i], recv_sem=recv.at[i],
                device_id={axis: lax.rem(at + i, size)}, device_id_type=MESH,
            ))
            copies[-1].start()
        meanwhile()
        for i in range(1, size):
            came = lax.rem(at + size - i, size)
            pltpu.make_async_remote_copy(
                src_ref=buffer.at[came], dst_ref=buffer.at[came], send_sem=send.at[i], recv_sem=recv.at[i],
                device_id={axis: came}, device_id_type=MESH,
            ).wait_recv()
        return copies

    def write_out():
        ent_back_ref[...] = ent_back.T
        rel_back_ref[...] = rel_back.T
        lane = iota(whole_ref.shape, 1)
        whole_ref[...] = jnp.where(lane == 0, ent_whole, jnp.where(lane == 1, rel_whole, 0.0))

    def settle():
        for copy in [to_mate, onward, through, over_x, direct] + count_copies:
            copy.wait_send()

        def gone(p, carry):
            forward(p).wait_send()
            return carry

        lax.fori_loop(0, devices, gone, 0)
        back_rel.left()
        back_ent.left()

    copies = share("mp", n_mp, mp, part_mp, sum_mp_send, sum_mp_recv, write_out)
    part_dp[dp] = jnp.sum(part_mp[...], 0)
    copies += share("dp", n_dp, dp, part_dp, sum_dp_send, sum_dp_recv, settle)
    total = jnp.sum(part_dp[...], 0)
    last = total[len(lines):len(lines) + 1, :]
    summed = [
        jnp.concatenate(
            [total[i * full + k:i * full + k + 1, :] for k in range(full)] + [last[:, i * rest:(i + 1) * rest]], 1
        )
        for i in range(len(rows))
    ]
    single = [last[:, rest * len(rows) + i:rest * len(rows) + i + 1] for i in range(len(scalars))]

    def finish(cols, col_sum, weighted, moment_sum, height):
        new = DECAY * cols + (1.0 - DECAY) * (col_sum / height + EPS_SQ)
        mean = moment_sum / height
        square = jnp.sum(weighted / new, 1, keepdims=True) * mean
        factor = jnp.maximum(1.0, jnp.sqrt(square / (height * width)) / CLIP)
        return new, LEARN * jnp.sqrt(mean) * lax.rsqrt(new) / factor

    new, step = finish(
        ent_cols_ref[...], summed[0], summed[1], single[1], owned * devices
    )
    ent_col_ref[...] = new
    moves = [step]
    for layer in range(layers):
        new, step = finish(
            rel_cols_ref[layer:layer + 1, :], summed[2], summed[3 + layer], single[2 + layer], owned_rel * devices,
        )
        rel_col_ref[layer:layer + 1, :] = new
        moves.append(step)
    step_ref[...] = stack_rows(moves, LANES, width).T
    lane = iota(loss_ref.shape, 1)
    loss_ref[...] = jnp.where(lane == 0, single[0], jnp.where(lane == 1, pairs, 0.0))
    for copy in copies:
        copy.wait_send()


def update_kernel(
    ent_ref, rel_ref, ent_back_ref, rel_back_ref, ids_ref, whole_ref, ent_rows_ref, rel_rows_ref, step_ref,
    ent_cols_ref, rel_cols_ref, loss_ref,
    ent_w_ref, ent_g_ref, ent_c_ref, rel_w_ref, rel_g_ref, rel_c_ref,
    ent_new_ref, rel_new_ref, ent_col_ref, rel_col_ref, loss_out_ref,
    ent_pick, rel_pick,
):
    layers = rel_ref.shape[0]
    width = ent_cols_ref.shape[1]

    @pl.when(pl.program_id(0) == 0)
    def _():
        def moments(pick, which, old):
            hit = iota(pick.shape, 1) == ids_ref[:, which:which + 1]
            pick[...] = jnp.where(hit, 1.0, 0.0).astype(BF16)
            whole = jnp.max(jnp.where(hit, whole_ref[:, which:which + 1], 0.0), 0, keepdims=True)
            return DECAY * old + (1.0 - DECAY) * (whole / width + EPS_SQ)

        ent_new_ref[...] = moments(ent_pick, 0, ent_rows_ref[...])
        rel_new_ref[...] = moments(rel_pick, 1, rel_rows_ref[...])
        ent_col_ref[...] = ent_cols_ref[...]
        rel_col_ref[...] = rel_cols_ref[...]
        for i in range(2):
            loss_out_ref[i] = loss_ref[0, i]

    grad = sum(mm(part, ent_pick[...]) for part in two(ent_back_ref[...]))
    ent_g_ref[...] = grad
    new = ent_ref[...] - grad * lax.rsqrt(ent_new_ref[...]) * step_ref[:, 0:1]
    ent_w_ref[...] = new
    ent_c_ref[...] = new.astype(BF16)
    grad = sum(mm(part, rel_pick[...]) for part in two(rel_back_ref[...]))
    for layer in range(layers):
        rel_g_ref[layer] = grad
        new = rel_ref[layer] - grad * lax.rsqrt(rel_new_ref[layer:layer + 1, :]) * step_ref[:, layer + 1:layer + 2]
        rel_w_ref[layer] = new
        rel_c_ref[layer] = new.astype(BF16)


def fused(
    entity_table, entity_rows, entity_cols, relation_table, relation_rows, relation_cols,
    requests, relation_requests, src_slot, dst_slot, relation_ids, edge_valid, neg_slot,
):
    n_mp, n_dp = lax.axis_size("mp"), lax.axis_size("dp")
    devices = n_dp * n_mp
    cap = requests.shape[3]
    slots = devices * cap
    negatives = neg_slot.shape[2] * n_mp
    ent_t = entity_table.T
    rel_t = jnp.swapaxes(relation_table, 1, 2)
    width, owned = ent_t.shape
    layers, _, owned_rel = rel_t.shape
    batches, edges = src_slot.shape
    lines = cap * width // LANES
    padded_rel = -(-owned_rel // LANES) * LANES
    V, sem = pltpu.VMEM, pltpu.SemaphoreType.DMA
    vmem = pl.BlockSpec(memory_space=pltpu.VMEM)
    hbm = pl.BlockSpec(memory_space=pl.ANY)
    shape = jax.ShapeDtypeStruct
    args = (
        ent_t, rel_t, requests, relation_requests, src_slot, dst_slot, relation_ids, edge_valid, neg_slot,
        entity_rows[None], relation_rows, entity_cols[None], relation_cols,
    )
    outs = [
        shape((width, slots), F32), shape((width, slots), F32), shape((slots, LANES), jnp.int32),
        shape((slots, LANES), F32), shape((1, width), F32), shape((layers, width), F32),
        shape((width, LANES), F32), shape((8, LANES), F32),
    ]
    many = sem((devices,))
    ent_back, rel_back, ids, whole, ent_col, rel_col, steps, loss = pl.pallas_call(
        functools.partial(step_kernel, n_mp, cap, negatives, 32),
        out_shape=outs,
        in_specs=[hbm, hbm] + [vmem] * (len(args) - 2),
        out_specs=[vmem] * len(outs),
        scratch_shapes=[
            V((width, owned), F32), V((layers, width, owned_rel), F32),
            V((2, width, owned), BF16), V((2, width, padded_rel), BF16),
            V((n_dp, n_mp, LANES), jnp.int32), V((devices, 1, LANES), jnp.int32),
            V((devices, lines, LANES), F32), V((devices, lines, LANES), F32),
            V((devices, lines, LANES), F32), V((devices, lines, LANES), F32),
            V((devices, lines, LANES), F32), V((devices, lines, LANES), F32),
            V((3, devices, lines, LANES), F32), V((2, slots, LANES), F32), V((n_mp, 8, slots), F32), V((n_mp, width, slots), F32),
            V((batches, 2 * slots, edges), BF16), V((batches, slots, edges), BF16),
            V((batches, width, edges), F32), V((batches, width, edges), F32), V((batches, width + AUX, edges), BF16),
            V((2, slots, edges), F32), V((2, slots, edges), BF16),
            V((n_mp, 2 * slots, slots), F32), V((2 * slots, slots), F32), V((slots, slots), F32),
            V((2, width, 2 * slots), BF16), V((n_mp, slots, width + AUX), BF16), V((2, width, n_mp * slots), BF16),
            V((n_mp, slots, LANES), F32),
            V((2 * slots, width), F32), V((4, width, slots), F32), V((2, width, slots), F32), V((width, slots), F32),
            V((n_mp, 16, LANES), F32), V((n_dp, 16, LANES), F32), V((8, LANES), F32),
            sem((2,)), many, many, many, many, many, many, sem((2,)), sem((2,)),
            many, many, sem((n_mp,)), sem((n_mp,)),
            many, many, many, many, sem((3,)), sem((3,)),
            sem((n_mp,)), sem((n_mp,)), sem((n_dp,)), sem((n_dp,)),
        ],
        compiler_params=pltpu.CompilerParams(
            collective_id=1, has_side_effects=True, vmem_limit_bytes=60 << 20
        ),
        name="step",
    )(*args)
    rows = 80 if width % 80 == 0 else width
    ent_block = pl.BlockSpec((rows, owned), lambda i: (i, 0))
    rel_block = pl.BlockSpec((layers, rows, owned_rel), lambda i: (0, i, 0))
    slot_block = pl.BlockSpec((rows, slots), lambda i: (i, 0))
    fixed = lambda a: pl.BlockSpec(a.shape, lambda i, n=a.ndim: (0,) * n)
    smem = pl.BlockSpec(memory_space=pltpu.SMEM)
    ent_rows, rel_rows = entity_rows[None], relation_rows
    small = (ent_rows, rel_rows, ent_col, rel_col)
    ent_w, ent_g, ent_c, rel_w, rel_g, rel_c, ent_new, rel_new, ent_col, rel_col, loss = pl.pallas_call(
        update_kernel,
        grid=(width // rows,),
        out_shape=[
            shape(ent_t.shape, F32), shape(ent_t.shape, F32), shape(ent_t.shape, BF16),
            shape(rel_t.shape, F32), shape(rel_t.shape, F32), shape(rel_t.shape, BF16),
        ] + [shape(a.shape, F32) for a in small] + [shape((2,), F32)],
        in_specs=[
            ent_block, rel_block, slot_block, slot_block, fixed(ids), fixed(whole), fixed(ent_rows), fixed(rel_rows),
            pl.BlockSpec((rows, LANES), lambda i: (i, 0)), fixed(ent_col), fixed(rel_col), smem,
        ],
        out_specs=[ent_block] * 3 + [rel_block] * 3 + [fixed(a) for a in small] + [smem],
        scratch_shapes=[V((slots, owned), BF16), V((slots, owned_rel), BF16)],
        compiler_params=pltpu.CompilerParams(vmem_limit_bytes=60 << 20),
        name="update",
    )(ent_t, rel_t, ent_back, rel_back, ids, whole, ent_rows, rel_rows, steps, ent_col, rel_col, loss)
    back = lambda x: jnp.swapaxes(x, -1, -2)
    return (
        loss, back(ent_w), back(ent_g), ent_new[0], ent_col[0], back(ent_c),
        back(rel_w), back(rel_g), rel_new, rel_col, back(rel_c),
    )


def solution(mesh):
    in_specs = (
        P(("dp", "mp"), None),
        P(("dp", "mp")),
        P(),
        P(None, ("dp", "mp"), None),
        P(None, ("dp", "mp")),
        P(),
        P(("dp", "mp"), None, None, None),
        P(("dp", "mp"), None, None, None),
        P(None, ("dp", "mp")),
        P(None, ("dp", "mp")),
        P(None, ("dp", "mp")),
        P(None, ("dp", "mp")),
        P(None, "dp", "mp"),
    )
    out_specs = (
        P(),
        P(("dp", "mp"), None),
        P(("dp", "mp"), None),
        P(("dp", "mp")),
        P(),
        P(("dp", "mp"), None),
        P(None, ("dp", "mp"), None),
        P(None, ("dp", "mp"), None),
        P(None, ("dp", "mp")),
        P(),
        P(None, ("dp", "mp"), None),
    )

    def step(*args):
        owners_dp, owners_mp, cap = args[6].shape[1:]
        small = owners_mp == 4 and cap == 8 and owners_dp * owners_mp * cap <= 512
        return (fused if small else shards)(*args)

    return jax.shard_map(step, mesh=mesh, in_specs=in_specs, out_specs=out_specs, check_vma=False)
```

```python
import functools

import jax
import jax.numpy as jnp
from jax import lax
from jax.experimental import pallas as pl
from jax.experimental.pallas import tpu as pltpu
from jax.sharding import PartitionSpec as P

MARGIN = 0.1
EPS_DIST = 1e-06
EPS_SQ = 1e-30
DECAY = 0.5
LEARN = 0.3
CLIP = 0.1
HIGH = lax.Precision.HIGHEST


def score_forward(heads, tails, negative_rows, valid_row):
    offset = heads - tails
    near_dist = jnp.sqrt(jnp.sum(offset * offset, 1) + EPS_DIST)
    cross = jnp.dot(heads, negative_rows.T, precision=HIGH, preferred_element_type=jnp.float32)
    far_dist = jnp.sqrt(
        jnp.sum(heads * heads, 1)[:, None]
        + jnp.sum(negative_rows * negative_rows, 1)[None, :]
        - 2.0 * cross
        + EPS_DIST
    )
    margin_z = MARGIN + near_dist[:, None] - far_dist
    part_sum = jnp.sum(jax.nn.softplus(margin_z) * valid_row[:, None])
    return ((offset, near_dist, far_dist, margin_z), part_sum)


def score_backward(heads, negative_rows, valid_row, kept, pairs):
    offset, near_dist, far_dist, margin_z = kept
    weight = jax.nn.sigmoid(margin_z) * valid_row[:, None] / pairs
    along = weight / far_dist
    pull = jnp.sum(weight, 1) / near_dist
    grad_head = (
        pull[:, None] * offset
        - jnp.sum(along, 1)[:, None] * heads
        + jnp.dot(along, negative_rows, precision=HIGH, preferred_element_type=jnp.float32)
    )
    grad_tail = -pull[:, None] * offset
    return (grad_head, grad_tail, along)


def local_moments(grad, row_moment):
    squares = grad * grad + EPS_SQ
    rows_new = DECAY * row_moment + (1.0 - DECAY) * jnp.mean(squares, 1)
    weighted = jnp.sum(grad * grad / rows_new[:, None], 0)
    return (rows_new, jnp.sum(squares, 0), jnp.sum(rows_new), weighted)


def scaled_update(grad, rows_new, cols_new, row_mean):
    return grad * lax.rsqrt(rows_new[:, None] * cols_new[None, :] / row_mean)


def shards(
    entity_table,
    entity_rows,
    entity_cols,
    relation_table,
    relation_rows,
    relation_cols,
    requests,
    relation_requests,
    src_slot,
    dst_slot,
    relation_ids,
    edge_valid,
    neg_slot,
):
    width = entity_table.shape[1]
    n_data = lax.axis_size("dp")
    n_model = lax.axis_size("mp")
    devices = n_data * n_model
    owned_rel = relation_table.shape[1]
    translation = lax.all_gather(jnp.sum(relation_table, 0), ("dp", "mp"), axis=0, tiled=True)
    rel_wanted = relation_requests[0]
    owner_base = (
        jnp.arange(n_data, dtype=jnp.int32)[:, None] * n_model
        + jnp.arange(n_model, dtype=jnp.int32)[None, :]
    ) * owned_rel
    rel_global = (rel_wanted + owner_base[:, :, None]).reshape(-1)
    valid_all = edge_valid.astype(jnp.float32)
    negatives_total = neg_slot.shape[2] * n_model
    pairs = lax.psum(jnp.sum(valid_all), ("dp", "mp")) * negatives_total
    wanted = requests[0]
    incoming = lax.all_to_all(
        lax.all_to_all(wanted, "dp", split_axis=0, concat_axis=0, tiled=True),
        "mp",
        split_axis=1,
        concat_axis=1,
        tiled=True,
    )
    served = entity_table[incoming]
    fetched = lax.all_to_all(
        lax.all_to_all(served, "dp", split_axis=0, concat_axis=0, tiled=True),
        "mp",
        split_axis=1,
        concat_axis=1,
        tiled=True,
    )
    slot_count = fetched.shape[0] * fetched.shape[1] * fetched.shape[2]
    fetched = fetched.reshape(slot_count, width)
    slot_grad = jnp.zeros((slot_count, width), jnp.float32)
    relation_sum = jnp.zeros((rel_global.shape[0], width), jnp.float32)
    loss_part = jnp.zeros((), jnp.float32)
    for batch_index in range(src_slot.shape[0]):
        valid_row = valid_all[batch_index]
        own_negatives = fetched[neg_slot[batch_index, 0]]
        negative_rows = lax.all_gather(own_negatives, "mp", axis=0, tiled=True)
        rel_rows = rel_global[relation_ids[batch_index]]
        heads = fetched[src_slot[batch_index]] + translation[rel_rows]
        tails = fetched[dst_slot[batch_index]]
        kept, part_sum = score_forward(heads, tails, negative_rows, valid_row)
        loss_part = loss_part + part_sum
        grad_head, grad_tail, along = score_backward(heads, negative_rows, valid_row, kept, pairs)
        pulled = lax.dot_general(
            along,
            heads,
            (((0,), (0,)), ((), ())),
            precision=HIGH,
            preferred_element_type=jnp.float32,
        )
        grad_negative = lax.psum_scatter(
            pulled - jnp.sum(along, 0)[:, None] * negative_rows,
            "mp",
            scatter_dimension=0,
            tiled=True,
        )
        slot_grad = slot_grad.at[src_slot[batch_index]].add(grad_head)
        slot_grad = slot_grad.at[dst_slot[batch_index]].add(grad_tail)
        slot_grad = slot_grad.at[neg_slot[batch_index, 0]].add(grad_negative)
        relation_sum = relation_sum.at[relation_ids[batch_index]].add(grad_head)
    returned = lax.all_to_all(
        lax.all_to_all(
            slot_grad.reshape(served.shape), "dp", split_axis=0, concat_axis=0, tiled=True
        ),
        "mp",
        split_axis=1,
        concat_axis=1,
        tiled=True,
    )
    entity_grad = (
        jnp.zeros(entity_table.shape, jnp.float32)
        .at[incoming.reshape(-1)]
        .add(returned.reshape(-1, width))
    )
    rel_incoming = lax.all_to_all(
        lax.all_to_all(rel_wanted, "dp", split_axis=0, concat_axis=0, tiled=True),
        "mp",
        split_axis=1,
        concat_axis=1,
        tiled=True,
    )
    rel_returned = lax.all_to_all(
        lax.all_to_all(
            relation_sum.reshape(rel_wanted.shape + (width,)),
            "dp",
            split_axis=0,
            concat_axis=0,
            tiled=True,
        ),
        "mp",
        split_axis=1,
        concat_axis=1,
        tiled=True,
    )
    relation_shard = (
        jnp.zeros((owned_rel, width), jnp.float32)
        .at[rel_incoming.reshape(-1)]
        .add(rel_returned.reshape(-1, width))
    )
    layers = relation_table.shape[0]
    relation_grad = jnp.broadcast_to(relation_shard[None], (layers,) + relation_shard.shape)
    entity_count = entity_table.shape[0] * devices
    relation_count = relation_shard.shape[0] * devices
    ent_rows, ent_colsq, ent_rsum, ent_weighted = local_moments(entity_grad, entity_rows)
    rel_rows, rel_colsq, rel_rsum, rel_weighted = jax.vmap(local_moments, in_axes=(None, 0))(
        relation_shard, relation_rows
    )
    totals = lax.psum((loss_part, ent_colsq, ent_rsum, rel_colsq, rel_rsum), ("dp", "mp"))
    loss_total, ent_colsq, ent_rsum, rel_colsq, rel_rsum = totals
    ent_cols = DECAY * entity_cols + (1.0 - DECAY) * ent_colsq / entity_count
    rel_cols = DECAY * relation_cols + (1.0 - DECAY) * rel_colsq / relation_count
    ent_mean = ent_rsum / entity_count
    rel_mean = rel_rsum / relation_count
    ent_update = scaled_update(entity_grad, ent_rows, ent_cols, ent_mean)
    rel_update = jax.vmap(scaled_update, in_axes=(None, 0, 0, 0))(
        relation_shard, rel_rows, rel_cols, rel_mean
    )
    ent_usq, rel_usq = lax.psum(
        (jnp.sum(ent_update * ent_update), jnp.sum(rel_update * rel_update, (1, 2))), ("dp", "mp")
    )
    ent_factor = jnp.maximum(1.0, jnp.sqrt(ent_usq / (entity_count * width)) / CLIP)
    rel_factor = jnp.maximum(1.0, jnp.sqrt(rel_usq / (relation_count * width)) / CLIP)
    entity_weight = entity_table - LEARN * (ent_update / ent_factor)
    relation_weight = relation_table - LEARN * (rel_update / rel_factor[:, None, None])
    loss = jnp.stack([loss_total, pairs])
    return (
        loss,
        entity_weight,
        entity_grad,
        ent_rows,
        ent_cols,
        entity_weight.astype(jnp.bfloat16),
        relation_weight,
        relation_grad,
        rel_rows,
        rel_cols,
        relation_weight.astype(jnp.bfloat16),
    )


F32, BF16 = jnp.float32, jnp.bfloat16
LOG2E = 1.4426950408889634
OUT_OF_REACH = 1e30
AUX = 16
LANES = 128
MESH = pl.DeviceIdType.MESH


def two(x):
    hi = x.astype(BF16)
    return hi, (x - hi.astype(F32)).astype(BF16)


def three(x):
    hi = x.astype(BF16)
    rest = x - hi.astype(F32)
    mid = rest.astype(BF16)
    return hi, mid, (rest - mid.astype(F32)).astype(BF16)


def mm(a, b):
    return lax.dot_general(a, b, (((1,), (0,)), ((), ())), preferred_element_type=F32)


def mm_t(a, b):
    return lax.dot_general(a, b, (((1,), (1,)), ((), ())), preferred_element_type=F32)


def iota(shape, axis):
    return lax.broadcasted_iota(jnp.int32, shape, axis)


def stack_rows(rows, count, width):
    at = iota((count, width), 0)
    out = jnp.zeros((count, width), F32)
    for i, row in enumerate(rows):
        out = jnp.where(at == i, row, out)
    return out


def stack_columns(columns, height):
    at = iota((height, LANES), 1)
    out = jnp.zeros((height, LANES), F32)
    for i, column in enumerate(columns):
        out = jnp.where(at == i, column, out)
    return out


def pack(rows, out, tail):
    devices, cap = out.shape[0], 8
    width = rows.shape[1]
    full, rest = width // LANES, width % LANES
    for k in range(full):
        out[:, k * cap:(k + 1) * cap, :] = rows[:, k * LANES:(k + 1) * LANES].reshape(devices, cap, LANES)
    tail[:, 0:rest] = rows[:, full * LANES:]
    line = jnp.concatenate([tail[pl.ds(s, devices, stride=cap), 0:rest] for s in range(cap)], 1)
    out[:, full * cap:, :] = line.reshape(devices, 1, LANES)


def unpack(block, tail):
    devices, cap = block.shape[0], 8
    full = block.shape[1] // cap
    rest = LANES // cap
    parts = [block[:, k * cap:(k + 1) * cap, :].reshape(devices * cap, LANES) for k in range(full)]
    line = block[:, full * cap:, :].reshape(devices, LANES)
    for s in range(cap):
        tail[pl.ds(s, devices, stride=cap), 0:rest] = line[:, s * rest:(s + 1) * rest]
    return jnp.concatenate(parts + [tail[:, 0:rest]], 1)


class Spread:
    def __init__(self, me, devices, place, src, dst, send_sem, recv_sem):
        self.me, self.devices, self.place = me, devices, place
        self.src, self.dst, self.send_sem, self.recv_sem = src, dst, send_sem, recv_sem

    def copy(self, p, at):
        return pltpu.make_async_remote_copy(
            src_ref=self.src(p),
            dst_ref=self.dst(at),
            send_sem=self.send_sem.at[p],
            recv_sem=self.recv_sem.at[at],
            device_id=self.place(p),
            device_id_type=MESH,
        )

    def each(self, act):
        def step(i, carry):
            act(lax.rem(self.me + i, self.devices))
            return carry

        lax.fori_loop(1, self.devices, step, 0)

    def start(self):
        self.each(lambda p: self.copy(p, self.me).start())

    def arrived(self):
        self.each(lambda p: self.copy(p, p).wait_recv())

    def left(self):
        self.each(lambda p: self.copy(p, self.me).wait_send())


def step_kernel(
    n_mp, cap, negatives, rb,
    ent_ref, rel_ref, req_ref, rel_req_ref, src_ref, dst_ref, rid_ref, val_ref, neg_slot_ref,
    ent_rows_ref, rel_rows_ref, ent_cols_ref, rel_cols_ref,
    ent_back_ref, rel_back_ref, ids_ref, whole_ref, ent_col_ref, rel_col_ref, step_ref, loss_ref,
    ent_s, rel_s, ent_parts, rel_parts, ask_s, asked, out_ent, out_rel, in_ent, in_rel, back_in_ent, back_in_rel,
    packed, tail_s, counts_s, neg_s, oh_s, oh_d, lead_s, gap_s, head_s, along_s, a_s, b1_s, b2_s, table, neg_rows, neg_parts, count_s,
    acc_s, gn_s, from_mate, from_across, part_mp, part_dp, loss_s, pull_s, weight_s, near_s, bound_s,
    load_sem, ask_send, ask_recv, ent_send, ent_recv, rel_send, rel_recv, mp_send, mp_recv,
    forward_send, forward_recv, count_send, count_recv,
    back_ent_send, back_ent_recv, back_rel_send, back_rel_recv, mate_send, mate_recv,
    sum_mp_send, sum_mp_recv, sum_dp_send, sum_dp_recv,
):
    width, owned = ent_s.shape
    layers, _, owned_rel = rel_s.shape
    devices = out_ent.shape[0]
    n_dp = devices // n_mp
    slots = devices * cap
    batches, edges = src_ref.shape
    main = width // LANES * LANES
    rest = width - main
    dp, mp = lax.axis_index("dp"), lax.axis_index("mp")
    me = dp * n_mp + mp
    mate, across = mp + 1 - 2 * lax.rem(mp, 2), lax.rem(mp + 2, n_mp)
    beyond = mate + across - mp

    def place(p):
        return lax.div(p, n_mp), lax.rem(p, n_mp)

    def by_columns(size, act):
        blocks = edges // size

        def step(t, carry):
            act(lax.div(t, blocks), pl.ds(pl.multiple_of(lax.rem(t, blocks) * size, size), size))
            return carry

        lax.fori_loop(0, batches * blocks, step, 0)

    block_of = lambda size: size if edges % size == 0 else edges
    narrow, broad = block_of(512), block_of(1024)

    barrier = pltpu.get_barrier_semaphore()

    def tell(i, carry):
        pl.semaphore_signal(
            barrier, inc=1, device_id=place(lax.rem(me + i, devices)), device_id_type=MESH
        )
        return carry

    lax.fori_loop(1, devices, tell, 0)
    load_ent = pltpu.make_async_copy(ent_ref, ent_s, load_sem.at[0])
    load_rel = pltpu.make_async_copy(rel_ref, rel_s, load_sem.at[1])
    load_ent.start()
    load_rel.start()
    valid = jnp.sum(jnp.sum(val_ref[...], 0, keepdims=True), 1, keepdims=True)
    lane = iota(ask_s.shape, 2)
    ask_s[...] = jnp.where(lane == 2 * cap, valid[None], 0)
    ask_s[:, :, 0:cap] = req_ref[0]
    ask_s[:, :, cap:2 * cap] = rel_req_ref[0]
    asked[me] = ask_s[dp, pl.ds(mp, 1)]
    ask = Spread(
        me, devices, place, lambda p: ask_s.at[place(p)[0], pl.ds(place(p)[1], 1)], lambda p: asked.at[p], ask_send, ask_recv
    )
    pl.semaphore_wait(barrier, devices - 1)

    ask.start()
    load_ent.wait()
    load_rel.wait()
    rows_at = 80 if width % 80 == 0 else width

    def split(t, carry):
        span = pl.ds(pl.multiple_of(t * rows_at, rows_at), rows_at)
        for i, part in enumerate(two(ent_s[span, :])):
            ent_parts[i, span, :] = part
        for i, part in enumerate(two(sum(rel_s[i, span, :] for i in range(layers)))):
            rel_parts[i, span, 0:owned_rel] = part
        return carry

    lax.fori_loop(0, width // rows_at, split, 0)
    if rel_parts.shape[2] > owned_rel:
        rel_parts[:, :, owned_rel:] = jnp.zeros((2, width, rel_parts.shape[2] - owned_rel), BF16)
    ask.arrived()
    wide = jnp.broadcast_to(asked[...], (devices, cap, LANES)).reshape(slots, LANES)
    at, lane = lax.rem(iota(wide.shape, 0), cap), iota(wide.shape, 1)
    ent_id = jnp.sum(jnp.where(lane == at, wide, 0), 1, keepdims=True)
    rel_id = jnp.sum(jnp.where(lane == at + cap, wide, 0), 1, keepdims=True)

    pick = jnp.where(iota((slots, owned), 1) == ent_id, 1.0, 0.0).astype(BF16)
    rows = mm_t(pick, ent_parts[0]) + mm_t(pick, ent_parts[1])
    pick = jnp.where(iota((slots, rel_parts.shape[2]), 1) == rel_id, 1.0, 0.0).astype(BF16)
    rel_rows = mm_t(pick, rel_parts[0]) + mm_t(pick, rel_parts[1])

    def block(ref):
        return lambda p: ref.at[p]

    pack(rows, out_ent, tail_s.at[0])
    give_ent = Spread(me, devices, place, block(out_ent), block(in_ent), ent_send, ent_recv)
    give_ent.start()
    pack(rel_rows, out_rel, tail_s.at[1])
    give_rel = Spread(me, devices, place, block(out_rel), block(in_rel), rel_send, rel_recv)
    give_rel.start()
    in_ent[me] = out_ent[me]
    in_rel[me] = out_rel[me]
    ids_ref[...] = jnp.where(iota(ids_ref.shape, 1) == 0, ent_id, jnp.where(iota(ids_ref.shape, 1) == 1, rel_id, 0))
    valid_all = jnp.sum(jnp.where(iota(asked.shape, 2) == 2 * cap, asked[...], 0), 0)
    pairs = jnp.sum(valid_all, 1, keepdims=True).astype(F32) * negatives
    slot = iota((slots, narrow), 0)

    def mark(m, cols):
        row = pl.ds(m, 1)
        oh_s[m, 0:slots, cols] = jnp.where(slot == src_ref[row, cols], 1.0, 0.0).astype(BF16)
        oh_s[m, slots:, cols] = jnp.where(slot == rid_ref[row, cols], 1.0, 0.0).astype(BF16)
        oh_d[m, :, cols] = jnp.where(slot == dst_ref[row, cols], 1.0, 0.0).astype(BF16)

    by_columns(narrow, mark)
    hits = [
        jnp.sum(jnp.where(iota((slots, neg_slot_ref.shape[2]), 0) == neg_slot_ref[m], 1.0, 0.0), 1, keepdims=True)
        for m in range(batches)
    ]
    counts_s[mp] = stack_columns(hits, slots).T[0:8]
    count_copies = []
    for i in range(1, n_mp):
        count_copies.append(pltpu.make_async_remote_copy(
            src_ref=counts_s.at[mp], dst_ref=counts_s.at[mp], send_sem=count_send.at[i], recv_sem=count_recv.at[i],
            device_id=(dp, lax.rem(mp + i, n_mp)), device_id_type=MESH,
        ))
        count_copies[-1].start()
    ask.left()

    def forward(p):
        return pltpu.make_async_remote_copy(
            src_ref=in_ent.at[p], dst_ref=packed.at[0, p], send_sem=forward_send.at[p], recv_sem=forward_recv.at[p],
            device_id=(dp, across), device_id_type=MESH,
        )

    forward(me).start()

    def pass_on(p):
        give_ent.copy(p, p).wait_recv()
        forward(p).start()

    give_ent.each(pass_on)

    def hand(i, src, dst):
        return pltpu.make_async_remote_copy(
            src_ref=src, dst_ref=packed.at[dst], send_sem=mp_send.at[i], recv_sem=mp_recv.at[i],
            device_id=(dp, mate), device_id_type=MESH,
        )

    to_mate, onward = hand(0, in_ent, 1), hand(1, packed.at[0], 2)
    to_mate.start()
    own_t = unpack(in_ent, tail_s.at[0]).T
    neg_s[3] = own_t
    for i, part in enumerate(two(own_t)):
        table[i, :, 0:slots] = part
    def start_of_head(m, cols):
        lead = mm(table[0, :, 0:slots], oh_s[m, 0:slots, cols]) + mm(table[1, :, 0:slots], oh_s[m, 0:slots, cols])
        lead_s[m, :, cols] = lead
        gap_s[m, :, cols] = lead - mm(table[0, :, 0:slots], oh_d[m, :, cols]) - mm(table[1, :, 0:slots], oh_d[m, :, cols])

    by_columns(narrow, start_of_head)

    give_rel.arrived()
    rel_got = unpack(in_rel, tail_s.at[1]).T
    for i, part in enumerate(two(rel_got)):
        table[i, :, slots:] = part
    def whole_head(m, cols):
        moved = mm(table[0, :, slots:], oh_s[m, slots:, cols]) + mm(table[1, :, slots:], oh_s[m, slots:, cols])
        head = lead_s[m, :, cols] + moved
        diff = gap_s[m, :, cols] + moved
        near2 = jnp.sum(diff * diff, 0, keepdims=True) + EPS_DIST
        inv_near = lax.rsqrt(near2)
        near_s[m, :, cols] = inv_near
        bound_s[m, :, cols] = jnp.where(
            val_ref[pl.ds(m, 1), cols] > 0, (MARGIN + near2 * inv_near) * LOG2E, -OUT_OF_REACH
        )
        norm = three((jnp.sum(head * head, 0, keepdims=True) + EPS_DIST) * (LOG2E * LOG2E))
        ones = jnp.ones_like(near2)
        head_s[m, 0:width, cols] = head.astype(BF16)
        extra = stack_rows([ones] * 3 + [part.astype(F32) for part in norm], AUX, near2.shape[1])
        head_s[m, width:, cols] = extra.astype(BF16)

    by_columns(broad, whole_head)
    order = (across, beyond, mate, mp)

    def ready(g):
        if g == 0:
            def came(p, carry):
                forward(p).wait_recv()
                return carry

            lax.fori_loop(0, devices, came, 0)
            onward.start()
            for i in range(1, n_mp):
                from_mp = lax.rem(mp + n_mp - i, n_mp)
                pltpu.make_async_remote_copy(
                    src_ref=counts_s.at[mp], dst_ref=counts_s.at[from_mp], send_sem=count_send.at[i],
                    recv_sem=count_recv.at[i], device_id=(dp, from_mp), device_id_type=MESH,
                ).wait_recv()
        elif g == 1:
            onward.wait_recv()
        elif g == 2:
            to_mate.wait_recv()
        if g < 3:
            neg_s[g] = unpack(packed.at[(0, 2, 1)[g]], tail_s.at[0]).T
        n = neg_s[g]
        norm = three(jnp.sum(n * n, 0, keepdims=True) * (LOG2E * LOG2E))
        ones = jnp.ones((1, slots), F32)
        extra = stack_rows([part.astype(F32) for part in norm] + [ones] * 3, AUX, slots)
        neg_rows[g] = jnp.concatenate([n * (-2.0 * LOG2E * LOG2E), extra], 0).T.astype(BF16)
        for i, part in enumerate(two(n)):
            neg_parts[i, :, g * slots:(g + 1) * slots] = part
        blank = jnp.zeros((LANES - 8, slots), F32)
        count_s[g] = jnp.concatenate([counts_s[order[g]], blank], 0).T

    loss_s[...] = jnp.zeros_like(loss_s)
    weight = [jnp.zeros((8, edges), F32) for _ in range(batches)]
    pulls = [jnp.zeros((8, edges), F32) for _ in range(batches)]

    steps = [(g, m) for g in range(n_mp) for m in range(batches)]
    pieces = slots // rb

    def distances(i, b):
        g, m = steps[i]
        part = slice(b * edges // pieces, (b + 1) * edges // pieces)
        lead_s[i % 2, 0:slots, part] = mm(neg_rows[g], head_s[m, :, part])

    def pair_terms(i, b):
        g, m = steps[i]
        span = slice(b * rb, (b + 1) * rb)
        count = count_s[g, span, m:m + 1]
        square = jnp.maximum(lead_s[i % 2, span, :], 1e-20)
        inv_far = lax.rsqrt(square)
        t = square * inv_far - bound_s[m]
        sig = pl.reciprocal(1.0 + jnp.exp2(t), approx=True)
        rest_sig = 1.0 - sig
        low, high = jnp.minimum(sig, rest_sig), jnp.maximum(sig, rest_sig)
        w = count * sig
        pulls[m] = pulls[m] + jnp.sum(w.reshape(rb // 8, 8, edges), 0)
        w = w * inv_far
        weight[m] = weight[m] + jnp.sum(w.reshape(rb // 8, 8, edges), 0)
        along_s[i % 2, span, :] = w.astype(BF16)
        q = jnp.zeros((rb, LANES), F32)
        over = jnp.zeros((rb, LANES), F32)
        for k in range(edges // LANES):
            part = slice(k * LANES, (k + 1) * LANES)
            q = q * high[:, part] + low[:, part]
            over = over + jnp.minimum(t[:, part], 0.0)
        term = count * (-jnp.log(1.0 - q) - over * (1.0 / LOG2E))
        loss_s[...] += jnp.sum(term.reshape(rb // 8, 8, LANES), 0)

    def by_slot(i, half):
        g, m = steps[i]
        rows = slice(half * slots, (half + 1) * slots)
        part = mm_t(oh_s[m, rows, :], along_s[i % 2])
        a_s[g, rows, :] = part if m == 0 else a_s[g, rows, :] + part

    def grads_of(g):
        total = a_s[g] * LOG2E
        hi, lo = two(total)
        whole = jnp.sum(total[0:slots], 0, keepdims=True)
        cols = slice(g * slots, (g + 1) * slots)
        slot_part = mm_t(hi, neg_parts[0, :, cols]) + mm_t(hi, neg_parts[1, :, cols]) + mm_t(lo, neg_parts[0, :, cols])
        acc_s[...] = slot_part if g == 0 else acc_s[...] + slot_part
        return mm(table[0], hi) + mm(table[1], hi) + mm(table[0], lo) - whole * neg_s[g]

    def swap(i, src, dst, to):
        return pltpu.make_async_remote_copy(
            src_ref=src, dst_ref=dst, send_sem=mate_send.at[i], recv_sem=mate_recv.at[i],
            device_id=(dp, to), device_id_type=MESH,
        )

    through = swap(0, gn_s.at[0], from_mate.at[0], mate)
    over_x = swap(1, gn_s.at[1], from_across, across)
    direct = swap(2, gn_s.at[2], from_mate.at[1], mate)
    def group_done(g):
        grad = grads_of(g)
        if g == 0:
            gn_s[1] = grad
        elif g == 1:
            gn_s[0] = grad
            through.start()
        elif g == 2:
            gn_s[2] = grad
            direct.start()
        else:
            gn_s[3] = grad

    ready(0)
    for b in range(pieces):
        distances(0, b)
    for i in range(len(steps)):
        if i + 1 < len(steps) and steps[i + 1][1] == 0:
            ready(steps[i + 1][0])
        for b in range(pieces):
            if i + 1 < len(steps):
                distances(i + 1, b)
            pair_terms(i, b)
        by_slot(i, 0)
        by_slot(i, 1)
        if steps[i][1] == batches - 1:
            group_done(steps[i][0])
        if i == 2 * batches:
            through.wait_recv()
            gn_s[1] = gn_s[1] + from_mate[0]
            over_x.start()

    broad_slot = iota((slots, broad), 0)
    for m in range(batches):
        pull_s[m] = pulls[m]
        weight_s[m] = weight[m]
    b1_s[...] = jnp.zeros_like(b1_s)
    b2_s[...] = jnp.zeros_like(b2_s)

    def edge_weights(m, cols):
        row = pl.ds(m, 1)
        pull = jnp.sum(pull_s[m, :, cols], 0, keepdims=True) * near_s[m, :, cols]
        excess = pull - jnp.sum(weight_s[m, :, cols], 0, keepdims=True) * LOG2E
        hit = broad_slot == dst_ref[row, cols]
        b1_s[...] += sum(
            mm_t(oh_s[m, :, cols], jnp.where(hit, piece.astype(F32), 0.0).astype(BF16)) for piece in two(pull)
        )
        hit = broad_slot == rid_ref[row, cols]
        b2_s[...] += sum(
            mm_t(oh_s[m, 0:slots, cols], jnp.where(hit, piece.astype(F32), 0.0).astype(BF16)) for piece in two(excess)
        )

    by_columns(broad, edge_weights)
    sd, rd, sr = b1_s[0:slots, :], b1_s[slots:, :], b2_s[...]
    eye = iota((slots, slots), 0) == iota((slots, slots), 1)
    ss = jnp.where(eye, jnp.sum(sr, 1, keepdims=True) + jnp.sum(sd, 0, keepdims=True), 0.0) - sd - sd.T
    rr = jnp.where(eye, jnp.sum(sr, 0, keepdims=True), 0.0)
    cross = sr - rd.T

    def grads(lo, hi, left, right):
        kept = two(jnp.concatenate([left, right], 1))
        return acc_s[lo:hi, :] + mm_t(kept[0], table[0]) + mm_t(kept[0], table[1]) + mm_t(kept[1], table[0])

    grad_rel = grads(slots, 2 * slots, cross.T, rr)
    give_ent.left()
    give_rel.left()
    pack(grad_rel, out_rel, tail_s.at[1])
    back_rel = Spread(me, devices, place, block(out_rel), block(back_in_rel), back_rel_send, back_rel_recv)
    back_ent = Spread(me, devices, place, block(out_ent), block(back_in_ent), back_ent_send, back_ent_recv)
    back_rel.start()
    grad_ent = grads(0, slots, ss, cross)
    direct.wait_recv()
    over_x.wait_recv()
    grad_ent = grad_ent + (gn_s[3] + from_mate[1] + from_across[...]).T
    pack(grad_ent, out_ent, tail_s.at[0])
    back_ent.start()
    back_in_rel[me] = out_rel[me]
    back_in_ent[me] = out_ent[me]

    def same_rows(column, rows, height):
        row = jnp.broadcast_to(column.astype(F32), (slots, LANES)).T[0:1]
        same = jnp.where(column.astype(F32) == row, 1.0, 0.0)
        share_of = 1.0 / jnp.sum(same, 1, keepdims=True)
        hit = iota((slots, height), 1) == column
        old = [jnp.sum(jnp.where(hit, r, 0.0), 1, keepdims=True) for r in rows]
        kept = [jnp.sum(DECAY * r + (1.0 - DECAY) * EPS_SQ, 1, keepdims=True) for r in rows]
        return same.astype(BF16), share_of, old, kept

    ent_same = same_rows(ent_id, [ent_rows_ref[...]], owned)
    rel_same = same_rows(rel_id, [rel_rows_ref[layer:layer + 1, :] for layer in range(layers)], owned_rel)
    scale = 1.0 / pairs

    def row_sums(back, same, share_of, old, kept):
        grad = sum(mm(same, part) for part in two(back))
        square = grad * grad
        whole = jnp.sum(square, 1, keepdims=True)
        moment = (1.0 - DECAY) / width * whole
        out = [jnp.sum(square * share_of, 0, keepdims=True)]
        sums = []
        for o, k in zip(old, kept):
            new = DECAY * o + (1.0 - DECAY) * EPS_SQ + moment
            out.append(jnp.sum(square * (share_of / new), 0, keepdims=True))
            sums.append(k + jnp.sum(moment * share_of, 0, keepdims=True))
        return whole, out, sums

    back_rel.arrived()
    rel_back = unpack(back_in_rel, tail_s.at[1]) * scale
    rel_whole, more_rows, more_sums = row_sums(rel_back, *rel_same)
    back_ent.arrived()
    ent_back = unpack(back_in_ent, tail_s.at[0]) * scale
    ent_whole, rows, sums = row_sums(ent_back, *ent_same)
    rows = rows + more_rows
    scalars = [jnp.sum(jnp.sum(loss_s[...], 0, keepdims=True), 1, keepdims=True)] + sums + more_sums
    full = main // LANES
    tails = [row[:, main:] for row in rows] + scalars
    tails.append(jnp.zeros((1, LANES - rest * len(rows) - len(scalars)), F32))
    lines = [row[:, i * LANES:(i + 1) * LANES] for row in rows for i in range(full)]
    part_mp[mp] = stack_rows(lines + [jnp.concatenate(tails, 1)], 16, LANES)

    def share(axis, size, at, buffer, send, recv, meanwhile):
        copies = []
        for i in range(1, size):
            copies.append(pltpu.make_async_remote_copy(
                src_ref=buffer.at[at], dst_ref=buffer.at[at], send_sem=send.at[i], recv_sem=recv.at[i],
                device_id={axis: lax.rem(at + i, size)}, device_id_type=MESH,
            ))
            copies[-1].start()
        meanwhile()
        for i in range(1, size):
            came = lax.rem(at + size - i, size)
            pltpu.make_async_remote_copy(
                src_ref=buffer.at[came], dst_ref=buffer.at[came], send_sem=send.at[i], recv_sem=recv.at[i],
                device_id={axis: came}, device_id_type=MESH,
            ).wait_recv()
        return copies

    def write_out():
        ent_back_ref[...] = ent_back.T
        rel_back_ref[...] = rel_back.T
        lane = iota(whole_ref.shape, 1)
        whole_ref[...] = jnp.where(lane == 0, ent_whole, jnp.where(lane == 1, rel_whole, 0.0))

    def settle():
        for copy in [to_mate, onward, through, over_x, direct] + count_copies:
            copy.wait_send()

        def gone(p, carry):
            forward(p).wait_send()
            return carry

        lax.fori_loop(0, devices, gone, 0)
        back_rel.left()
        back_ent.left()

    copies = share("mp", n_mp, mp, part_mp, sum_mp_send, sum_mp_recv, write_out)
    part_dp[dp] = jnp.sum(part_mp[...], 0)
    copies += share("dp", n_dp, dp, part_dp, sum_dp_send, sum_dp_recv, settle)
    total = jnp.sum(part_dp[...], 0)
    last = total[len(lines):len(lines) + 1, :]
    summed = [
        jnp.concatenate(
            [total[i * full + k:i * full + k + 1, :] for k in range(full)] + [last[:, i * rest:(i + 1) * rest]], 1
        )
        for i in range(len(rows))
    ]
    single = [last[:, rest * len(rows) + i:rest * len(rows) + i + 1] for i in range(len(scalars))]

    def finish(cols, col_sum, weighted, moment_sum, height):
        new = DECAY * cols + (1.0 - DECAY) * (col_sum / height + EPS_SQ)
        mean = moment_sum / height
        square = jnp.sum(weighted / new, 1, keepdims=True) * mean
        factor = jnp.maximum(1.0, jnp.sqrt(square / (height * width)) / CLIP)
        return new, LEARN * jnp.sqrt(mean) * lax.rsqrt(new) / factor

    new, step = finish(
        ent_cols_ref[...], summed[0], summed[1], single[1], owned * devices
    )
    ent_col_ref[...] = new
    moves = [step]
    for layer in range(layers):
        new, step = finish(
            rel_cols_ref[layer:layer + 1, :], summed[2], summed[3 + layer], single[2 + layer], owned_rel * devices,
        )
        rel_col_ref[layer:layer + 1, :] = new
        moves.append(step)
    step_ref[...] = stack_rows(moves, LANES, width).T
    lane = iota(loss_ref.shape, 1)
    loss_ref[...] = jnp.where(lane == 0, single[0], jnp.where(lane == 1, pairs, 0.0))
    for copy in copies:
        copy.wait_send()


def update_kernel(
    ent_ref, rel_ref, ent_back_ref, rel_back_ref, ids_ref, whole_ref, ent_rows_ref, rel_rows_ref, step_ref,
    ent_cols_ref, rel_cols_ref, loss_ref,
    ent_w_ref, ent_g_ref, ent_c_ref, rel_w_ref, rel_g_ref, rel_c_ref,
    ent_new_ref, rel_new_ref, ent_col_ref, rel_col_ref, loss_out_ref,
    ent_pick, rel_pick,
):
    layers = rel_ref.shape[0]
    width = ent_cols_ref.shape[1]

    @pl.when(pl.program_id(0) == 0)
    def _():
        def moments(pick, which, old):
            hit = iota(pick.shape, 1) == ids_ref[:, which:which + 1]
            pick[...] = jnp.where(hit, 1.0, 0.0).astype(BF16)
            whole = jnp.max(jnp.where(hit, whole_ref[:, which:which + 1], 0.0), 0, keepdims=True)
            return DECAY * old + (1.0 - DECAY) * (whole / width + EPS_SQ)

        ent_new_ref[...] = moments(ent_pick, 0, ent_rows_ref[...])
        rel_new_ref[...] = moments(rel_pick, 1, rel_rows_ref[...])
        ent_col_ref[...] = ent_cols_ref[...]
        rel_col_ref[...] = rel_cols_ref[...]
        for i in range(2):
            loss_out_ref[i] = loss_ref[0, i]

    grad = sum(mm(part, ent_pick[...]) for part in two(ent_back_ref[...]))
    ent_g_ref[...] = grad
    new = ent_ref[...] - grad * lax.rsqrt(ent_new_ref[...]) * step_ref[:, 0:1]
    ent_w_ref[...] = new
    ent_c_ref[...] = new.astype(BF16)
    grad = sum(mm(part, rel_pick[...]) for part in two(rel_back_ref[...]))
    for layer in range(layers):
        rel_g_ref[layer] = grad
        new = rel_ref[layer] - grad * lax.rsqrt(rel_new_ref[layer:layer + 1, :]) * step_ref[:, layer + 1:layer + 2]
        rel_w_ref[layer] = new
        rel_c_ref[layer] = new.astype(BF16)


def fused(
    entity_table, entity_rows, entity_cols, relation_table, relation_rows, relation_cols,
    requests, relation_requests, src_slot, dst_slot, relation_ids, edge_valid, neg_slot,
):
    n_mp, n_dp = lax.axis_size("mp"), lax.axis_size("dp")
    devices = n_dp * n_mp
    cap = requests.shape[3]
    slots = devices * cap
    negatives = neg_slot.shape[2] * n_mp
    ent_t = entity_table.T
    rel_t = jnp.swapaxes(relation_table, 1, 2)
    width, owned = ent_t.shape
    layers, _, owned_rel = rel_t.shape
    batches, edges = src_slot.shape
    lines = cap * width // LANES
    padded_rel = -(-owned_rel // LANES) * LANES
    V, sem = pltpu.VMEM, pltpu.SemaphoreType.DMA
    vmem = pl.BlockSpec(memory_space=pltpu.VMEM)
    hbm = pl.BlockSpec(memory_space=pl.ANY)
    shape = jax.ShapeDtypeStruct
    args = (
        ent_t, rel_t, requests, relation_requests, src_slot, dst_slot, relation_ids, edge_valid, neg_slot,
        entity_rows[None], relation_rows, entity_cols[None], relation_cols,
    )
    outs = [
        shape((width, slots), F32), shape((width, slots), F32), shape((slots, LANES), jnp.int32),
        shape((slots, LANES), F32), shape((1, width), F32), shape((layers, width), F32),
        shape((width, LANES), F32), shape((8, LANES), F32),
    ]
    many = sem((devices,))
    ent_back, rel_back, ids, whole, ent_col, rel_col, steps, loss = pl.pallas_call(
        functools.partial(step_kernel, n_mp, cap, negatives, 32),
        out_shape=outs,
        in_specs=[hbm, hbm] + [vmem] * (len(args) - 2),
        out_specs=[vmem] * len(outs),
        scratch_shapes=[
            V((width, owned), F32), V((layers, width, owned_rel), F32),
            V((2, width, owned), BF16), V((2, width, padded_rel), BF16),
            V((n_dp, n_mp, LANES), jnp.int32), V((devices, 1, LANES), jnp.int32),
            V((devices, lines, LANES), F32), V((devices, lines, LANES), F32),
            V((devices, lines, LANES), F32), V((devices, lines, LANES), F32),
            V((devices, lines, LANES), F32), V((devices, lines, LANES), F32),
            V((3, devices, lines, LANES), F32), V((2, slots, LANES), F32), V((n_mp, 8, slots), F32), V((n_mp, width, slots), F32),
            V((batches, 2 * slots, edges), BF16), V((batches, slots, edges), BF16),
            V((batches, width, edges), F32), V((batches, width, edges), F32), V((batches, width + AUX, edges), BF16),
            V((2, slots, edges), BF16),
            V((n_mp, 2 * slots, slots), F32), V((2 * slots, slots), F32), V((slots, slots), F32),
            V((2, width, 2 * slots), BF16), V((n_mp, slots, width + AUX), BF16), V((2, width, n_mp * slots), BF16),
            V((n_mp, slots, LANES), F32),
            V((2 * slots, width), F32), V((4, width, slots), F32), V((2, width, slots), F32), V((width, slots), F32),
            V((n_mp, 16, LANES), F32), V((n_dp, 16, LANES), F32), V((8, LANES), F32),
            V((batches, 8, edges), F32), V((batches, 8, edges), F32),
            V((batches, 1, edges), F32), V((batches, 1, edges), F32),
            sem((2,)), many, many, many, many, many, many, sem((2,)), sem((2,)),
            many, many, sem((n_mp,)), sem((n_mp,)),
            many, many, many, many, sem((3,)), sem((3,)),
            sem((n_mp,)), sem((n_mp,)), sem((n_dp,)), sem((n_dp,)),
        ],
        compiler_params=pltpu.CompilerParams(
            collective_id=1, has_side_effects=True, vmem_limit_bytes=60 << 20
        ),
        name="step",
    )(*args)
    rows = 80 if width % 80 == 0 else width
    ent_block = pl.BlockSpec((rows, owned), lambda i: (i, 0))
    rel_block = pl.BlockSpec((layers, rows, owned_rel), lambda i: (0, i, 0))
    slot_block = pl.BlockSpec((rows, slots), lambda i: (i, 0))
    fixed = lambda a: pl.BlockSpec(a.shape, lambda i, n=a.ndim: (0,) * n)
    smem = pl.BlockSpec(memory_space=pltpu.SMEM)
    ent_rows, rel_rows = entity_rows[None], relation_rows
    small = (ent_rows, rel_rows, ent_col, rel_col)
    ent_w, ent_g, ent_c, rel_w, rel_g, rel_c, ent_new, rel_new, ent_col, rel_col, loss = pl.pallas_call(
        update_kernel,
        grid=(width // rows,),
        out_shape=[
            shape(ent_t.shape, F32), shape(ent_t.shape, F32), shape(ent_t.shape, BF16),
            shape(rel_t.shape, F32), shape(rel_t.shape, F32), shape(rel_t.shape, BF16),
        ] + [shape(a.shape, F32) for a in small] + [shape((2,), F32)],
        in_specs=[
            ent_block, rel_block, slot_block, slot_block, fixed(ids), fixed(whole), fixed(ent_rows), fixed(rel_rows),
            pl.BlockSpec((rows, LANES), lambda i: (i, 0)), fixed(ent_col), fixed(rel_col), smem,
        ],
        out_specs=[ent_block] * 3 + [rel_block] * 3 + [fixed(a) for a in small] + [smem],
        scratch_shapes=[V((slots, owned), BF16), V((slots, owned_rel), BF16)],
        compiler_params=pltpu.CompilerParams(vmem_limit_bytes=60 << 20),
        name="update",
    )(ent_t, rel_t, ent_back, rel_back, ids, whole, ent_rows, rel_rows, steps, ent_col, rel_col, loss)
    back = lambda x: jnp.swapaxes(x, -1, -2)
    return (
        loss, back(ent_w), back(ent_g), ent_new[0], ent_col[0], back(ent_c),
        back(rel_w), back(rel_g), rel_new, rel_col, back(rel_c),
    )


def solution(mesh):
    in_specs = (
        P(("dp", "mp"), None),
        P(("dp", "mp")),
        P(),
        P(None, ("dp", "mp"), None),
        P(None, ("dp", "mp")),
        P(),
        P(("dp", "mp"), None, None, None),
        P(("dp", "mp"), None, None, None),
        P(None, ("dp", "mp")),
        P(None, ("dp", "mp")),
        P(None, ("dp", "mp")),
        P(None, ("dp", "mp")),
        P(None, "dp", "mp"),
    )
    out_specs = (
        P(),
        P(("dp", "mp"), None),
        P(("dp", "mp"), None),
        P(("dp", "mp")),
        P(),
        P(("dp", "mp"), None),
        P(None, ("dp", "mp"), None),
        P(None, ("dp", "mp"), None),
        P(None, ("dp", "mp")),
        P(),
        P(None, ("dp", "mp"), None),
    )

    def step(*args):
        owners_dp, owners_mp, cap = args[6].shape[1:]
        fits = args[0].shape[0] <= args[8].shape[1] and args[8].shape[1] % 128 == 0
        small = fits and owners_mp == 4 and cap == 8 and owners_dp * owners_mp * cap <= 512
        return (fused if small else shards)(*args)

    return jax.shard_map(step, mesh=mesh, in_specs=in_specs, out_specs=out_specs, check_vma=False)
```

```python
import functools

import jax
import jax.numpy as jnp
from jax import lax
from jax.experimental import pallas as pl
from jax.experimental.pallas import tpu as pltpu
from jax.sharding import PartitionSpec as P

MARGIN = 0.1
EPS_DIST = 1e-06
EPS_SQ = 1e-30
DECAY = 0.5
LEARN = 0.3
CLIP = 0.1
HIGH = lax.Precision.HIGHEST


def score_forward(heads, tails, negative_rows, valid_row):
    offset = heads - tails
    near_dist = jnp.sqrt(jnp.sum(offset * offset, 1) + EPS_DIST)
    cross = jnp.dot(heads, negative_rows.T, precision=HIGH, preferred_element_type=jnp.float32)
    far_dist = jnp.sqrt(
        jnp.sum(heads * heads, 1)[:, None]
        + jnp.sum(negative_rows * negative_rows, 1)[None, :]
        - 2.0 * cross
        + EPS_DIST
    )
    margin_z = MARGIN + near_dist[:, None] - far_dist
    part_sum = jnp.sum(jax.nn.softplus(margin_z) * valid_row[:, None])
    return ((offset, near_dist, far_dist, margin_z), part_sum)


def score_backward(heads, negative_rows, valid_row, kept, pairs):
    offset, near_dist, far_dist, margin_z = kept
    weight = jax.nn.sigmoid(margin_z) * valid_row[:, None] / pairs
    along = weight / far_dist
    pull = jnp.sum(weight, 1) / near_dist
    grad_head = (
        pull[:, None] * offset
        - jnp.sum(along, 1)[:, None] * heads
        + jnp.dot(along, negative_rows, precision=HIGH, preferred_element_type=jnp.float32)
    )
    grad_tail = -pull[:, None] * offset
    return (grad_head, grad_tail, along)


def local_moments(grad, row_moment):
    squares = grad * grad + EPS_SQ
    rows_new = DECAY * row_moment + (1.0 - DECAY) * jnp.mean(squares, 1)
    weighted = jnp.sum(grad * grad / rows_new[:, None], 0)
    return (rows_new, jnp.sum(squares, 0), jnp.sum(rows_new), weighted)


def scaled_update(grad, rows_new, cols_new, row_mean):
    return grad * lax.rsqrt(rows_new[:, None] * cols_new[None, :] / row_mean)


def shards(
    entity_table,
    entity_rows,
    entity_cols,
    relation_table,
    relation_rows,
    relation_cols,
    requests,
    relation_requests,
    src_slot,
    dst_slot,
    relation_ids,
    edge_valid,
    neg_slot,
):
    width = entity_table.shape[1]
    n_data = lax.axis_size("dp")
    n_model = lax.axis_size("mp")
    devices = n_data * n_model
    owned_rel = relation_table.shape[1]
    translation = lax.all_gather(jnp.sum(relation_table, 0), ("dp", "mp"), axis=0, tiled=True)
    rel_wanted = relation_requests[0]
    owner_base = (
        jnp.arange(n_data, dtype=jnp.int32)[:, None] * n_model
        + jnp.arange(n_model, dtype=jnp.int32)[None, :]
    ) * owned_rel
    rel_global = (rel_wanted + owner_base[:, :, None]).reshape(-1)
    valid_all = edge_valid.astype(jnp.float32)
    negatives_total = neg_slot.shape[2] * n_model
    pairs = lax.psum(jnp.sum(valid_all), ("dp", "mp")) * negatives_total
    wanted = requests[0]
    incoming = lax.all_to_all(
        lax.all_to_all(wanted, "dp", split_axis=0, concat_axis=0, tiled=True),
        "mp",
        split_axis=1,
        concat_axis=1,
        tiled=True,
    )
    served = entity_table[incoming]
    fetched = lax.all_to_all(
        lax.all_to_all(served, "dp", split_axis=0, concat_axis=0, tiled=True),
        "mp",
        split_axis=1,
        concat_axis=1,
        tiled=True,
    )
    slot_count = fetched.shape[0] * fetched.shape[1] * fetched.shape[2]
    fetched = fetched.reshape(slot_count, width)
    slot_grad = jnp.zeros((slot_count, width), jnp.float32)
    relation_sum = jnp.zeros((rel_global.shape[0], width), jnp.float32)
    loss_part = jnp.zeros((), jnp.float32)
    for batch_index in range(src_slot.shape[0]):
        valid_row = valid_all[batch_index]
        own_negatives = fetched[neg_slot[batch_index, 0]]
        negative_rows = lax.all_gather(own_negatives, "mp", axis=0, tiled=True)
        rel_rows = rel_global[relation_ids[batch_index]]
        heads = fetched[src_slot[batch_index]] + translation[rel_rows]
        tails = fetched[dst_slot[batch_index]]
        kept, part_sum = score_forward(heads, tails, negative_rows, valid_row)
        loss_part = loss_part + part_sum
        grad_head, grad_tail, along = score_backward(heads, negative_rows, valid_row, kept, pairs)
        pulled = lax.dot_general(
            along,
            heads,
            (((0,), (0,)), ((), ())),
            precision=HIGH,
            preferred_element_type=jnp.float32,
        )
        grad_negative = lax.psum_scatter(
            pulled - jnp.sum(along, 0)[:, None] * negative_rows,
            "mp",
            scatter_dimension=0,
            tiled=True,
        )
        slot_grad = slot_grad.at[src_slot[batch_index]].add(grad_head)
        slot_grad = slot_grad.at[dst_slot[batch_index]].add(grad_tail)
        slot_grad = slot_grad.at[neg_slot[batch_index, 0]].add(grad_negative)
        relation_sum = relation_sum.at[relation_ids[batch_index]].add(grad_head)
    returned = lax.all_to_all(
        lax.all_to_all(
            slot_grad.reshape(served.shape), "dp", split_axis=0, concat_axis=0, tiled=True
        ),
        "mp",
        split_axis=1,
        concat_axis=1,
        tiled=True,
    )
    entity_grad = (
        jnp.zeros(entity_table.shape, jnp.float32)
        .at[incoming.reshape(-1)]
        .add(returned.reshape(-1, width))
    )
    rel_incoming = lax.all_to_all(
        lax.all_to_all(rel_wanted, "dp", split_axis=0, concat_axis=0, tiled=True),
        "mp",
        split_axis=1,
        concat_axis=1,
        tiled=True,
    )
    rel_returned = lax.all_to_all(
        lax.all_to_all(
            relation_sum.reshape(rel_wanted.shape + (width,)),
            "dp",
            split_axis=0,
            concat_axis=0,
            tiled=True,
        ),
        "mp",
        split_axis=1,
        concat_axis=1,
        tiled=True,
    )
    relation_shard = (
        jnp.zeros((owned_rel, width), jnp.float32)
        .at[rel_incoming.reshape(-1)]
        .add(rel_returned.reshape(-1, width))
    )
    layers = relation_table.shape[0]
    relation_grad = jnp.broadcast_to(relation_shard[None], (layers,) + relation_shard.shape)
    entity_count = entity_table.shape[0] * devices
    relation_count = relation_shard.shape[0] * devices
    ent_rows, ent_colsq, ent_rsum, ent_weighted = local_moments(entity_grad, entity_rows)
    rel_rows, rel_colsq, rel_rsum, rel_weighted = jax.vmap(local_moments, in_axes=(None, 0))(
        relation_shard, relation_rows
    )
    totals = lax.psum((loss_part, ent_colsq, ent_rsum, rel_colsq, rel_rsum), ("dp", "mp"))
    loss_total, ent_colsq, ent_rsum, rel_colsq, rel_rsum = totals
    ent_cols = DECAY * entity_cols + (1.0 - DECAY) * ent_colsq / entity_count
    rel_cols = DECAY * relation_cols + (1.0 - DECAY) * rel_colsq / relation_count
    ent_mean = ent_rsum / entity_count
    rel_mean = rel_rsum / relation_count
    ent_update = scaled_update(entity_grad, ent_rows, ent_cols, ent_mean)
    rel_update = jax.vmap(scaled_update, in_axes=(None, 0, 0, 0))(
        relation_shard, rel_rows, rel_cols, rel_mean
    )
    ent_usq, rel_usq = lax.psum(
        (jnp.sum(ent_update * ent_update), jnp.sum(rel_update * rel_update, (1, 2))), ("dp", "mp")
    )
    ent_factor = jnp.maximum(1.0, jnp.sqrt(ent_usq / (entity_count * width)) / CLIP)
    rel_factor = jnp.maximum(1.0, jnp.sqrt(rel_usq / (relation_count * width)) / CLIP)
    entity_weight = entity_table - LEARN * (ent_update / ent_factor)
    relation_weight = relation_table - LEARN * (rel_update / rel_factor[:, None, None])
    loss = jnp.stack([loss_total, pairs])
    return (
        loss,
        entity_weight,
        entity_grad,
        ent_rows,
        ent_cols,
        entity_weight.astype(jnp.bfloat16),
        relation_weight,
        relation_grad,
        rel_rows,
        rel_cols,
        relation_weight.astype(jnp.bfloat16),
    )


F32, BF16 = jnp.float32, jnp.bfloat16
LOG2E = 1.4426950408889634
OUT_OF_REACH = 1e30
AUX = 16
LANES = 128
MESH = pl.DeviceIdType.MESH


def two(x):
    hi = x.astype(BF16)
    return hi, (x - hi.astype(F32)).astype(BF16)


def three(x):
    hi = x.astype(BF16)
    rest = x - hi.astype(F32)
    mid = rest.astype(BF16)
    return hi, mid, (rest - mid.astype(F32)).astype(BF16)


def mm(a, b):
    return lax.dot_general(a, b, (((1,), (0,)), ((), ())), preferred_element_type=F32)


def mm_t(a, b):
    return lax.dot_general(a, b, (((1,), (1,)), ((), ())), preferred_element_type=F32)


def iota(shape, axis):
    return lax.broadcasted_iota(jnp.int32, shape, axis)


def stack_rows(rows, count, width):
    at = iota((count, width), 0)
    out = jnp.zeros((count, width), F32)
    for i, row in enumerate(rows):
        out = jnp.where(at == i, row, out)
    return out


def stack_columns(columns, height):
    at = iota((height, LANES), 1)
    out = jnp.zeros((height, LANES), F32)
    for i, column in enumerate(columns):
        out = jnp.where(at == i, column, out)
    return out


def pack(rows, out, tail):
    devices, cap = out.shape[0], 8
    width = rows.shape[1]
    full, rest = width // LANES, width % LANES
    for k in range(full):
        out[:, k * cap:(k + 1) * cap, :] = rows[:, k * LANES:(k + 1) * LANES].reshape(devices, cap, LANES)
    tail[:, 0:rest] = rows[:, full * LANES:]
    line = jnp.concatenate([tail[pl.ds(s, devices, stride=cap), 0:rest] for s in range(cap)], 1)
    out[:, full * cap:, :] = line.reshape(devices, 1, LANES)


def unpack(block, tail):
    devices, cap = block.shape[0], 8
    full = block.shape[1] // cap
    rest = LANES // cap
    parts = [block[:, k * cap:(k + 1) * cap, :].reshape(devices * cap, LANES) for k in range(full)]
    line = block[:, full * cap:, :].reshape(devices, LANES)
    for s in range(cap):
        tail[pl.ds(s, devices, stride=cap), 0:rest] = line[:, s * rest:(s + 1) * rest]
    return jnp.concatenate(parts + [tail[:, 0:rest]], 1)


class Spread:
    def __init__(self, me, devices, place, src, dst, send_sem, recv_sem):
        self.me, self.devices, self.place = me, devices, place
        self.src, self.dst, self.send_sem, self.recv_sem = src, dst, send_sem, recv_sem

    def copy(self, p, at):
        return pltpu.make_async_remote_copy(
            src_ref=self.src(p),
            dst_ref=self.dst(at),
            send_sem=self.send_sem.at[p],
            recv_sem=self.recv_sem.at[at],
            device_id=self.place(p),
            device_id_type=MESH,
        )

    def each(self, act):
        def step(i, carry):
            act(lax.rem(self.me + i, self.devices))
            return carry

        lax.fori_loop(1, self.devices, step, 0)

    def start(self):
        self.each(lambda p: self.copy(p, self.me).start())

    def arrived(self):
        self.each(lambda p: self.copy(p, p).wait_recv())

    def left(self):
        self.each(lambda p: self.copy(p, self.me).wait_send())


def step_kernel(
    n_mp, cap, negatives, rb,
    ent_ref, rel_ref, *refs,
):
    inputs, kept = refs[:11], refs[-11:]
    step_body(n_mp, cap, negatives, rb, ent_ref, rel_ref, inputs, *kept, *refs[11:-11])


def step_body(
    n_mp, cap, negatives, rb, ent_ref, rel_ref, inputs,
    req_ref, rel_req_ref, src_ref, dst_ref, rid_ref, val_ref, neg_slot_ref,
    ent_rows_ref, rel_rows_ref, ent_cols_ref, rel_cols_ref,
    ent_back_ref, rel_back_ref, ids_ref, whole_ref, ent_col_ref, rel_col_ref, step_ref, loss_ref,
    ent_s, rel_s, ent_parts, rel_parts, ask_s, asked, out_ent, out_rel, in_ent, in_rel, back_in_ent, back_in_rel,
    packed, tail_s, counts_s, neg_s, oh_s, oh_d, lead_s, gap_s, head_s, along_s, a_s, b1_s, b2_s, table, neg_rows, neg_parts, count_s,
    acc_s, gn_s, from_mate, from_across, part_mp, part_dp, loss_s, pull_s, weight_s, near_s, bound_s,
    load_sem, ask_send, ask_recv, ent_send, ent_recv, rel_send, rel_recv, mp_send, mp_recv,
    forward_send, forward_recv, count_send, count_recv,
    back_ent_send, back_ent_recv, back_rel_send, back_rel_recv, mate_send, mate_recv,
    sum_mp_send, sum_mp_recv, sum_dp_send, sum_dp_recv,
):
    width, owned = ent_s.shape
    layers, _, owned_rel = rel_s.shape
    devices = out_ent.shape[0]
    n_dp = devices // n_mp
    slots = devices * cap
    batches, edges = src_ref.shape
    main = width // LANES * LANES
    rest = width - main
    dp, mp = lax.axis_index("dp"), lax.axis_index("mp")
    me = dp * n_mp + mp
    mate, across = mp + 1 - 2 * lax.rem(mp, 2), lax.rem(mp + 2, n_mp)
    beyond = mate + across - mp

    def place(p):
        return lax.div(p, n_mp), lax.rem(p, n_mp)

    def by_columns(size, act):
        blocks = edges // size

        def step(t, carry):
            act(lax.div(t, blocks), pl.ds(pl.multiple_of(lax.rem(t, blocks) * size, size), size))
            return carry

        lax.fori_loop(0, batches * blocks, step, 0)

    block_of = lambda size: size if edges % size == 0 else edges
    narrow, broad = block_of(512), block_of(2048)

    barrier = pltpu.get_barrier_semaphore()

    def tell(i, carry):
        pl.semaphore_signal(
            barrier, inc=1, device_id=place(lax.rem(me + i, devices)), device_id_type=MESH
        )
        return carry

    lax.fori_loop(1, devices, tell, 0)
    load_ent = pltpu.make_async_copy(ent_ref, ent_s, load_sem.at[0])
    load_rel = pltpu.make_async_copy(rel_ref, rel_s, load_sem.at[1])
    kept = (
        req_ref, rel_req_ref, src_ref, dst_ref, rid_ref, val_ref, neg_slot_ref,
        ent_rows_ref, rel_rows_ref, ent_cols_ref, rel_cols_ref,
    )
    small = [pltpu.make_async_copy(a, b, load_sem.at[2 + i]) for i, (a, b) in enumerate(zip(inputs, kept))]
    for copy in small:
        copy.start()
    load_ent.start()
    load_rel.start()
    for copy in small:
        copy.wait()
    valid = jnp.sum(jnp.sum(val_ref[...], 0, keepdims=True), 1, keepdims=True)
    lane = iota(ask_s.shape, 2)
    ask_s[...] = jnp.where(lane == 2 * cap, valid[None], 0)
    ask_s[:, :, 0:cap] = req_ref[0]
    ask_s[:, :, cap:2 * cap] = rel_req_ref[0]
    asked[me] = ask_s[dp, pl.ds(mp, 1)]
    ask = Spread(
        me, devices, place, lambda p: ask_s.at[place(p)[0], pl.ds(place(p)[1], 1)], lambda p: asked.at[p], ask_send, ask_recv
    )
    pl.semaphore_wait(barrier, devices - 1)

    ask.start()
    load_ent.wait()
    load_rel.wait()
    rows_at = 80 if width % 80 == 0 else width

    def split(t, carry):
        span = pl.ds(pl.multiple_of(t * rows_at, rows_at), rows_at)
        for i, part in enumerate(two(ent_s[span, :])):
            ent_parts[i, span, :] = part
        for i, part in enumerate(two(sum(rel_s[i, span, :] for i in range(layers)))):
            rel_parts[i, span, 0:owned_rel] = part
        return carry

    lax.fori_loop(0, width // rows_at, split, 0)
    if rel_parts.shape[2] > owned_rel:
        rel_parts[:, :, owned_rel:] = jnp.zeros((2, width, rel_parts.shape[2] - owned_rel), BF16)
    ask.arrived()
    wide = jnp.broadcast_to(asked[...], (devices, cap, LANES)).reshape(slots, LANES)
    at, lane = lax.rem(iota(wide.shape, 0), cap), iota(wide.shape, 1)
    ent_id = jnp.sum(jnp.where(lane == at, wide, 0), 1, keepdims=True)
    rel_id = jnp.sum(jnp.where(lane == at + cap, wide, 0), 1, keepdims=True)

    pick = jnp.where(iota((slots, owned), 1) == ent_id, 1.0, 0.0).astype(BF16)
    rows = mm_t(pick, ent_parts[0]) + mm_t(pick, ent_parts[1])
    pick = jnp.where(iota((slots, rel_parts.shape[2]), 1) == rel_id, 1.0, 0.0).astype(BF16)
    rel_rows = mm_t(pick, rel_parts[0]) + mm_t(pick, rel_parts[1])

    def block(ref):
        return lambda p: ref.at[p]

    pack(rows, out_ent, tail_s.at[0])
    give_ent = Spread(me, devices, place, block(out_ent), block(in_ent), ent_send, ent_recv)
    give_ent.start()
    pack(rel_rows, out_rel, tail_s.at[1])
    give_rel = Spread(me, devices, place, block(out_rel), block(in_rel), rel_send, rel_recv)
    give_rel.start()
    in_ent[me] = out_ent[me]
    in_rel[me] = out_rel[me]
    ids_ref[...] = jnp.where(iota(ids_ref.shape, 1) == 0, ent_id, jnp.where(iota(ids_ref.shape, 1) == 1, rel_id, 0))
    valid_all = jnp.sum(jnp.where(iota(asked.shape, 2) == 2 * cap, asked[...], 0), 0)
    pairs = jnp.sum(valid_all, 1, keepdims=True).astype(F32) * negatives
    slot = iota((slots, narrow), 0)

    def mark(m, cols):
        row = pl.ds(m, 1)
        oh_s[m, 0:slots, cols] = jnp.where(slot == src_ref[row, cols], 1.0, 0.0).astype(BF16)
        oh_s[m, slots:, cols] = jnp.where(slot == rid_ref[row, cols], 1.0, 0.0).astype(BF16)
        oh_d[m, :, cols] = jnp.where(slot == dst_ref[row, cols], 1.0, 0.0).astype(BF16)

    by_columns(narrow, mark)
    hits = [
        jnp.sum(jnp.where(iota((slots, neg_slot_ref.shape[2]), 0) == neg_slot_ref[m], 1.0, 0.0), 1, keepdims=True)
        for m in range(batches)
    ]
    counts_s[mp] = stack_columns(hits, slots).T[0:8]
    count_copies = []
    for i in range(1, n_mp):
        count_copies.append(pltpu.make_async_remote_copy(
            src_ref=counts_s.at[mp], dst_ref=counts_s.at[mp], send_sem=count_send.at[i], recv_sem=count_recv.at[i],
            device_id=(dp, lax.rem(mp + i, n_mp)), device_id_type=MESH,
        ))
        count_copies[-1].start()
    ask.left()

    def forward(p):
        return pltpu.make_async_remote_copy(
            src_ref=in_ent.at[p], dst_ref=packed.at[0, p], send_sem=forward_send.at[p], recv_sem=forward_recv.at[p],
            device_id=(dp, across), device_id_type=MESH,
        )

    forward(me).start()

    def pass_on(p):
        give_ent.copy(p, p).wait_recv()
        forward(p).start()

    give_ent.each(pass_on)

    def hand(i, src, dst):
        return pltpu.make_async_remote_copy(
            src_ref=src, dst_ref=packed.at[dst], send_sem=mp_send.at[i], recv_sem=mp_recv.at[i],
            device_id=(dp, mate), device_id_type=MESH,
        )

    to_mate, onward = hand(0, in_ent, 1), hand(1, packed.at[0], 2)
    to_mate.start()
    own_t = unpack(in_ent, tail_s.at[0]).T
    neg_s[3] = own_t
    for i, part in enumerate(two(own_t)):
        table[i, :, 0:slots] = part
    def start_of_head(m, cols):
        lead = mm(table[0, :, 0:slots], oh_s[m, 0:slots, cols]) + mm(table[1, :, 0:slots], oh_s[m, 0:slots, cols])
        lead_s[m, :, cols] = lead
        gap_s[m, :, cols] = lead - mm(table[0, :, 0:slots], oh_d[m, :, cols]) - mm(table[1, :, 0:slots], oh_d[m, :, cols])

    by_columns(narrow, start_of_head)

    give_rel.arrived()
    rel_got = unpack(in_rel, tail_s.at[1]).T
    for i, part in enumerate(two(rel_got)):
        table[i, :, slots:] = part
    def whole_head(m, cols):
        moved = mm(table[0, :, slots:], oh_s[m, slots:, cols]) + mm(table[1, :, slots:], oh_s[m, slots:, cols])
        head = lead_s[m, :, cols] + moved
        diff = gap_s[m, :, cols] + moved
        near2 = jnp.sum(diff * diff, 0, keepdims=True) + EPS_DIST
        inv_near = lax.rsqrt(near2)
        near_s[m, :, cols] = inv_near
        bound_s[m, :, cols] = jnp.where(
            val_ref[pl.ds(m, 1), cols] > 0, (MARGIN + near2 * inv_near) * LOG2E, -OUT_OF_REACH
        )
        norm = three((jnp.sum(head * head, 0, keepdims=True) + EPS_DIST) * (LOG2E * LOG2E))
        ones = jnp.ones_like(near2)
        head_s[m, 0:width, cols] = head.astype(BF16)
        extra = stack_rows([ones] * 3 + [part.astype(F32) for part in norm], AUX, near2.shape[1])
        head_s[m, width:, cols] = extra.astype(BF16)

    by_columns(broad, whole_head)
    order = (across, beyond, mate, mp)

    def ready(g):
        if g == 0:
            def came(p, carry):
                forward(p).wait_recv()
                return carry

            lax.fori_loop(0, devices, came, 0)
            onward.start()
            for i in range(1, n_mp):
                from_mp = lax.rem(mp + n_mp - i, n_mp)
                pltpu.make_async_remote_copy(
                    src_ref=counts_s.at[mp], dst_ref=counts_s.at[from_mp], send_sem=count_send.at[i],
                    recv_sem=count_recv.at[i], device_id=(dp, from_mp), device_id_type=MESH,
                ).wait_recv()
        elif g == 1:
            onward.wait_recv()
        elif g == 2:
            to_mate.wait_recv()
        if g < 3:
            neg_s[g] = unpack(packed.at[(0, 2, 1)[g]], tail_s.at[0]).T
        n = neg_s[g]
        norm = three(jnp.sum(n * n, 0, keepdims=True) * (LOG2E * LOG2E))
        ones = jnp.ones((1, slots), F32)
        extra = stack_rows([part.astype(F32) for part in norm] + [ones] * 3, AUX, slots)
        neg_rows[g] = jnp.concatenate([n * (-2.0 * LOG2E * LOG2E), extra], 0).T.astype(BF16)
        for i, part in enumerate(two(n)):
            neg_parts[i, :, g * slots:(g + 1) * slots] = part
        blank = jnp.zeros((LANES - 8, slots), F32)
        count_s[g] = jnp.concatenate([counts_s[order[g]], blank], 0).T

    loss_s[...] = jnp.zeros_like(loss_s)
    weight = [jnp.zeros((8, edges), F32) for _ in range(batches)]
    pulls = [jnp.zeros((8, edges), F32) for _ in range(batches)]

    steps = [(g, m) for g in range(n_mp) for m in range(batches)]
    pieces = slots // rb

    def distances(i, b):
        g, m = steps[i]
        part = slice(b * edges // pieces, (b + 1) * edges // pieces)
        lead_s[i % 2, 0:slots, part] = mm(neg_rows[g], head_s[m, :, part])

    def pair_terms(i, b):
        g, m = steps[i]
        span = slice(b * rb, (b + 1) * rb)
        count = count_s[g, span, m:m + 1]
        square = jnp.maximum(lead_s[i % 2, span, :], 1e-20)
        inv_far = lax.rsqrt(square)
        t = square * inv_far - bound_s[m]
        sig = pl.reciprocal(1.0 + jnp.exp2(t), approx=True)
        rest_sig = 1.0 - sig
        low, high = jnp.minimum(sig, rest_sig), jnp.maximum(sig, rest_sig)
        w = count * sig
        pulls[m] = pulls[m] + jnp.sum(w.reshape(rb // 8, 8, edges), 0)
        w = w * inv_far
        weight[m] = weight[m] + jnp.sum(w.reshape(rb // 8, 8, edges), 0)
        along_s[i % 2, span, :] = w.astype(BF16)
        q = jnp.zeros((rb, LANES), F32)
        over = jnp.zeros((rb, LANES), F32)
        for k in range(edges // LANES):
            part = slice(k * LANES, (k + 1) * LANES)
            q = q * high[:, part] + low[:, part]
            over = over + jnp.minimum(t[:, part], 0.0)
        term = count * (-jnp.log(1.0 - q) - over * (1.0 / LOG2E))
        loss_s[...] += jnp.sum(term.reshape(rb // 8, 8, LANES), 0)

    def by_slot(i, half):
        g, m = steps[i]
        rows = slice(half * slots, (half + 1) * slots)
        part = mm_t(oh_s[m, rows, :], along_s[i % 2])
        a_s[g, rows, :] = part if m == 0 else a_s[g, rows, :] + part

    def grads_of(g):
        total = a_s[g] * LOG2E
        hi, lo = two(total)
        whole = jnp.sum(total[0:slots], 0, keepdims=True)
        cols = slice(g * slots, (g + 1) * slots)
        slot_part = mm_t(hi, neg_parts[0, :, cols]) + mm_t(hi, neg_parts[1, :, cols]) + mm_t(lo, neg_parts[0, :, cols])
        acc_s[...] = slot_part if g == 0 else acc_s[...] + slot_part
        return mm(table[0], hi) + mm(table[1], hi) + mm(table[0], lo) - whole * neg_s[g]

    def swap(i, src, dst, to):
        return pltpu.make_async_remote_copy(
            src_ref=src, dst_ref=dst, send_sem=mate_send.at[i], recv_sem=mate_recv.at[i],
            device_id=(dp, to), device_id_type=MESH,
        )

    through = swap(0, gn_s.at[0], from_mate.at[0], mate)
    over_x = swap(1, gn_s.at[1], from_across, across)
    direct = swap(2, gn_s.at[2], from_mate.at[1], mate)
    def group_done(g):
        grad = grads_of(g)
        if g == 0:
            gn_s[1] = grad
        elif g == 1:
            gn_s[0] = grad
            through.start()
        elif g == 2:
            gn_s[2] = grad
            direct.start()
        else:
            gn_s[3] = grad

    ready(0)
    for b in range(pieces):
        distances(0, b)
    for i in range(len(steps)):
        if i + 1 < len(steps) and steps[i + 1][1] == 0:
            ready(steps[i + 1][0])
        for b in range(pieces):
            if i + 1 < len(steps):
                distances(i + 1, b)
            pair_terms(i, b)
        by_slot(i, 0)
        by_slot(i, 1)
        if steps[i][1] == batches - 1:
            group_done(steps[i][0])
        if i == 2 * batches:
            through.wait_recv()
            gn_s[1] = gn_s[1] + from_mate[0]
            over_x.start()

    broad_slot = iota((slots, broad), 0)
    for m in range(batches):
        pull_s[m] = pulls[m]
        weight_s[m] = weight[m]
    b1_s[...] = jnp.zeros_like(b1_s)
    b2_s[...] = jnp.zeros_like(b2_s)

    def edge_weights(m, cols):
        row = pl.ds(m, 1)
        pull = jnp.sum(pull_s[m, :, cols], 0, keepdims=True) * near_s[m, :, cols]
        excess = pull - jnp.sum(weight_s[m, :, cols], 0, keepdims=True) * LOG2E
        hit = broad_slot == dst_ref[row, cols]
        b1_s[...] += sum(
            mm_t(oh_s[m, :, cols], jnp.where(hit, piece.astype(F32), 0.0).astype(BF16)) for piece in two(pull)
        )
        hit = broad_slot == rid_ref[row, cols]
        b2_s[...] += sum(
            mm_t(oh_s[m, 0:slots, cols], jnp.where(hit, piece.astype(F32), 0.0).astype(BF16)) for piece in two(excess)
        )

    by_columns(broad, edge_weights)
    sd, rd, sr = b1_s[0:slots, :], b1_s[slots:, :], b2_s[...]
    eye = iota((slots, slots), 0) == iota((slots, slots), 1)
    ss = jnp.where(eye, jnp.sum(sr, 1, keepdims=True) + jnp.sum(sd, 0, keepdims=True), 0.0) - sd - sd.T
    rr = jnp.where(eye, jnp.sum(sr, 0, keepdims=True), 0.0)
    cross = sr - rd.T

    def grads(lo, hi, left, right):
        kept = two(jnp.concatenate([left, right], 1))
        return acc_s[lo:hi, :] + mm_t(kept[0], table[0]) + mm_t(kept[0], table[1]) + mm_t(kept[1], table[0])

    grad_rel = grads(slots, 2 * slots, cross.T, rr)
    give_ent.left()
    give_rel.left()
    pack(grad_rel, out_rel, tail_s.at[1])
    back_rel = Spread(me, devices, place, block(out_rel), block(back_in_rel), back_rel_send, back_rel_recv)
    back_ent = Spread(me, devices, place, block(out_ent), block(back_in_ent), back_ent_send, back_ent_recv)
    back_rel.start()
    grad_ent = grads(0, slots, ss, cross)
    direct.wait_recv()
    over_x.wait_recv()
    grad_ent = grad_ent + (gn_s[3] + from_mate[1] + from_across[...]).T
    pack(grad_ent, out_ent, tail_s.at[0])
    back_ent.start()
    back_in_rel[me] = out_rel[me]
    back_in_ent[me] = out_ent[me]

    def same_rows(column, rows, height):
        row = jnp.broadcast_to(column.astype(F32), (slots, LANES)).T[0:1]
        same = jnp.where(column.astype(F32) == row, 1.0, 0.0)
        share_of = 1.0 / jnp.sum(same, 1, keepdims=True)
        hit = iota((slots, height), 1) == column
        old = [jnp.sum(jnp.where(hit, r, 0.0), 1, keepdims=True) for r in rows]
        kept = [jnp.sum(DECAY * r + (1.0 - DECAY) * EPS_SQ, 1, keepdims=True) for r in rows]
        return same.astype(BF16), share_of, old, kept

    ent_same = same_rows(ent_id, [ent_rows_ref[...]], owned)
    rel_same = same_rows(rel_id, [rel_rows_ref[layer:layer + 1, :] for layer in range(layers)], owned_rel)
    scale = 1.0 / pairs

    def row_sums(back, same, share_of, old, kept):
        grad = sum(mm(same, part) for part in two(back))
        square = grad * grad
        whole = jnp.sum(square, 1, keepdims=True)
        moment = (1.0 - DECAY) / width * whole
        out = [jnp.sum(square * share_of, 0, keepdims=True)]
        sums = []
        for o, k in zip(old, kept):
            new = DECAY * o + (1.0 - DECAY) * EPS_SQ + moment
            out.append(jnp.sum(square * (share_of / new), 0, keepdims=True))
            sums.append(k + jnp.sum(moment * share_of, 0, keepdims=True))
        return whole, out, sums

    back_rel.arrived()
    rel_back = unpack(back_in_rel, tail_s.at[1]) * scale
    rel_whole, more_rows, more_sums = row_sums(rel_back, *rel_same)
    back_ent.arrived()
    ent_back = unpack(back_in_ent, tail_s.at[0]) * scale
    ent_whole, rows, sums = row_sums(ent_back, *ent_same)
    rows = rows + more_rows
    scalars = [jnp.sum(jnp.sum(loss_s[...], 0, keepdims=True), 1, keepdims=True)] + sums + more_sums
    full = main // LANES
    tails = [row[:, main:] for row in rows] + scalars
    tails.append(jnp.zeros((1, LANES - rest * len(rows) - len(scalars)), F32))
    lines = [row[:, i * LANES:(i + 1) * LANES] for row in rows for i in range(full)]
    part_mp[mp] = stack_rows(lines + [jnp.concatenate(tails, 1)], 16, LANES)

    def share(axis, size, at, buffer, send, recv, meanwhile):
        copies = []
        for i in range(1, size):
            copies.append(pltpu.make_async_remote_copy(
                src_ref=buffer.at[at], dst_ref=buffer.at[at], send_sem=send.at[i], recv_sem=recv.at[i],
                device_id={axis: lax.rem(at + i, size)}, device_id_type=MESH,
            ))
            copies[-1].start()
        meanwhile()
        for i in range(1, size):
            came = lax.rem(at + size - i, size)
            pltpu.make_async_remote_copy(
                src_ref=buffer.at[came], dst_ref=buffer.at[came], send_sem=send.at[i], recv_sem=recv.at[i],
                device_id={axis: came}, device_id_type=MESH,
            ).wait_recv()
        return copies

    def write_out():
        ent_back_ref[...] = ent_back.T
        rel_back_ref[...] = rel_back.T
        lane = iota(whole_ref.shape, 1)
        whole_ref[...] = jnp.where(lane == 0, ent_whole, jnp.where(lane == 1, rel_whole, 0.0))

    def settle():
        for copy in [to_mate, onward, through, over_x, direct] + count_copies:
            copy.wait_send()

        def gone(p, carry):
            forward(p).wait_send()
            return carry

        lax.fori_loop(0, devices, gone, 0)
        back_rel.left()
        back_ent.left()

    copies = share("mp", n_mp, mp, part_mp, sum_mp_send, sum_mp_recv, write_out)
    part_dp[dp] = jnp.sum(part_mp[...], 0)
    copies += share("dp", n_dp, dp, part_dp, sum_dp_send, sum_dp_recv, settle)
    total = jnp.sum(part_dp[...], 0)
    last = total[len(lines):len(lines) + 1, :]
    summed = [
        jnp.concatenate(
            [total[i * full + k:i * full + k + 1, :] for k in range(full)] + [last[:, i * rest:(i + 1) * rest]], 1
        )
        for i in range(len(rows))
    ]
    single = [last[:, rest * len(rows) + i:rest * len(rows) + i + 1] for i in range(len(scalars))]

    def finish(cols, col_sum, weighted, moment_sum, height):
        new = DECAY * cols + (1.0 - DECAY) * (col_sum / height + EPS_SQ)
        mean = moment_sum / height
        square = jnp.sum(weighted / new, 1, keepdims=True) * mean
        factor = jnp.maximum(1.0, jnp.sqrt(square / (height * width)) / CLIP)
        return new, LEARN * jnp.sqrt(mean) * lax.rsqrt(new) / factor

    new, step = finish(
        ent_cols_ref[...], summed[0], summed[1], single[1], owned * devices
    )
    ent_col_ref[...] = new
    moves = [step]
    for layer in range(layers):
        new, step = finish(
            rel_cols_ref[layer:layer + 1, :], summed[2], summed[3 + layer], single[2 + layer], owned_rel * devices,
        )
        rel_col_ref[layer:layer + 1, :] = new
        moves.append(step)
    step_ref[...] = stack_rows(moves, LANES, width).T
    lane = iota(loss_ref.shape, 1)
    loss_ref[...] = jnp.where(lane == 0, single[0], jnp.where(lane == 1, pairs, 0.0))
    for copy in copies:
        copy.wait_send()


def update_kernel(
    rows,
    ent_ref, rel_ref, ent_back_ref, rel_back_ref, ids_ref, whole_ref, ent_rows_ref, rel_rows_ref, step_ref,
    ent_cols_ref, rel_cols_ref, loss_ref,
    ent_w_ref, ent_g_ref, ent_c_ref, rel_w_ref, rel_g_ref, rel_c_ref,
    ent_new_ref, rel_new_ref, ent_col_ref, rel_col_ref, loss_out_ref,
    ent_pick, rel_pick, ent_s, rel_s, ent_w, ent_g, ent_c, rel_w, rel_g, rel_c, load_sem, store_sem, grad_sem,
):
    layers, width, _ = rel_s.shape
    blocks = width // rows

    def span_of(t):
        return pl.ds(pl.multiple_of(t * rows, rows), rows)

    def loads(t):
        span = span_of(t)
        return (
            pltpu.make_async_copy(ent_ref.at[span], ent_s.at[span], load_sem.at[0, t]),
            pltpu.make_async_copy(rel_ref.at[:, span], rel_s.at[:, span], load_sem.at[1, t]),
        )

    def stores(t):
        span = span_of(t)
        pairs = [
            (ent_w.at[span], ent_w_ref.at[span]), (ent_c.at[span], ent_c_ref.at[span]),
            (rel_w.at[:, span], rel_w_ref.at[:, span]), (rel_c.at[:, span], rel_c_ref.at[:, span]),
        ]
        return [pltpu.make_async_copy(a, b, store_sem.at[i, t]) for i, (a, b) in enumerate(pairs)]

    def begin(t, carry):
        for copy in loads(t):
            copy.start()
        return carry

    lax.fori_loop(0, blocks, begin, 0)

    def moments(pick, which, old):
        hit = iota(pick.shape, 1) == ids_ref[:, which:which + 1]
        pick[...] = jnp.where(hit, 1.0, 0.0).astype(BF16)
        whole = jnp.max(jnp.where(hit, whole_ref[:, which:which + 1], 0.0), 0, keepdims=True)
        return DECAY * old + (1.0 - DECAY) * (whole / width + EPS_SQ)

    ent_new_ref[...] = moments(ent_pick, 0, ent_rows_ref[...])
    ent_g[...] = sum(mm(part, ent_pick[...]) for part in two(ent_back_ref[...]))
    grads = [pltpu.make_async_copy(ent_g, ent_g_ref, grad_sem.at[layers])]
    grads[0].start()
    rel_new_ref[...] = moments(rel_pick, 1, rel_rows_ref[...])
    rel_g[...] = sum(mm(part, rel_pick[...]) for part in two(rel_back_ref[...]))
    for layer in range(layers):
        grads.append(pltpu.make_async_copy(rel_g, rel_g_ref.at[layer], grad_sem.at[layer]))
        grads[-1].start()
    ent_col_ref[...] = ent_cols_ref[...]
    rel_col_ref[...] = rel_cols_ref[...]
    for i in range(2):
        loss_out_ref[i] = loss_ref[0, i]
    ent_root, rel_root = lax.rsqrt(ent_new_ref[...]), lax.rsqrt(rel_new_ref[...])

    def block(t, carry):
        span = span_of(t)
        for copy in loads(t):
            copy.wait()
        new = ent_s[span, :] - ent_g[span, :] * ent_root * step_ref[span, 0:1]
        ent_w[span, :] = new
        ent_c[span, :] = new.astype(BF16)
        grad = rel_g[span, :]
        for layer in range(layers):
            new = rel_s[layer, span, :] - grad * rel_root[layer:layer + 1, :] * step_ref[span, layer + 1:layer + 2]
            rel_w[layer, span, :] = new
            rel_c[layer, span, :] = new.astype(BF16)
        for copy in stores(t):
            copy.start()
        return carry

    lax.fori_loop(0, blocks, block, 0)

    def end(t, carry):
        for copy in stores(t):
            copy.wait()
        return carry

    lax.fori_loop(0, blocks, end, 0)
    for copy in grads:
        copy.wait()


def fused(
    entity_table, entity_rows, entity_cols, relation_table, relation_rows, relation_cols,
    requests, relation_requests, src_slot, dst_slot, relation_ids, edge_valid, neg_slot,
):
    n_mp, n_dp = lax.axis_size("mp"), lax.axis_size("dp")
    devices = n_dp * n_mp
    cap = requests.shape[3]
    slots = devices * cap
    negatives = neg_slot.shape[2] * n_mp
    ent_t = entity_table.T
    rel_t = jnp.swapaxes(relation_table, 1, 2)
    width, owned = ent_t.shape
    layers, _, owned_rel = rel_t.shape
    batches, edges = src_slot.shape
    lines = cap * width // LANES
    padded_rel = -(-owned_rel // LANES) * LANES
    V, sem = pltpu.VMEM, pltpu.SemaphoreType.DMA
    vmem = pl.BlockSpec(memory_space=pltpu.VMEM)
    hbm = pl.BlockSpec(memory_space=pl.ANY)
    shape = jax.ShapeDtypeStruct
    args = (
        ent_t, rel_t, requests, relation_requests, src_slot, dst_slot, relation_ids, edge_valid, neg_slot,
        entity_rows[None], relation_rows, entity_cols[None], relation_cols,
    )
    outs = [
        shape((width, slots), F32), shape((width, slots), F32), shape((slots, LANES), jnp.int32),
        shape((slots, LANES), F32), shape((1, width), F32), shape((layers, width), F32),
        shape((width, LANES), F32), shape((8, LANES), F32),
    ]
    many = sem((devices,))
    ent_back, rel_back, ids, whole, ent_col, rel_col, steps, loss = pl.pallas_call(
        functools.partial(step_kernel, n_mp, cap, negatives, 32),
        out_shape=outs,
        in_specs=[hbm] * len(args),
        out_specs=[vmem] * len(outs),
        scratch_shapes=[
            V((width, owned), F32), V((layers, width, owned_rel), F32),
            V((2, width, owned), BF16), V((2, width, padded_rel), BF16),
            V((n_dp, n_mp, LANES), jnp.int32), V((devices, 1, LANES), jnp.int32),
            V((devices, lines, LANES), F32), V((devices, lines, LANES), F32),
            V((devices, lines, LANES), F32), V((devices, lines, LANES), F32),
            V((devices, lines, LANES), F32), V((devices, lines, LANES), F32),
            V((3, devices, lines, LANES), F32), V((2, slots, LANES), F32), V((n_mp, 8, slots), F32), V((n_mp, width, slots), F32),
            V((batches, 2 * slots, edges), BF16), V((batches, slots, edges), BF16),
            V((batches, width, edges), F32), V((batches, width, edges), F32), V((batches, width + AUX, edges), BF16),
            V((2, slots, edges), BF16),
            V((n_mp, 2 * slots, slots), F32), V((2 * slots, slots), F32), V((slots, slots), F32),
            V((2, width, 2 * slots), BF16), V((n_mp, slots, width + AUX), BF16), V((2, width, n_mp * slots), BF16),
            V((n_mp, slots, LANES), F32),
            V((2 * slots, width), F32), V((4, width, slots), F32), V((2, width, slots), F32), V((width, slots), F32),
            V((n_mp, 16, LANES), F32), V((n_dp, 16, LANES), F32), V((8, LANES), F32),
            V((batches, 8, edges), F32), V((batches, 8, edges), F32),
            V((batches, 1, edges), F32), V((batches, 1, edges), F32),
            sem((2 + len(args) - 2,)), many, many, many, many, many, many, sem((2,)), sem((2,)),
            many, many, sem((n_mp,)), sem((n_mp,)),
            many, many, many, many, sem((3,)), sem((3,)),
            sem((n_mp,)), sem((n_mp,)), sem((n_dp,)), sem((n_dp,)),
        ] + [V(a.shape, a.dtype) for a in args[2:]],
        compiler_params=pltpu.CompilerParams(
            collective_id=1, has_side_effects=True, vmem_limit_bytes=60 << 20
        ),
        name="step",
    )(*args)
    rows = 80 if width % 80 == 0 else width
    smem = pl.BlockSpec(memory_space=pltpu.SMEM)
    ent_rows, rel_rows = entity_rows[None], relation_rows
    small = (ent_rows, rel_rows, ent_col, rel_col)
    ent_w, ent_g, ent_c, rel_w, rel_g, rel_c, ent_new, rel_new, ent_col, rel_col, loss = pl.pallas_call(
        functools.partial(update_kernel, rows),
        out_shape=[
            shape(ent_t.shape, F32), shape(ent_t.shape, F32), shape(ent_t.shape, BF16),
            shape(rel_t.shape, F32), shape(rel_t.shape, F32), shape(rel_t.shape, BF16),
        ] + [shape(a.shape, F32) for a in small] + [shape((2,), F32)],
        in_specs=[hbm, hbm] + [vmem] * 9 + [smem],
        out_specs=[hbm] * 6 + [vmem] * 4 + [smem],
        scratch_shapes=[
            V((slots, owned), BF16), V((slots, owned_rel), BF16), V(ent_t.shape, F32), V(rel_t.shape, F32),
            V(ent_t.shape, F32), V(ent_t.shape, F32), V(ent_t.shape, BF16),
            V(rel_t.shape, F32), V(rel_t.shape[1:], F32), V(rel_t.shape, BF16),
            sem((2, width // rows)), sem((4, width // rows)), sem((layers + 1,)),
        ],
        compiler_params=pltpu.CompilerParams(vmem_limit_bytes=60 << 20),
        name="update",
    )(ent_t, rel_t, ent_back, rel_back, ids, whole, ent_rows, rel_rows, steps, ent_col, rel_col, loss)
    back = lambda x: jnp.swapaxes(x, -1, -2)
    return (
        loss, back(ent_w), back(ent_g), ent_new[0], ent_col[0], back(ent_c),
        back(rel_w), back(rel_g), rel_new, rel_col, back(rel_c),
    )


def solution(mesh):
    in_specs = (
        P(("dp", "mp"), None),
        P(("dp", "mp")),
        P(),
        P(None, ("dp", "mp"), None),
        P(None, ("dp", "mp")),
        P(),
        P(("dp", "mp"), None, None, None),
        P(("dp", "mp"), None, None, None),
        P(None, ("dp", "mp")),
        P(None, ("dp", "mp")),
        P(None, ("dp", "mp")),
        P(None, ("dp", "mp")),
        P(None, "dp", "mp"),
    )
    out_specs = (
        P(),
        P(("dp", "mp"), None),
        P(("dp", "mp"), None),
        P(("dp", "mp")),
        P(),
        P(("dp", "mp"), None),
        P(None, ("dp", "mp"), None),
        P(None, ("dp", "mp"), None),
        P(None, ("dp", "mp")),
        P(),
        P(None, ("dp", "mp"), None),
    )

    def step(*args):
        owners_dp, owners_mp, cap = args[6].shape[1:]
        fits = args[0].shape[0] <= args[8].shape[1] and args[8].shape[1] % 128 == 0
        small = fits and owners_mp == 4 and cap == 8 and owners_dp * owners_mp * cap <= 512
        return (fused if small else shards)(*args)

    return jax.shard_map(step, mesh=mesh, in_specs=in_specs, out_specs=out_specs, check_vma=False)
```

```python
import functools

import jax
import jax.numpy as jnp
from jax import lax
from jax.experimental import pallas as pl
from jax.experimental.pallas import tpu as pltpu
from jax.sharding import PartitionSpec as P

MARGIN = 0.1
EPS_DIST = 1e-06
EPS_SQ = 1e-30
DECAY = 0.5
LEARN = 0.3
CLIP = 0.1
HIGH = lax.Precision.HIGHEST


def score_forward(heads, tails, negative_rows, valid_row):
    offset = heads - tails
    near_dist = jnp.sqrt(jnp.sum(offset * offset, 1) + EPS_DIST)
    cross = jnp.dot(heads, negative_rows.T, precision=HIGH, preferred_element_type=jnp.float32)
    far_dist = jnp.sqrt(
        jnp.sum(heads * heads, 1)[:, None]
        + jnp.sum(negative_rows * negative_rows, 1)[None, :]
        - 2.0 * cross
        + EPS_DIST
    )
    margin_z = MARGIN + near_dist[:, None] - far_dist
    part_sum = jnp.sum(jax.nn.softplus(margin_z) * valid_row[:, None])
    return ((offset, near_dist, far_dist, margin_z), part_sum)


def score_backward(heads, negative_rows, valid_row, kept, pairs):
    offset, near_dist, far_dist, margin_z = kept
    weight = jax.nn.sigmoid(margin_z) * valid_row[:, None] / pairs
    along = weight / far_dist
    pull = jnp.sum(weight, 1) / near_dist
    grad_head = (
        pull[:, None] * offset
        - jnp.sum(along, 1)[:, None] * heads
        + jnp.dot(along, negative_rows, precision=HIGH, preferred_element_type=jnp.float32)
    )
    grad_tail = -pull[:, None] * offset
    return (grad_head, grad_tail, along)


def local_moments(grad, row_moment):
    squares = grad * grad + EPS_SQ
    rows_new = DECAY * row_moment + (1.0 - DECAY) * jnp.mean(squares, 1)
    weighted = jnp.sum(grad * grad / rows_new[:, None], 0)
    return (rows_new, jnp.sum(squares, 0), jnp.sum(rows_new), weighted)


def scaled_update(grad, rows_new, cols_new, row_mean):
    return grad * lax.rsqrt(rows_new[:, None] * cols_new[None, :] / row_mean)


def shards(
    entity_table,
    entity_rows,
    entity_cols,
    relation_table,
    relation_rows,
    relation_cols,
    requests,
    relation_requests,
    src_slot,
    dst_slot,
    relation_ids,
    edge_valid,
    neg_slot,
):
    width = entity_table.shape[1]
    n_data = lax.axis_size("dp")
    n_model = lax.axis_size("mp")
    devices = n_data * n_model
    owned_rel = relation_table.shape[1]
    translation = lax.all_gather(jnp.sum(relation_table, 0), ("dp", "mp"), axis=0, tiled=True)
    rel_wanted = relation_requests[0]
    owner_base = (
        jnp.arange(n_data, dtype=jnp.int32)[:, None] * n_model
        + jnp.arange(n_model, dtype=jnp.int32)[None, :]
    ) * owned_rel
    rel_global = (rel_wanted + owner_base[:, :, None]).reshape(-1)
    valid_all = edge_valid.astype(jnp.float32)
    negatives_total = neg_slot.shape[2] * n_model
    pairs = lax.psum(jnp.sum(valid_all), ("dp", "mp")) * negatives_total
    wanted = requests[0]
    incoming = lax.all_to_all(
        lax.all_to_all(wanted, "dp", split_axis=0, concat_axis=0, tiled=True),
        "mp",
        split_axis=1,
        concat_axis=1,
        tiled=True,
    )
    served = entity_table[incoming]
    fetched = lax.all_to_all(
        lax.all_to_all(served, "dp", split_axis=0, concat_axis=0, tiled=True),
        "mp",
        split_axis=1,
        concat_axis=1,
        tiled=True,
    )
    slot_count = fetched.shape[0] * fetched.shape[1] * fetched.shape[2]
    fetched = fetched.reshape(slot_count, width)
    slot_grad = jnp.zeros((slot_count, width), jnp.float32)
    relation_sum = jnp.zeros((rel_global.shape[0], width), jnp.float32)
    loss_part = jnp.zeros((), jnp.float32)
    for batch_index in range(src_slot.shape[0]):
        valid_row = valid_all[batch_index]
        own_negatives = fetched[neg_slot[batch_index, 0]]
        negative_rows = lax.all_gather(own_negatives, "mp", axis=0, tiled=True)
        rel_rows = rel_global[relation_ids[batch_index]]
        heads = fetched[src_slot[batch_index]] + translation[rel_rows]
        tails = fetched[dst_slot[batch_index]]
        kept, part_sum = score_forward(heads, tails, negative_rows, valid_row)
        loss_part = loss_part + part_sum
        grad_head, grad_tail, along = score_backward(heads, negative_rows, valid_row, kept, pairs)
        pulled = lax.dot_general(
            along,
            heads,
            (((0,), (0,)), ((), ())),
            precision=HIGH,
            preferred_element_type=jnp.float32,
        )
        grad_negative = lax.psum_scatter(
            pulled - jnp.sum(along, 0)[:, None] * negative_rows,
            "mp",
            scatter_dimension=0,
            tiled=True,
        )
        slot_grad = slot_grad.at[src_slot[batch_index]].add(grad_head)
        slot_grad = slot_grad.at[dst_slot[batch_index]].add(grad_tail)
        slot_grad = slot_grad.at[neg_slot[batch_index, 0]].add(grad_negative)
        relation_sum = relation_sum.at[relation_ids[batch_index]].add(grad_head)
    returned = lax.all_to_all(
        lax.all_to_all(
            slot_grad.reshape(served.shape), "dp", split_axis=0, concat_axis=0, tiled=True
        ),
        "mp",
        split_axis=1,
        concat_axis=1,
        tiled=True,
    )
    entity_grad = (
        jnp.zeros(entity_table.shape, jnp.float32)
        .at[incoming.reshape(-1)]
        .add(returned.reshape(-1, width))
    )
    rel_incoming = lax.all_to_all(
        lax.all_to_all(rel_wanted, "dp", split_axis=0, concat_axis=0, tiled=True),
        "mp",
        split_axis=1,
        concat_axis=1,
        tiled=True,
    )
    rel_returned = lax.all_to_all(
        lax.all_to_all(
            relation_sum.reshape(rel_wanted.shape + (width,)),
            "dp",
            split_axis=0,
            concat_axis=0,
            tiled=True,
        ),
        "mp",
        split_axis=1,
        concat_axis=1,
        tiled=True,
    )
    relation_shard = (
        jnp.zeros((owned_rel, width), jnp.float32)
        .at[rel_incoming.reshape(-1)]
        .add(rel_returned.reshape(-1, width))
    )
    layers = relation_table.shape[0]
    relation_grad = jnp.broadcast_to(relation_shard[None], (layers,) + relation_shard.shape)
    entity_count = entity_table.shape[0] * devices
    relation_count = relation_shard.shape[0] * devices
    ent_rows, ent_colsq, ent_rsum, ent_weighted = local_moments(entity_grad, entity_rows)
    rel_rows, rel_colsq, rel_rsum, rel_weighted = jax.vmap(local_moments, in_axes=(None, 0))(
        relation_shard, relation_rows
    )
    totals = lax.psum((loss_part, ent_colsq, ent_rsum, rel_colsq, rel_rsum), ("dp", "mp"))
    loss_total, ent_colsq, ent_rsum, rel_colsq, rel_rsum = totals
    ent_cols = DECAY * entity_cols + (1.0 - DECAY) * ent_colsq / entity_count
    rel_cols = DECAY * relation_cols + (1.0 - DECAY) * rel_colsq / relation_count
    ent_mean = ent_rsum / entity_count
    rel_mean = rel_rsum / relation_count
    ent_update = scaled_update(entity_grad, ent_rows, ent_cols, ent_mean)
    rel_update = jax.vmap(scaled_update, in_axes=(None, 0, 0, 0))(
        relation_shard, rel_rows, rel_cols, rel_mean
    )
    ent_usq, rel_usq = lax.psum(
        (jnp.sum(ent_update * ent_update), jnp.sum(rel_update * rel_update, (1, 2))), ("dp", "mp")
    )
    ent_factor = jnp.maximum(1.0, jnp.sqrt(ent_usq / (entity_count * width)) / CLIP)
    rel_factor = jnp.maximum(1.0, jnp.sqrt(rel_usq / (relation_count * width)) / CLIP)
    entity_weight = entity_table - LEARN * (ent_update / ent_factor)
    relation_weight = relation_table - LEARN * (rel_update / rel_factor[:, None, None])
    loss = jnp.stack([loss_total, pairs])
    return (
        loss,
        entity_weight,
        entity_grad,
        ent_rows,
        ent_cols,
        entity_weight.astype(jnp.bfloat16),
        relation_weight,
        relation_grad,
        rel_rows,
        rel_cols,
        relation_weight.astype(jnp.bfloat16),
    )


F32, BF16 = jnp.float32, jnp.bfloat16
LOG2E = 1.4426950408889634
OUT_OF_REACH = 1e30
AUX = 16
LANES = 128
MESH = pl.DeviceIdType.MESH


def two(x):
    hi = x.astype(BF16)
    return hi, (x - hi.astype(F32)).astype(BF16)


def three(x):
    hi = x.astype(BF16)
    rest = x - hi.astype(F32)
    mid = rest.astype(BF16)
    return hi, mid, (rest - mid.astype(F32)).astype(BF16)


def mm(a, b):
    return lax.dot_general(a, b, (((1,), (0,)), ((), ())), preferred_element_type=F32)


def mm_t(a, b):
    return lax.dot_general(a, b, (((1,), (1,)), ((), ())), preferred_element_type=F32)


def iota(shape, axis):
    return lax.broadcasted_iota(jnp.int32, shape, axis)


def stack_rows(rows, count, width):
    at = iota((count, width), 0)
    out = jnp.zeros((count, width), F32)
    for i, row in enumerate(rows):
        out = jnp.where(at == i, row, out)
    return out


def stack_columns(columns, height):
    at = iota((height, LANES), 1)
    out = jnp.zeros((height, LANES), F32)
    for i, column in enumerate(columns):
        out = jnp.where(at == i, column, out)
    return out


def pack(rows, out, tail):
    devices, cap = out.shape[0], 8
    width = rows.shape[1]
    full, rest = width // LANES, width % LANES
    for k in range(full):
        out[:, k * cap:(k + 1) * cap, :] = rows[:, k * LANES:(k + 1) * LANES].reshape(devices, cap, LANES)
    tail[:, 0:rest] = rows[:, full * LANES:]
    line = jnp.concatenate([tail[pl.ds(s, devices, stride=cap), 0:rest] for s in range(cap)], 1)
    out[:, full * cap:, :] = line.reshape(devices, 1, LANES)


def unpack(block, tail):
    devices, cap = block.shape[0], 8
    full = block.shape[1] // cap
    rest = LANES // cap
    parts = [block[:, k * cap:(k + 1) * cap, :].reshape(devices * cap, LANES) for k in range(full)]
    line = block[:, full * cap:, :].reshape(devices, LANES)
    for s in range(cap):
        tail[pl.ds(s, devices, stride=cap), 0:rest] = line[:, s * rest:(s + 1) * rest]
    return jnp.concatenate(parts + [tail[:, 0:rest]], 1)


class Spread:
    def __init__(self, me, devices, place, src, dst, send_sem, recv_sem):
        self.me, self.devices, self.place = me, devices, place
        self.src, self.dst, self.send_sem, self.recv_sem = src, dst, send_sem, recv_sem

    def copy(self, p, at):
        return pltpu.make_async_remote_copy(
            src_ref=self.src(p),
            dst_ref=self.dst(at),
            send_sem=self.send_sem.at[p],
            recv_sem=self.recv_sem.at[at],
            device_id=self.place(p),
            device_id_type=MESH,
        )

    def each(self, act):
        def step(i, carry):
            act(lax.rem(self.me + i, self.devices))
            return carry

        lax.fori_loop(1, self.devices, step, 0)

    def each_sender(self, act):
        def step(i, carry):
            act(lax.rem(self.me + self.devices - i, self.devices))
            return carry

        lax.fori_loop(1, self.devices, step, 0)

    def start(self):
        self.each(lambda p: self.copy(p, self.me).start())

    def arrived(self):
        self.each_sender(lambda p: self.copy(p, p).wait_recv())

    def left(self):
        self.each(lambda p: self.copy(p, self.me).wait_send())


def step_kernel(
    n_mp, cap, negatives, rb,
    ent_ref, rel_ref, *refs,
):
    inputs, kept = refs[:11], refs[-11:]
    step_body(n_mp, cap, negatives, rb, ent_ref, rel_ref, inputs, *kept, *refs[11:-11])


def step_body(
    n_mp, cap, negatives, rb, ent_ref, rel_ref, inputs,
    req_ref, rel_req_ref, src_ref, dst_ref, rid_ref, val_ref, neg_slot_ref,
    ent_rows_ref, rel_rows_ref, ent_cols_ref, rel_cols_ref,
    ent_back_ref, rel_back_ref, ids_ref, whole_ref, ent_col_ref, rel_col_ref, step_ref, loss_ref,
    ent_s, rel_s, ent_parts, rel_parts, ask_s, asked, out_ent, out_rel, in_ent, in_rel, back_in_ent, back_in_rel,
    packed, tail_s, counts_s, neg_s, oh_s, oh_d, lead_s, gap_s, head_s, along_s, a_s, b1_s, b2_s, table, neg_rows, neg_parts, count_s,
    acc_s, gn_s, from_mate, from_across, part_mp, part_dp, loss_s, pull_s, weight_s, near_s, bound_s,
    load_sem, ask_send, ask_recv, ent_send, ent_recv, rel_send, rel_recv, mp_send, mp_recv,
    forward_send, forward_recv, count_send, count_recv,
    back_ent_send, back_ent_recv, back_rel_send, back_rel_recv, mate_send, mate_recv,
    sum_mp_send, sum_mp_recv, sum_dp_send, sum_dp_recv,
):
    width, owned = ent_s.shape
    layers, _, owned_rel = rel_s.shape
    devices = out_ent.shape[0]
    n_dp = devices // n_mp
    slots = devices * cap
    batches, edges = src_ref.shape
    main = width // LANES * LANES
    rest = width - main
    dp, mp = lax.axis_index("dp"), lax.axis_index("mp")
    me = dp * n_mp + mp
    mate, across = mp + 1 - 2 * lax.rem(mp, 2), lax.rem(mp + 2, n_mp)
    beyond = mate + across - mp

    def place(p):
        return lax.div(p, n_mp), lax.rem(p, n_mp)

    def by_columns(size, act):
        blocks = edges // size

        def step(t, carry):
            act(lax.div(t, blocks), pl.ds(pl.multiple_of(lax.rem(t, blocks) * size, size), size))
            return carry

        lax.fori_loop(0, batches * blocks, step, 0)

    block_of = lambda size: size if edges % size == 0 else edges
    narrow, broad = block_of(512), block_of(2048)

    barrier = pltpu.get_barrier_semaphore()

    def tell(i, carry):
        pl.semaphore_signal(
            barrier, inc=1, device_id=place(lax.rem(me + i, devices)), device_id_type=MESH
        )
        return carry

    lax.fori_loop(1, devices, tell, 0)
    load_ent = pltpu.make_async_copy(ent_ref, ent_s, load_sem.at[0])
    load_rel = pltpu.make_async_copy(rel_ref, rel_s, load_sem.at[1])
    kept = (
        req_ref, rel_req_ref, src_ref, dst_ref, rid_ref, val_ref, neg_slot_ref,
        ent_rows_ref, rel_rows_ref, ent_cols_ref, rel_cols_ref,
    )
    small = [pltpu.make_async_copy(a, b, load_sem.at[2 + i]) for i, (a, b) in enumerate(zip(inputs, kept))]
    for copy in small:
        copy.start()
    load_ent.start()
    load_rel.start()
    for copy in small:
        copy.wait()
    valid = jnp.sum(jnp.sum(val_ref[...], 0, keepdims=True), 1, keepdims=True)
    lane = iota(ask_s.shape, 2)
    ask_s[...] = jnp.where(lane == 2 * cap, valid[None], 0)
    ask_s[:, :, 0:cap] = req_ref[0]
    ask_s[:, :, cap:2 * cap] = rel_req_ref[0]
    asked[me] = ask_s[dp, pl.ds(mp, 1)]
    ask = Spread(
        me, devices, place, lambda p: ask_s.at[place(p)[0], pl.ds(place(p)[1], 1)], lambda p: asked.at[p], ask_send, ask_recv
    )
    pl.semaphore_wait(barrier, devices - 1)

    ask.start()
    load_ent.wait()
    load_rel.wait()
    rows_at = 80 if width % 80 == 0 else width

    def split(t, carry):
        span = pl.ds(pl.multiple_of(t * rows_at, rows_at), rows_at)
        for i, part in enumerate(two(ent_s[span, :])):
            ent_parts[i, span, :] = part
        for i, part in enumerate(two(sum(rel_s[i, span, :] for i in range(layers)))):
            rel_parts[i, span, 0:owned_rel] = part
        return carry

    lax.fori_loop(0, width // rows_at, split, 0)
    if rel_parts.shape[2] > owned_rel:
        rel_parts[:, :, owned_rel:] = jnp.zeros((2, width, rel_parts.shape[2] - owned_rel), BF16)
    ask.arrived()
    wide = jnp.broadcast_to(asked[...], (devices, cap, LANES)).reshape(slots, LANES)
    at, lane = lax.rem(iota(wide.shape, 0), cap), iota(wide.shape, 1)
    ent_id = jnp.sum(jnp.where(lane == at, wide, 0), 1, keepdims=True)
    rel_id = jnp.sum(jnp.where(lane == at + cap, wide, 0), 1, keepdims=True)

    pick = jnp.where(iota((slots, owned), 1) == ent_id, 1.0, 0.0).astype(BF16)
    rows = mm_t(pick, ent_parts[0]) + mm_t(pick, ent_parts[1])
    pick = jnp.where(iota((slots, rel_parts.shape[2]), 1) == rel_id, 1.0, 0.0).astype(BF16)
    rel_rows = mm_t(pick, rel_parts[0]) + mm_t(pick, rel_parts[1])

    def block(ref):
        return lambda p: ref.at[p]

    pack(rows, out_ent, tail_s.at[0])
    give_ent = Spread(me, devices, place, block(out_ent), block(in_ent), ent_send, ent_recv)
    give_ent.start()
    pack(rel_rows, out_rel, tail_s.at[1])
    give_rel = Spread(me, devices, place, block(out_rel), block(in_rel), rel_send, rel_recv)
    give_rel.start()
    in_ent[me] = out_ent[me]
    in_rel[me] = out_rel[me]
    ids_ref[...] = jnp.where(iota(ids_ref.shape, 1) == 0, ent_id, jnp.where(iota(ids_ref.shape, 1) == 1, rel_id, 0))
    valid_all = jnp.sum(jnp.where(iota(asked.shape, 2) == 2 * cap, asked[...], 0), 0)
    pairs = jnp.sum(valid_all, 1, keepdims=True).astype(F32) * negatives
    slot = iota((slots, narrow), 0)

    def mark(m, cols):
        row = pl.ds(m, 1)
        oh_s[m, 0:slots, cols] = jnp.where(slot == src_ref[row, cols], 1.0, 0.0).astype(BF16)
        oh_s[m, slots:, cols] = jnp.where(slot == rid_ref[row, cols], 1.0, 0.0).astype(BF16)
        oh_d[m, :, cols] = jnp.where(slot == dst_ref[row, cols], 1.0, 0.0).astype(BF16)

    by_columns(narrow, mark)
    hits = [
        jnp.sum(jnp.where(iota((slots, neg_slot_ref.shape[2]), 0) == neg_slot_ref[m], 1.0, 0.0), 1, keepdims=True)
        for m in range(batches)
    ]
    counts_s[mp] = stack_columns(hits, slots).T[0:8]
    count_copies = []
    for i in range(1, n_mp):
        count_copies.append(pltpu.make_async_remote_copy(
            src_ref=counts_s.at[mp], dst_ref=counts_s.at[mp], send_sem=count_send.at[i], recv_sem=count_recv.at[i],
            device_id=(dp, lax.rem(mp + i, n_mp)), device_id_type=MESH,
        ))
        count_copies[-1].start()
    ask.left()

    def forward(p):
        return pltpu.make_async_remote_copy(
            src_ref=in_ent.at[p], dst_ref=packed.at[0, p], send_sem=forward_send.at[p], recv_sem=forward_recv.at[p],
            device_id=(dp, across), device_id_type=MESH,
        )

    forward(me).start()

    def pass_on(p):
        give_ent.copy(p, p).wait_recv()
        forward(p).start()

    give_ent.each_sender(pass_on)

    def hand(i, src, dst):
        return pltpu.make_async_remote_copy(
            src_ref=src, dst_ref=packed.at[dst], send_sem=mp_send.at[i], recv_sem=mp_recv.at[i],
            device_id=(dp, mate), device_id_type=MESH,
        )

    to_mate, onward = hand(0, in_ent, 1), hand(1, packed.at[0], 2)
    to_mate.start()
    own_t = unpack(in_ent, tail_s.at[0]).T
    neg_s[3] = own_t
    for i, part in enumerate(two(own_t)):
        table[i, :, 0:slots] = part
    def start_of_head(m, cols):
        lead = mm(table[0, :, 0:slots], oh_s[m, 0:slots, cols]) + mm(table[1, :, 0:slots], oh_s[m, 0:slots, cols])
        lead_s[m, :, cols] = lead
        gap_s[m, :, cols] = lead - mm(table[0, :, 0:slots], oh_d[m, :, cols]) - mm(table[1, :, 0:slots], oh_d[m, :, cols])

    by_columns(narrow, start_of_head)

    give_rel.arrived()
    rel_got = unpack(in_rel, tail_s.at[1]).T
    for i, part in enumerate(two(rel_got)):
        table[i, :, slots:] = part
    def whole_head(m, cols):
        moved = mm(table[0, :, slots:], oh_s[m, slots:, cols]) + mm(table[1, :, slots:], oh_s[m, slots:, cols])
        head = lead_s[m, :, cols] + moved
        diff = gap_s[m, :, cols] + moved
        near2 = jnp.sum(diff * diff, 0, keepdims=True) + EPS_DIST
        inv_near = lax.rsqrt(near2)
        near_s[m, :, cols] = inv_near
        bound_s[m, :, cols] = jnp.where(
            val_ref[pl.ds(m, 1), cols] > 0, (MARGIN + near2 * inv_near) * LOG2E, -OUT_OF_REACH
        )
        norm = three((jnp.sum(head * head, 0, keepdims=True) + EPS_DIST) * (LOG2E * LOG2E))
        ones = jnp.ones_like(near2)
        head_s[m, 0:width, cols] = head.astype(BF16)
        extra = stack_rows([ones] * 3 + [part.astype(F32) for part in norm], AUX, near2.shape[1])
        head_s[m, width:, cols] = extra.astype(BF16)

    by_columns(broad, whole_head)
    order = (across, beyond, mate, mp)

    def ready(g):
        if g == 0:
            def came(p, carry):
                forward(p).wait_recv()
                return carry

            lax.fori_loop(0, devices, came, 0)
            onward.start()
            for i in range(1, n_mp):
                from_mp = lax.rem(mp + n_mp - i, n_mp)
                pltpu.make_async_remote_copy(
                    src_ref=counts_s.at[mp], dst_ref=counts_s.at[from_mp], send_sem=count_send.at[i],
                    recv_sem=count_recv.at[i], device_id=(dp, from_mp), device_id_type=MESH,
                ).wait_recv()
        elif g == 1:
            onward.wait_recv()
        elif g == 2:
            to_mate.wait_recv()
        if g < 3:
            neg_s[g] = unpack(packed.at[(0, 2, 1)[g]], tail_s.at[0]).T
        n = neg_s[g]
        norm = three(jnp.sum(n * n, 0, keepdims=True) * (LOG2E * LOG2E))
        ones = jnp.ones((1, slots), F32)
        extra = stack_rows([part.astype(F32) for part in norm] + [ones] * 3, AUX, slots)
        neg_rows[g] = jnp.concatenate([n * (-2.0 * LOG2E * LOG2E), extra], 0).T.astype(BF16)
        for i, part in enumerate(two(n)):
            neg_parts[i, :, g * slots:(g + 1) * slots] = part
        blank = jnp.zeros((LANES - 8, slots), F32)
        count_s[g] = jnp.concatenate([counts_s[order[g]], blank], 0).T

    loss_s[...] = jnp.zeros_like(loss_s)
    weight = [jnp.zeros((8, edges), F32) for _ in range(batches)]
    pulls = [jnp.zeros((8, edges), F32) for _ in range(batches)]

    steps = [(g, m) for g in range(n_mp) for m in range(batches)]
    pieces = slots // rb

    def distances(i, b):
        g, m = steps[i]
        part = slice(b * edges // pieces, (b + 1) * edges // pieces)
        lead_s[i % 2, 0:slots, part] = mm(neg_rows[g], head_s[m, :, part])

    def pair_terms(i, b):
        g, m = steps[i]
        span = slice(b * rb, (b + 1) * rb)
        count = count_s[g, span, m:m + 1]
        square = jnp.maximum(lead_s[i % 2, span, :], 1e-20)
        inv_far = lax.rsqrt(square)
        t = square * inv_far - bound_s[m]
        sig = pl.reciprocal(1.0 + jnp.exp2(t), approx=True)
        rest_sig = 1.0 - sig
        low, high = jnp.minimum(sig, rest_sig), jnp.maximum(sig, rest_sig)
        w = count * sig
        pulls[m] = pulls[m] + jnp.sum(w.reshape(rb // 8, 8, edges), 0)
        w = w * inv_far
        weight[m] = weight[m] + jnp.sum(w.reshape(rb // 8, 8, edges), 0)
        along_s[i % 2, span, :] = w.astype(BF16)
        q = jnp.zeros((rb, LANES), F32)
        over = jnp.zeros((rb, LANES), F32)
        for k in range(edges // LANES):
            part = slice(k * LANES, (k + 1) * LANES)
            q = q * high[:, part] + low[:, part]
            over = over + jnp.minimum(t[:, part], 0.0)
        term = count * (-jnp.log(1.0 - q) - over * (1.0 / LOG2E))
        loss_s[...] += jnp.sum(term.reshape(rb // 8, 8, LANES), 0)

    def by_slot(i, half):
        g, m = steps[i]
        rows = slice(half * slots, (half + 1) * slots)
        part = mm_t(oh_s[m, rows, :], along_s[i % 2])
        a_s[g, rows, :] = part if m == 0 else a_s[g, rows, :] + part

    def grads_of(g):
        total = a_s[g] * LOG2E
        hi, lo = two(total)
        whole = jnp.sum(total[0:slots], 0, keepdims=True)
        cols = slice(g * slots, (g + 1) * slots)
        slot_part = mm_t(hi, neg_parts[0, :, cols]) + mm_t(hi, neg_parts[1, :, cols]) + mm_t(lo, neg_parts[0, :, cols])
        acc_s[...] = slot_part if g == 0 else acc_s[...] + slot_part
        return mm(table[0], hi) + mm(table[1], hi) + mm(table[0], lo) - whole * neg_s[g]

    def swap(i, src, dst, to):
        return pltpu.make_async_remote_copy(
            src_ref=src, dst_ref=dst, send_sem=mate_send.at[i], recv_sem=mate_recv.at[i],
            device_id=(dp, to), device_id_type=MESH,
        )

    through = swap(0, gn_s.at[0], from_mate.at[0], mate)
    over_x = swap(1, gn_s.at[1], from_across, across)
    direct = swap(2, gn_s.at[2], from_mate.at[1], mate)
    def group_done(g):
        grad = grads_of(g)
        if g == 0:
            gn_s[1] = grad
        elif g == 1:
            gn_s[0] = grad
            through.start()
        elif g == 2:
            gn_s[2] = grad
            direct.start()
        else:
            gn_s[3] = grad

    ready(0)
    for b in range(pieces):
        distances(0, b)
    for i in range(len(steps)):
        if i + 1 < len(steps) and steps[i + 1][1] == 0:
            ready(steps[i + 1][0])
        for b in range(pieces):
            if i + 1 < len(steps):
                distances(i + 1, b)
            pair_terms(i, b)
        by_slot(i, 0)
        by_slot(i, 1)
        if steps[i][1] == batches - 1:
            group_done(steps[i][0])
        if i == 2 * batches:
            through.wait_recv()
            gn_s[1] = gn_s[1] + from_mate[0]
            over_x.start()

    broad_slot = iota((slots, broad), 0)
    for m in range(batches):
        pull_s[m] = pulls[m]
        weight_s[m] = weight[m]
    b1_s[...] = jnp.zeros_like(b1_s)
    b2_s[...] = jnp.zeros_like(b2_s)

    def edge_weights(m, cols):
        row = pl.ds(m, 1)
        pull = jnp.sum(pull_s[m, :, cols], 0, keepdims=True) * near_s[m, :, cols]
        excess = pull - jnp.sum(weight_s[m, :, cols], 0, keepdims=True) * LOG2E
        hit = broad_slot == dst_ref[row, cols]
        b1_s[...] += sum(
            mm_t(oh_s[m, :, cols], jnp.where(hit, piece.astype(F32), 0.0).astype(BF16)) for piece in two(pull)
        )
        hit = broad_slot == rid_ref[row, cols]
        b2_s[...] += sum(
            mm_t(oh_s[m, 0:slots, cols], jnp.where(hit, piece.astype(F32), 0.0).astype(BF16)) for piece in two(excess)
        )

    by_columns(broad, edge_weights)
    sd, rd, sr = b1_s[0:slots, :], b1_s[slots:, :], b2_s[...]
    eye = iota((slots, slots), 0) == iota((slots, slots), 1)
    ss = jnp.where(eye, jnp.sum(sr, 1, keepdims=True) + jnp.sum(sd, 0, keepdims=True), 0.0) - sd - sd.T
    rr = jnp.where(eye, jnp.sum(sr, 0, keepdims=True), 0.0)
    cross = sr - rd.T

    def grads(lo, hi, left, right):
        kept = two(jnp.concatenate([left, right], 1))
        return acc_s[lo:hi, :] + mm_t(kept[0], table[0]) + mm_t(kept[0], table[1]) + mm_t(kept[1], table[0])

    grad_rel = grads(slots, 2 * slots, cross.T, rr)
    give_ent.left()
    give_rel.left()
    pack(grad_rel, out_rel, tail_s.at[1])
    back_rel = Spread(me, devices, place, block(out_rel), block(back_in_rel), back_rel_send, back_rel_recv)
    back_ent = Spread(me, devices, place, block(out_ent), block(back_in_ent), back_ent_send, back_ent_recv)
    back_rel.start()
    grad_ent = grads(0, slots, ss, cross)
    direct.wait_recv()
    over_x.wait_recv()
    grad_ent = grad_ent + (gn_s[3] + from_mate[1] + from_across[...]).T
    pack(grad_ent, out_ent, tail_s.at[0])
    back_ent.start()
    back_in_rel[me] = out_rel[me]
    back_in_ent[me] = out_ent[me]

    def same_rows(column, rows, height):
        row = jnp.broadcast_to(column.astype(F32), (slots, LANES)).T[0:1]
        same = jnp.where(column.astype(F32) == row, 1.0, 0.0)
        share_of = 1.0 / jnp.sum(same, 1, keepdims=True)
        hit = iota((slots, height), 1) == column
        old = [jnp.sum(jnp.where(hit, r, 0.0), 1, keepdims=True) for r in rows]
        kept = [jnp.sum(DECAY * r + (1.0 - DECAY) * EPS_SQ, 1, keepdims=True) for r in rows]
        return same.astype(BF16), share_of, old, kept

    ent_same = same_rows(ent_id, [ent_rows_ref[...]], owned)
    rel_same = same_rows(rel_id, [rel_rows_ref[layer:layer + 1, :] for layer in range(layers)], owned_rel)
    scale = 1.0 / pairs

    def row_sums(back, same, share_of, old, kept):
        grad = sum(mm(same, part) for part in two(back))
        square = grad * grad
        whole = jnp.sum(square, 1, keepdims=True)
        moment = (1.0 - DECAY) / width * whole
        out = [jnp.sum(square * share_of, 0, keepdims=True)]
        sums = []
        for o, k in zip(old, kept):
            new = DECAY * o + (1.0 - DECAY) * EPS_SQ + moment
            out.append(jnp.sum(square * (share_of / new), 0, keepdims=True))
            sums.append(k + jnp.sum(moment * share_of, 0, keepdims=True))
        return whole, out, sums

    for copy in [to_mate, onward, through, over_x, direct] + count_copies:
        copy.wait_send()

    def gone(p, carry):
        forward(p).wait_send()
        return carry

    lax.fori_loop(0, devices, gone, 0)
    back_rel.arrived()
    rel_back = unpack(back_in_rel, tail_s.at[1]) * scale
    rel_whole, more_rows, more_sums = row_sums(rel_back, *rel_same)
    back_rel.left()
    back_ent.arrived()
    ent_back = unpack(back_in_ent, tail_s.at[0]) * scale
    ent_whole, rows, sums = row_sums(ent_back, *ent_same)
    rows = rows + more_rows
    scalars = [jnp.sum(jnp.sum(loss_s[...], 0, keepdims=True), 1, keepdims=True)] + sums + more_sums
    full = main // LANES
    tails = [row[:, main:] for row in rows] + scalars
    tails.append(jnp.zeros((1, LANES - rest * len(rows) - len(scalars)), F32))
    lines = [row[:, i * LANES:(i + 1) * LANES] for row in rows for i in range(full)]
    part_mp[mp] = stack_rows(lines + [jnp.concatenate(tails, 1)], 16, LANES)

    def share(axis, size, at, buffer, send, recv, meanwhile):
        copies = []
        for i in range(1, size):
            copies.append(pltpu.make_async_remote_copy(
                src_ref=buffer.at[at], dst_ref=buffer.at[at], send_sem=send.at[i], recv_sem=recv.at[i],
                device_id={axis: lax.rem(at + i, size)}, device_id_type=MESH,
            ))
            copies[-1].start()
        meanwhile()
        for i in range(1, size):
            came = lax.rem(at + size - i, size)
            pltpu.make_async_remote_copy(
                src_ref=buffer.at[came], dst_ref=buffer.at[came], send_sem=send.at[i], recv_sem=recv.at[i],
                device_id={axis: came}, device_id_type=MESH,
            ).wait_recv()
        return copies

    def write_out():
        ent_back_ref[...] = ent_back.T
        rel_back_ref[...] = rel_back.T
        lane = iota(whole_ref.shape, 1)
        whole_ref[...] = jnp.where(lane == 0, ent_whole, jnp.where(lane == 1, rel_whole, 0.0))

    copies = share("mp", n_mp, mp, part_mp, sum_mp_send, sum_mp_recv, write_out)
    part_dp[dp] = jnp.sum(part_mp[...], 0)
    copies += share("dp", n_dp, dp, part_dp, sum_dp_send, sum_dp_recv, back_ent.left)
    total = jnp.sum(part_dp[...], 0)
    last = total[len(lines):len(lines) + 1, :]
    summed = [
        jnp.concatenate(
            [total[i * full + k:i * full + k + 1, :] for k in range(full)] + [last[:, i * rest:(i + 1) * rest]], 1
        )
        for i in range(len(rows))
    ]
    single = [last[:, rest * len(rows) + i:rest * len(rows) + i + 1] for i in range(len(scalars))]

    def finish(cols, col_sum, weighted, moment_sum, height):
        new = DECAY * cols + (1.0 - DECAY) * (col_sum / height + EPS_SQ)
        mean = moment_sum / height
        square = jnp.sum(weighted / new, 1, keepdims=True) * mean
        factor = jnp.maximum(1.0, jnp.sqrt(square / (height * width)) / CLIP)
        return new, LEARN * jnp.sqrt(mean) * lax.rsqrt(new) / factor

    new, step = finish(
        ent_cols_ref[...], summed[0], summed[1], single[1], owned * devices
    )
    ent_col_ref[...] = new
    moves = [step]
    for layer in range(layers):
        new, step = finish(
            rel_cols_ref[layer:layer + 1, :], summed[2], summed[3 + layer], single[2 + layer], owned_rel * devices,
        )
        rel_col_ref[layer:layer + 1, :] = new
        moves.append(step)
    step_ref[...] = stack_rows(moves, LANES, width).T
    lane = iota(loss_ref.shape, 1)
    loss_ref[...] = jnp.where(lane == 0, single[0], jnp.where(lane == 1, pairs, 0.0))
    for copy in copies:
        copy.wait_send()


def update_kernel(
    rows,
    ent_ref, rel_ref, ent_back_ref, rel_back_ref, ids_ref, whole_ref, ent_rows_ref, rel_rows_ref, step_ref,
    ent_cols_ref, rel_cols_ref, loss_ref,
    ent_w_ref, ent_g_ref, ent_c_ref, rel_w_ref, rel_g_ref, rel_c_ref,
    ent_new_ref, rel_new_ref, ent_col_ref, rel_col_ref, loss_out_ref,
    ent_pick, rel_pick, ent_s, rel_s, ent_w, ent_g, ent_c, rel_w, rel_g, rel_c, load_sem, store_sem, grad_sem,
):
    layers, width, _ = rel_s.shape
    blocks = width // rows

    def span_of(t):
        return pl.ds(pl.multiple_of(t * rows, rows), rows)

    def loads(t):
        span = span_of(t)
        return (
            pltpu.make_async_copy(ent_ref.at[span], ent_s.at[span], load_sem.at[0, t]),
            pltpu.make_async_copy(rel_ref.at[:, span], rel_s.at[:, span], load_sem.at[1, t]),
        )

    def stores(t):
        span = span_of(t)
        pairs = [
            (ent_w.at[span], ent_w_ref.at[span]), (ent_c.at[span], ent_c_ref.at[span]),
            (rel_w.at[:, span], rel_w_ref.at[:, span]), (rel_c.at[:, span], rel_c_ref.at[:, span]),
        ]
        return [pltpu.make_async_copy(a, b, store_sem.at[i, t]) for i, (a, b) in enumerate(pairs)]

    def begin(t, carry):
        for copy in loads(t):
            copy.start()
        return carry

    lax.fori_loop(0, blocks, begin, 0)

    def moments(pick, which, old):
        hit = iota(pick.shape, 1) == ids_ref[:, which:which + 1]
        pick[...] = jnp.where(hit, 1.0, 0.0).astype(BF16)
        whole = jnp.max(jnp.where(hit, whole_ref[:, which:which + 1], 0.0), 0, keepdims=True)
        return DECAY * old + (1.0 - DECAY) * (whole / width + EPS_SQ)

    ent_new_ref[...] = moments(ent_pick, 0, ent_rows_ref[...])
    ent_g[...] = sum(mm(part, ent_pick[...]) for part in two(ent_back_ref[...]))
    grads = [pltpu.make_async_copy(ent_g, ent_g_ref, grad_sem.at[layers])]
    grads[0].start()
    rel_new_ref[...] = moments(rel_pick, 1, rel_rows_ref[...])
    rel_g[...] = sum(mm(part, rel_pick[...]) for part in two(rel_back_ref[...]))
    for layer in range(layers):
        grads.append(pltpu.make_async_copy(rel_g, rel_g_ref.at[layer], grad_sem.at[layer]))
        grads[-1].start()
    ent_col_ref[...] = ent_cols_ref[...]
    rel_col_ref[...] = rel_cols_ref[...]
    for i in range(2):
        loss_out_ref[i] = loss_ref[0, i]
    ent_root, rel_root = lax.rsqrt(ent_new_ref[...]), lax.rsqrt(rel_new_ref[...])

    def block(t, carry):
        span = span_of(t)
        for copy in loads(t):
            copy.wait()
        new = ent_s[span, :] - ent_g[span, :] * ent_root * step_ref[span, 0:1]
        ent_w[span, :] = new
        ent_c[span, :] = new.astype(BF16)
        grad = rel_g[span, :]
        for layer in range(layers):
            new = rel_s[layer, span, :] - grad * rel_root[layer:layer + 1, :] * step_ref[span, layer + 1:layer + 2]
            rel_w[layer, span, :] = new
            rel_c[layer, span, :] = new.astype(BF16)
        for copy in stores(t):
            copy.start()
        return carry

    lax.fori_loop(0, blocks, block, 0)

    def end(t, carry):
        for copy in stores(t):
            copy.wait()
        return carry

    lax.fori_loop(0, blocks, end, 0)
    for copy in grads:
        copy.wait()


def fused(
    entity_table, entity_rows, entity_cols, relation_table, relation_rows, relation_cols,
    requests, relation_requests, src_slot, dst_slot, relation_ids, edge_valid, neg_slot,
):
    n_mp, n_dp = lax.axis_size("mp"), lax.axis_size("dp")
    devices = n_dp * n_mp
    cap = requests.shape[3]
    slots = devices * cap
    negatives = neg_slot.shape[2] * n_mp
    ent_t = entity_table.T
    rel_t = jnp.swapaxes(relation_table, 1, 2)
    width, owned = ent_t.shape
    layers, _, owned_rel = rel_t.shape
    batches, edges = src_slot.shape
    lines = cap * width // LANES
    padded_rel = -(-owned_rel // LANES) * LANES
    V, sem = pltpu.VMEM, pltpu.SemaphoreType.DMA
    vmem = pl.BlockSpec(memory_space=pltpu.VMEM)
    hbm = pl.BlockSpec(memory_space=pl.ANY)
    shape = jax.ShapeDtypeStruct
    args = (
        ent_t, rel_t, requests, relation_requests, src_slot, dst_slot, relation_ids, edge_valid, neg_slot,
        entity_rows[None], relation_rows, entity_cols[None], relation_cols,
    )
    outs = [
        shape((width, slots), F32), shape((width, slots), F32), shape((slots, LANES), jnp.int32),
        shape((slots, LANES), F32), shape((1, width), F32), shape((layers, width), F32),
        shape((width, LANES), F32), shape((8, LANES), F32),
    ]
    many = sem((devices,))
    ent_back, rel_back, ids, whole, ent_col, rel_col, steps, loss = pl.pallas_call(
        functools.partial(step_kernel, n_mp, cap, negatives, 32),
        out_shape=outs,
        in_specs=[hbm] * len(args),
        out_specs=[vmem] * len(outs),
        scratch_shapes=[
            V((width, owned), F32), V((layers, width, owned_rel), F32),
            V((2, width, owned), BF16), V((2, width, padded_rel), BF16),
            V((n_dp, n_mp, LANES), jnp.int32), V((devices, 1, LANES), jnp.int32),
            V((devices, lines, LANES), F32), V((devices, lines, LANES), F32),
            V((devices, lines, LANES), F32), V((devices, lines, LANES), F32),
            V((devices, lines, LANES), F32), V((devices, lines, LANES), F32),
            V((3, devices, lines, LANES), F32), V((2, slots, LANES), F32), V((n_mp, 8, slots), F32), V((n_mp, width, slots), F32),
            V((batches, 2 * slots, edges), BF16), V((batches, slots, edges), BF16),
            V((batches, width, edges), F32), V((batches, width, edges), F32), V((batches, width + AUX, edges), BF16),
            V((2, slots, edges), BF16),
            V((n_mp, 2 * slots, slots), F32), V((2 * slots, slots), F32), V((slots, slots), F32),
            V((2, width, 2 * slots), BF16), V((n_mp, slots, width + AUX), BF16), V((2, width, n_mp * slots), BF16),
            V((n_mp, slots, LANES), F32),
            V((2 * slots, width), F32), V((4, width, slots), F32), V((2, width, slots), F32), V((width, slots), F32),
            V((n_mp, 16, LANES), F32), V((n_dp, 16, LANES), F32), V((8, LANES), F32),
            V((batches, 8, edges), F32), V((batches, 8, edges), F32),
            V((batches, 1, edges), F32), V((batches, 1, edges), F32),
            sem((2 + len(args) - 2,)), many, many, many, many, many, many, sem((2,)), sem((2,)),
            many, many, sem((n_mp,)), sem((n_mp,)),
            many, many, many, many, sem((3,)), sem((3,)),
            sem((n_mp,)), sem((n_mp,)), sem((n_dp,)), sem((n_dp,)),
        ] + [V(a.shape, a.dtype) for a in args[2:]],
        compiler_params=pltpu.CompilerParams(
            collective_id=1, has_side_effects=True, vmem_limit_bytes=60 << 20
        ),
        name="step",
    )(*args)
    rows = 80 if width % 80 == 0 else width
    smem = pl.BlockSpec(memory_space=pltpu.SMEM)
    ent_rows, rel_rows = entity_rows[None], relation_rows
    small = (ent_rows, rel_rows, ent_col, rel_col)
    ent_w, ent_g, ent_c, rel_w, rel_g, rel_c, ent_new, rel_new, ent_col, rel_col, loss = pl.pallas_call(
        functools.partial(update_kernel, rows),
        out_shape=[
            shape(ent_t.shape, F32), shape(ent_t.shape, F32), shape(ent_t.shape, BF16),
            shape(rel_t.shape, F32), shape(rel_t.shape, F32), shape(rel_t.shape, BF16),
        ] + [shape(a.shape, F32) for a in small] + [shape((2,), F32)],
        in_specs=[hbm, hbm] + [vmem] * 9 + [smem],
        out_specs=[hbm] * 6 + [vmem] * 4 + [smem],
        scratch_shapes=[
            V((slots, owned), BF16), V((slots, owned_rel), BF16), V(ent_t.shape, F32), V(rel_t.shape, F32),
            V(ent_t.shape, F32), V(ent_t.shape, F32), V(ent_t.shape, BF16),
            V(rel_t.shape, F32), V(rel_t.shape[1:], F32), V(rel_t.shape, BF16),
            sem((2, width // rows)), sem((4, width // rows)), sem((layers + 1,)),
        ],
        compiler_params=pltpu.CompilerParams(vmem_limit_bytes=60 << 20),
        name="update",
    )(ent_t, rel_t, ent_back, rel_back, ids, whole, ent_rows, rel_rows, steps, ent_col, rel_col, loss)
    back = lambda x: jnp.swapaxes(x, -1, -2)
    return (
        loss, back(ent_w), back(ent_g), ent_new[0], ent_col[0], back(ent_c),
        back(rel_w), back(rel_g), rel_new, rel_col, back(rel_c),
    )


def solution(mesh):
    in_specs = (
        P(("dp", "mp"), None),
        P(("dp", "mp")),
        P(),
        P(None, ("dp", "mp"), None),
        P(None, ("dp", "mp")),
        P(),
        P(("dp", "mp"), None, None, None),
        P(("dp", "mp"), None, None, None),
        P(None, ("dp", "mp")),
        P(None, ("dp", "mp")),
        P(None, ("dp", "mp")),
        P(None, ("dp", "mp")),
        P(None, "dp", "mp"),
    )
    out_specs = (
        P(),
        P(("dp", "mp"), None),
        P(("dp", "mp"), None),
        P(("dp", "mp")),
        P(),
        P(("dp", "mp"), None),
        P(None, ("dp", "mp"), None),
        P(None, ("dp", "mp"), None),
        P(None, ("dp", "mp")),
        P(),
        P(None, ("dp", "mp"), None),
    )

    def step(*args):
        owners_dp, owners_mp, cap = args[6].shape[1:]
        fits = args[0].shape[0] <= args[8].shape[1] and args[8].shape[1] % 128 == 0
        small = fits and owners_mp == 4 and cap == 8 and owners_dp * owners_mp * cap <= 512
        return (fused if small else shards)(*args)

    return jax.shard_map(step, mesh=mesh, in_specs=in_specs, out_specs=out_specs, check_vma=False)
```
